32 devices in a mesh: cores: 8 (over y, x, core), face: 4 (over z).
Axes of the slice: x: 2, y: 2, z: 4, core: 2. Of those that a mesh axis runs over, the one named last changes fastest.
Arguments:
- fields: bfloat16 [2, 16, 16, 128, 256], P(None, 'cores', 'face'), may hold values from -6 to 6
- pore_mask: int32 [16, 16, 128], P('cores', 'face'), may hold values 0 or 1
- conv_kernel: bfloat16 [54, 32], replicated, may hold values from -0.875 to 0.875
- conv_bias: float32 [32], replicated, may hold values from -3 to 3
- read_weight: float32 [32], replicated, may hold values from -1 to 1
- obs_cells: int32 [2048], P(('cores', 'face')), may hold values from 0 to 1023
- obs_values: float32 [2048], P(('cores', 'face')), may hold values from 0 to 1
- obs_sigma: float32 [2048], P(('cores', 'face')), may hold values from 0.3 to 3
Outputs:
- analysis: bfloat16 [3, 16, 16, 128, 256], P(None, 'cores', 'face')
The draws below stay inside these ranges and needn't reach their ends.
Inputs may be any that keep to these rules, and one draw needn't show every extreme that they name: obs_cells holds the index (z * 4 + x) * 128 + y of a cell in the block of the device that holds the observation.
All inputs are finite; a program needn't handle non-finite values. No bound on the sum of `pore_mask` on one device may be relied on, other than what follows from the above.
Results may differ from the reference program's by a relative error of at most 0.0091.
Values may be sent and summed in bfloat16 or wider, within the bound.
No kernel may reach another device: no remote copies, remote signals or barrier semaphores. Data moves between devices by JAX's collectives and lax.ppermute only.
A program may use at most 64 MiB of HBM per device.

```python
import math
import jax
import jax.numpy as jnp
from jax import lax

MEM = 256
CH = 32
CZ = 2
CX = 4
CY = 128
OBS = 64
CELLS_CORE_AXIS = 16
CELLS_FIRST_DIM = 16
NOBS = 2048
N_FACE = 4


def plant(array, key, smallest, largest):
    shape = array.shape
    index_at = [jax.random.randint(jax.random.fold_in(key, axis), (), 0, shape[axis]) for axis in range(len(shape))]
    array = array.at[tuple(index_at)].set(smallest)
    longest = shape.index(max(shape))
    index_at[longest] = (index_at[longest] + 1) % shape[longest]
    return array.at[tuple(index_at)].set(largest)


def steps_of(own_key, extent, split, smallest, top_value):
    loudness = 1.0
    for dim, shards_of in split:
        draws = jax.random.uniform(jax.random.fold_in(jax.random.fold_in(own_key, 6), dim), (shards_of,), jnp.float32, smallest / len(split), top_value / len(split))
        loudness = loudness * jnp.repeat(jnp.exp(draws), extent[dim] // shards_of).reshape((-1,) + (1,) * (len(extent) - 1 - dim))
    return loudness


def centred(stream_key, shape, width, most, cuts=(), kind=jnp.bfloat16):
    entries = width * jax.random.normal(stream_key, shape, jnp.float32)
    if cuts:
        entries = entries * steps_of(stream_key, shape, cuts, -0.22, 0.18)
    return jnp.clip(entries, -most, most).astype(kind)


def setup_inputs(seed: int = 0) -> dict:
    key_of = jax.random.split(jax.random.key(seed), 9)
    fields = centred(key_of[0], (2, CELLS_CORE_AXIS, CELLS_FIRST_DIM, CY, MEM), 1.0, 6.0, ((1, 8), (2, 4)))
    pore_mask = plant((jax.random.randint(key_of[1], (CELLS_CORE_AXIS, CELLS_FIRST_DIM, CY), 0, 4) < 3).astype(jnp.int32), jax.random.fold_in(key_of[1], 1), 0, 1)
    conv_kernel = centred(key_of[2], (54, CH), 54 ** -0.5, 0.875)
    conv_bias = centred(key_of[3], (CH,), 0.5, 3.0, (), jnp.float32)
    read_weight = centred(key_of[4], (CH,), CH ** -0.5, 1.0, (), jnp.float32)
    obs_cells = plant(jax.random.randint(key_of[5], (NOBS,), 0, CZ * CX * CY), jax.random.fold_in(key_of[5], 1), 0, (CZ * CX * CY) - 1).astype(jnp.int32)
    obs_values = jnp.clip(1.0 * jax.random.uniform(key_of[6], (NOBS,), jnp.float32) ** steps_of(key_of[6], (NOBS,), ((0, 32),), -0.2, 0.2), 0.0, 1.0)
    obs_sigma = jnp.clip(jnp.exp(math.log(3.0) - 2.3025851 * jax.random.uniform(key_of[7], (NOBS,), jnp.float32) ** steps_of(key_of[7], (NOBS,), ((0, 32),), -0.2, 0.2)), 0.3, 3.0)
    return {"fields": fields, "pore_mask": pore_mask, "conv_kernel": conv_kernel, "conv_bias": conv_bias, "read_weight": read_weight, "obs_cells": obs_cells, "obs_values": obs_values, "obs_sigma": obs_sigma}


def ensemble_terms(predicted, obs_values, obs_sigma):
    members = predicted.shape[1]
    root_count = math.sqrt(members - 1)
    center = lax.optimization_barrier(jnp.mean(predicted, axis=1))
    spread = predicted - center[:, None]
    inverse_sigma = 1.0 / obs_sigma
    scaled = spread * (inverse_sigma / root_count)[:, None]
    innovation = (obs_values - center) * inverse_sigma
    gram_part = jnp.einsum('om,on->mn', scaled, scaled, precision=lax.Precision.HIGHEST)
    coeff_part = jnp.einsum('om,o->m', scaled, innovation, precision=lax.Precision.HIGHEST) / root_count
    return (gram_part, coeff_part)

def finish_mixing(gram_sum, coeff_sum):
    members = gram_sum.shape[0]
    identity = jnp.eye(members, dtype=jnp.float32)
    lower_factor = jnp.linalg.cholesky(gram_sum + identity)
    transform = jax.scipy.linalg.solve_triangular(lower_factor, identity, lower=True, trans='T')
    mean_weights = jax.scipy.linalg.cho_solve((lower_factor, True), coeff_sum)
    return (transform + mean_weights[:, None]).astype(jnp.bfloat16)

def blend_state(state, mixing):
    members = state.shape[-1]
    state_float = state.astype(jnp.float32)
    state_mean = lax.optimization_barrier(jnp.mean(state_float, axis=-1, keepdims=True))
    anomalies = (state_float - state_mean).astype(jnp.bfloat16)
    moved = jnp.dot(anomalies.reshape(-1, members).astype(jnp.float32), mixing.astype(jnp.float32), preferred_element_type=jnp.float32)
    return (state_mean + moved.reshape(state.shape)).astype(jnp.bfloat16)

def reference(fields, pore_mask, conv_kernel, conv_bias, read_weight, obs_cells, obs_values, obs_sigma):
    wrapped = jnp.concatenate([fields[:, -1:], fields, fields[:, :1]], axis=1)
    padded = jnp.pad(wrapped, ((0, 0), (0, 0), (1, 1), (1, 1), (0, 0)))
    mask_float = pore_mask.astype(jnp.float32)
    kernel_float = conv_kernel.astype(jnp.float32)
    zero_index = jnp.int32(0)

    def prior_row(current_row):
        plane_index = (current_row // CELLS_FIRST_DIM).astype(jnp.int32)
        column_index = (current_row % CELLS_FIRST_DIM).astype(jnp.int32)
        window = lax.dynamic_slice(padded, (zero_index, plane_index, column_index, zero_index, zero_index), (2, 3, 3, CY + 2, MEM))
        stencil_taps = jnp.stack([window[:, :, :, offset:offset + CY, :] for offset in range(3)], axis=3).reshape(54, CY * MEM)
        hidden = jnp.einsum('kc,kn->cn', kernel_float, stencil_taps.astype(jnp.float32), precision=lax.Precision.HIGHEST)
        hidden = jax.nn.silu(hidden + conv_bias[:, None])
        logits_sat = jnp.einsum('c,cn->n', read_weight, hidden, precision=lax.Precision.HIGHEST)
        row_mask = lax.dynamic_slice(mask_float, (plane_index, column_index, zero_index), (1, 1, CY)).reshape(CY, 1)
        return (jax.nn.sigmoid(logits_sat).reshape(CY, MEM) * row_mask).astype(jnp.bfloat16)
    finished_rows = lax.map(prior_row, jnp.arange(CELLS_CORE_AXIS * CELLS_FIRST_DIM, dtype=jnp.int32))
    saturation = finished_rows.reshape(CELLS_CORE_AXIS, CELLS_FIRST_DIM, CY, MEM)
    owner = jnp.arange(NOBS, dtype=jnp.int32) // OBS
    core_slot = owner // N_FACE
    face_slot = owner % N_FACE
    plane_of = core_slot * CZ + obs_cells // (CX * CY)
    column_of = face_slot * CX + obs_cells // CY % CX
    lane_of = obs_cells % CY
    predicted = saturation[plane_of, column_of, lane_of].astype(jnp.float32)
    gram_sum, coeff_sum = ensemble_terms(predicted, obs_values, obs_sigma)
    mixing = finish_mixing(gram_sum, coeff_sum)

    def update_plane(plane_index):
        part_fields = lax.dynamic_index_in_dim(fields, plane_index, 1, keepdims=False)
        part_sat = lax.dynamic_index_in_dim(saturation, plane_index, 0, keepdims=True)
        state = jnp.concatenate([part_fields, part_sat], axis=0)
        return blend_state(state, mixing)
    planes_done = lax.map(update_plane, jnp.arange(CELLS_CORE_AXIS, dtype=jnp.int32))
    return jnp.moveaxis(planes_done, 0, 1)
```

```python
import functools
import math

import jax
import jax.numpy as jnp
import numpy as np
from jax import lax
from jax.experimental import pallas as pl
from jax.experimental.pallas import tpu as pltpu
from jax.sharding import PartitionSpec as P

HIGHEST = lax.Precision.HIGHEST
PAY_ROWS = 16
GATHER_DEVICES = 64
BLOCK = 64
VMEM_BYTES = 48 * 1024 * 1024


def plane_places(planes, columns):
    own = [(f, z + 1, x + 1) for f in range(2) for z in range(planes) for x in range(columns)]
    low = [(f, 0, x + 1) for f in range(2) for x in range(columns)]
    high = [(f, planes + 1, x + 1) for f in range(2) for x in range(columns)]
    left = [(f, z + 1, 0) for f in range(2) for z in range(planes)]
    right = [(f, z + 1, columns + 1) for f in range(2) for z in range(planes)]
    corner_left = [(f, z, 0) for f in range(2) for z in (0, planes + 1)]
    corner_right = [(f, z, columns + 1) for f in range(2) for z in (0, planes + 1)]
    return own + low + high + left + right + corner_left + corner_right


def tap_selector(planes, columns):
    places = plane_places(planes, columns)
    chosen = np.zeros((54, planes * columns, 3 * len(places)), np.float32)
    for z in range(planes):
        for x in range(columns):
            for n, (f, zz, xx) in enumerate(places):
                a, b = zz - z, xx - x
                if 0 <= a <= 2 and 0 <= b <= 2:
                    for c in range(3):
                        chosen[27 * f + 9 * a + 3 * b + c, z * columns + x, c * len(places) + n] = 1.0
    return chosen


def swap_matrix(outer, inner):
    matrix = np.zeros((outer * inner, outer * inner), np.float32)
    for i in range(outer):
        for j in range(inner):
            matrix[j * outer + i, i * inner + j] = 1.0
    return matrix


def three_pieces(value):
    first = lax.reduce_precision(value, 8, 7)
    second = lax.reduce_precision(value - first, 8, 7)
    third = lax.reduce_precision(value - first - second, 8, 7)
    return first, second, third


def surrogate_kernel(
    own, low, high, left, right, corner_left, corner_right, weights, swap_in, swap_out, mask,
    sigma, values, read_half, cells, sat_out, pay_out, packed, sat_rows, sat_float, pred
):
    lanes, members = own.shape[1], own.shape[2]
    count = packed.shape[1]
    rows = mask.shape[0]
    channels = read_half.shape[0]
    packed[0] = jnp.zeros((count, members), jnp.bfloat16)
    packed[lanes + 1] = jnp.zeros((count, members), jnp.bfloat16)

    def pack(step, carry):
        at = pl.multiple_of(step * 16, 16)
        groups = ((own,), (low, high), (left, right, corner_left, corner_right))
        for g, refs in enumerate(groups):
            parts = [ref[:, pl.ds(at, 16), :] for ref in refs]
            block = parts[0] if len(parts) == 1 else jnp.concatenate(parts, axis=0)
            moved = jnp.dot(
                swap_in[...], block.reshape(256, members), preferred_element_type=jnp.float32
            )
            packed[pl.ds(at + 1, 16), 16 * g : 16 * g + 16, :] = (
                moved.astype(jnp.bfloat16).reshape(16, 16, members)
            )
        return carry

    lax.fori_loop(0, lanes // 16, pack, 0)

    row_index = lax.broadcasted_iota(jnp.int32, (16, members), 0)
    ones = jnp.where(row_index < 3, 1.0, 0.0).astype(jnp.bfloat16)
    lane_index = lax.broadcasted_iota(jnp.int32, (rows, lanes), 1)

    def two_rows(step, carry):
        found = []
        for k in range(2):
            y = step * 2 + k
            taps = jnp.concatenate(
                [packed[pl.ds(y, 3)].reshape(3 * count, members), ones], axis=0
            )
            half = jnp.dot(weights[...], taps, preferred_element_type=jnp.float32)
            total = jnp.zeros((rows, members), jnp.float32)
            for c in range(channels):
                part = half[rows * c : rows * c + rows]
                total = total + read_half[c] * (part * (1.0 + jnp.tanh(part)))
            here = jnp.sum(jnp.where(lane_index == y, mask[...], 0.0), axis=1, keepdims=True)
            found.append(here * (0.5 + 0.5 * jnp.tanh(total)))
        both = jnp.concatenate(found, axis=0).astype(jnp.bfloat16)
        at = pl.multiple_of(step * 2 * rows, 2 * rows)
        sat_rows[pl.ds(at, 2 * rows), :] = both
        sat_float[pl.ds(at, 2 * rows), :] = both.astype(jnp.float32)
        return carry

    lax.fori_loop(0, lanes // 2, two_rows, 0)

    span = 256 // rows
    for b in range(lanes // span):
        moved = jnp.dot(
            swap_out[...], sat_rows[256 * b : 256 * b + 256, :], preferred_element_type=jnp.float32
        )
        sat_out[:, span * b : span * b + span, :] = moved.astype(jnp.bfloat16).reshape(
            rows, span, members
        )

    for o in range(cells.shape[0]):
        cell = cells[o]
        row = (cell % lanes) * rows + cell // lanes
        pred[o : o + 1, :] = sat_float[pl.ds(row, 1), :]

    root_count = math.sqrt(members - 1)
    predicted = pred[...]
    center = jnp.mean(predicted, axis=1, keepdims=True)
    inverse_sigma = 1.0 / sigma[...]
    scaled = (predicted - center) * (inverse_sigma / root_count)
    innovation = (values[...] - center) * inverse_sigma
    coeff = jnp.sum(scaled * innovation, axis=0, keepdims=True) / root_count
    first = coeff.astype(jnp.bfloat16).astype(jnp.float32)
    second = (coeff - first).astype(jnp.bfloat16).astype(jnp.float32)
    third = coeff - first - second
    index = lax.broadcasted_iota(jnp.int32, (PAY_ROWS, members), 0)
    tail = jnp.where(index == 0, first, jnp.where(index == 1, second, jnp.where(index == 2, third, 0.0)))
    observed = cells.shape[0]
    pay_out[0:observed, :] = scaled.astype(jnp.bfloat16)
    pay_out[observed : observed + PAY_ROWS, :] = tail.astype(jnp.bfloat16)


def transposed_dot(a, b, precision):
    return lax.dot_general(
        a, b, (((0,), (0,)), ((), ())), preferred_element_type=jnp.float32, precision=precision
    )


def inverse_factor_block(block):
    lane = lax.broadcasted_iota(jnp.int32, (8, 2 * BLOCK), 1)
    sub = lax.broadcasted_iota(jnp.int32, (8, 2 * BLOCK), 0)
    parts = []
    for i in range(BLOCK // 8):
        unit = jnp.where(lane == sub + (BLOCK + 8 * i), 1.0, 0.0)
        known = jnp.concatenate(
            [block[8 * i : 8 * i + 8, :], jnp.zeros((8, BLOCK), jnp.float32)], axis=1
        )
        parts.append(known + unit)
    pivots = [jnp.ones((8, 2 * BLOCK), jnp.float32) for _ in parts]
    for j in range(BLOCK):
        top, inner = j // 8, j % 8
        row = jnp.broadcast_to(parts[top][inner : inner + 1, :], (8, 2 * BLOCK))
        pivot = jnp.broadcast_to(row[:, j : j + 1], (8, 2 * BLOCK))
        pivots[top] = jnp.where(sub == inner, pivot, pivots[top])
        row = row * (1.0 / pivot)
        for i in range(top, BLOCK // 8):
            column = jnp.broadcast_to(parts[i][:, j : j + 1], (8, 2 * BLOCK))
            if i == top:
                column = jnp.where(sub > inner, column, 0.0)
            parts[i] = parts[i] - column * row
    return jnp.concatenate(
        [(part * lax.rsqrt(pivot))[:, BLOCK:] for part, pivot in zip(parts, pivots)], axis=0
    )


def update_kernel(gathered, *refs):
    if gathered:
        pay, fields, sat, out, joint, mixing = refs
    else:
        gram, coeff_in, fields, sat, out, joint, mixing = refs
    members = fields.shape[1]
    sub = lax.broadcasted_iota(jnp.int32, (members, members), 0)
    lane = lax.broadcasted_iota(jnp.int32, (members, members), 1)
    identity = jnp.where(sub == lane, 1.0, 0.0)
    if gathered:
        devices, observed = pay.shape[0], pay.shape[1] - PAY_ROWS
        group = max(1, 256 // observed)
        total = identity
        for d in range(0, devices, group):
            block = pay[d : d + group, 0:observed, :].reshape(-1, members)
            total = total + transposed_dot(block, block, None)
        coeff = jnp.zeros((PAY_ROWS, members), jnp.float32)
        for d in range(devices):
            coeff = coeff + pay[d, observed:, :].astype(jnp.float32)
        coeff = jnp.sum(coeff, axis=0, keepdims=True)
    else:
        total = identity + gram[...]
        coeff = coeff_in[...]
    joint[:, 0:members] = total
    joint[:, members:] = identity
    for k in range(members // BLOCK):
        at = k * BLOCK
        inverse = inverse_factor_block(joint[at : at + BLOCK, at : at + BLOCK])
        rows = jnp.dot(
            inverse, joint[at : at + BLOCK, :], precision=HIGHEST, preferred_element_type=jnp.float32
        )
        joint[at : at + BLOCK, :] = rows
        if at + BLOCK < members:
            joint[at + BLOCK :, :] = joint[at + BLOCK :, :] - transposed_dot(
                rows[:, at + BLOCK : members], rows, HIGHEST
            )
    inverse = joint[:, members:]
    wide = jnp.broadcast_to(coeff, (8, members))
    half = lax.dot_general(
        wide, inverse, (((1,), (1,)), ((), ())), preferred_element_type=jnp.float32, precision=HIGHEST
    )
    weight = jnp.dot(half, inverse, preferred_element_type=jnp.float32, precision=HIGHEST)
    mixing[...] = jnp.transpose(inverse + weight[0:1, :]).astype(jnp.bfloat16)

    def blend(source, target, base):
        span = 256

        def step(s, carry):
            at = pl.multiple_of(s * span, span)
            state = source[pl.ds(at, span), :].astype(jnp.float32)
            mean = jnp.mean(state, axis=1, keepdims=True)
            anomalies = (state - mean).astype(jnp.bfloat16)
            moved = jnp.dot(anomalies, mixing[...], preferred_element_type=jnp.float32)
            target[pl.ds(base + at, span), :] = (mean + moved).astype(jnp.bfloat16)
            return carry

        lax.fori_loop(0, source.shape[0] // span, step, 0)

    blend(fields, out, 0)
    blend(sat, out, fields.shape[0])


def shift(value, axis, by, closed):
    count = lax.axis_size(axis)
    if by > 0:
        pairs = [(i, (i + 1) % count) for i in range(count if closed else count - 1)]
    else:
        pairs = [((i + 1) % count, i) for i in range(count if closed else count - 1)]
    return lax.ppermute(value, axis, pairs)


def gather_rows(block, steps):
    for axis, bit in steps:
        count = lax.axis_size(axis)
        other = lax.ppermute(block, axis, [(i, i ^ bit) for i in range(count)])
        block = jnp.concatenate([block, other], axis=0)
    return block


def bits_of(axis, count):
    bits = []
    while (1 << len(bits)) < count:
        bits.append((axis, 1 << len(bits)))
    return bits


def vmem():
    return pl.BlockSpec(memory_space=pltpu.VMEM)


def smem():
    return pl.BlockSpec(memory_space=pltpu.SMEM)


def shards(
    fields, pore_mask, conv_kernel, conv_bias, read_weight, obs_cells, obs_values, obs_sigma
):
    _, planes, columns, lanes, members = fields.shape
    channels = conv_kernel.shape[1]
    rows = planes * columns
    observed = obs_cells.shape[0]

    low = shift(fields[:, -1:], "cores", 1, True)
    high = shift(fields[:, :1], "cores", -1, True)
    left = shift(fields[:, :, -1:], "face", 1, False)
    right = shift(fields[:, :, :1], "face", -1, False)
    corner_left = shift(
        jnp.concatenate([low[:, :, -1:], high[:, :, -1:]], axis=1), "face", 1, False
    )
    corner_right = shift(
        jnp.concatenate([low[:, :, :1], high[:, :, :1]], axis=1), "face", -1, False
    )

    selector = tap_selector(planes, columns)
    count = selector.shape[2] // 3
    taps = jnp.dot(
        jnp.transpose(conv_kernel),
        jnp.asarray(selector.reshape(54, -1), jnp.bfloat16),
        preferred_element_type=jnp.float32,
    ).reshape(channels, rows, 3 * count)
    bias = jnp.stack(three_pieces(0.5 * conv_bias), axis=1)
    bias = jnp.broadcast_to(bias[:, None, :], (channels, rows, 3))
    weights = (
        jnp.concatenate(
            [0.5 * taps, bias, jnp.zeros((channels, rows, 13), jnp.float32)], axis=2
        )
        .reshape(channels * rows, 3 * count + 16)
        .astype(jnp.bfloat16)
    )
    flat = lambda a: a.reshape(-1, lanes, members)
    sat, pay = pl.pallas_call(
        surrogate_kernel,
        out_shape=(
            jax.ShapeDtypeStruct((rows, lanes, members), jnp.bfloat16),
            jax.ShapeDtypeStruct((observed + PAY_ROWS, members), jnp.bfloat16),
        ),
        in_specs=[vmem()] * 13 + [smem()] * 2,
        out_specs=(vmem(), vmem()),
        scratch_shapes=[
            pltpu.VMEM((lanes + 2, count, members), jnp.bfloat16),
            pltpu.VMEM((rows * lanes, members), jnp.bfloat16),
            pltpu.VMEM((rows * lanes, members), jnp.float32),
            pltpu.VMEM((observed, members), jnp.float32),
        ],
        compiler_params=pltpu.CompilerParams(vmem_limit_bytes=VMEM_BYTES),
        name="surrogate",
    )(
        flat(fields), flat(low), flat(high), flat(left), flat(right), flat(corner_left),
        flat(corner_right), weights,
        jnp.asarray(swap_matrix(16, 16), jnp.bfloat16),
        jnp.asarray(swap_matrix(256 // rows, rows), jnp.bfloat16),
        pore_mask.reshape(rows, lanes).astype(jnp.float32),
        obs_sigma.reshape(observed, 1), obs_values.reshape(observed, 1),
        0.5 * read_weight, obs_cells,
    )

    core_count, face_count = lax.axis_size("cores"), lax.axis_size("face")
    devices = core_count * face_count
    gathered = devices <= GATHER_DEVICES and devices & (devices - 1) == 0
    if gathered:
        steps = bits_of("face", face_count)[::-1] + bits_of("cores", core_count)[1:]
        steps = steps + bits_of("cores", core_count)[:1]
        terms = (gather_rows(pay[None], steps),)
    else:
        part = pay[:observed]
        gram = lax.dot_general(
            part, part, (((0,), (0,)), ((), ())), preferred_element_type=jnp.float32
        )
        coeff = jnp.sum(pay[observed:].astype(jnp.float32), axis=0, keepdims=True)
        terms = lax.psum((gram, coeff), ("cores", "face"))
    out = pl.pallas_call(
        functools.partial(update_kernel, gathered),
        out_shape=jax.ShapeDtypeStruct((3 * rows * lanes, members), jnp.bfloat16),
        in_specs=[vmem()] * (len(terms) + 2),
        out_specs=vmem(),
        scratch_shapes=[
            pltpu.VMEM((members, 2 * members), jnp.float32),
            pltpu.VMEM((members, members), jnp.bfloat16),
        ],
        compiler_params=pltpu.CompilerParams(vmem_limit_bytes=VMEM_BYTES),
        name="update",
    )(*terms, fields.reshape(-1, members), sat.reshape(-1, members))
    return out.reshape(3, planes, columns, lanes, members)


def solution(mesh):
    return jax.shard_map(
        shards,
        mesh=mesh,
        in_specs=(
            P(None, "cores", "face", None, None),
            P("cores", "face", None),
            P(),
            P(),
            P(),
            P(("cores", "face")),
            P(("cores", "face")),
            P(("cores", "face")),
        ),
        out_specs=P(None, "cores", "face", None, None),
        check_vma=False,
    )
```

```python
import functools
import math

import jax
import jax.numpy as jnp
import numpy as np
from jax import lax
from jax.experimental import pallas as pl
from jax.experimental.pallas import tpu as pltpu
from jax.sharding import PartitionSpec as P

HIGHEST = lax.Precision.HIGHEST
PAY_ROWS = 16
GATHER_DEVICES = 64
BLOCK = 64
PIECES = 4
VMEM_BYTES = 32 * 1024 * 1024


def plane_places(planes, columns):
    own = [(f, z + 1, x + 1) for f in range(2) for z in range(planes) for x in range(columns)]
    low = [(f, 0, x + 1) for f in range(2) for x in range(columns)]
    high = [(f, planes + 1, x + 1) for f in range(2) for x in range(columns)]
    left = [(f, z + 1, 0) for f in range(2) for z in range(planes)]
    right = [(f, z + 1, columns + 1) for f in range(2) for z in range(planes)]
    corner_left = [(f, z, 0) for f in range(2) for z in (0, planes + 1)]
    corner_right = [(f, z, columns + 1) for f in range(2) for z in (0, planes + 1)]
    return own + low + high + left + right + corner_left + corner_right


def tap_selector(planes, columns):
    places = plane_places(planes, columns)
    chosen = np.zeros((54, planes * columns, 3 * len(places)), np.float32)
    for z in range(planes):
        for x in range(columns):
            for n, (f, zz, xx) in enumerate(places):
                a, b = zz - z, xx - x
                if 0 <= a <= 2 and 0 <= b <= 2:
                    for c in range(3):
                        chosen[27 * f + 9 * a + 3 * b + c, z * columns + x, c * len(places) + n] = 1.0
    return chosen


def swap_matrix(outer, inner):
    matrix = np.zeros((outer * inner, outer * inner), np.float32)
    for i in range(outer):
        for j in range(inner):
            matrix[j * outer + i, i * inner + j] = 1.0
    return matrix


def three_pieces(value):
    first = lax.reduce_precision(value, 8, 7)
    second = lax.reduce_precision(value - first, 8, 7)
    third = lax.reduce_precision(value - first - second, 8, 7)
    return first, second, third


def ones_rows(members):
    row_index = lax.broadcasted_iota(jnp.int32, (16, members), 0)
    return jnp.where(row_index < 3, 1.0, 0.0).astype(jnp.bfloat16)


def observe_kernel(
    own, low, high, left, right, corner_left, corner_right, by_row, swap_in, read_column,
    sigma, values, cells, mask, packed, pay_out, pred
):
    lanes, members = own.shape[1], own.shape[2]
    count = packed.shape[1]
    observed = cells.shape[0]
    packed[0] = jnp.zeros((count, members), jnp.bfloat16)
    packed[lanes + 1] = jnp.zeros((count, members), jnp.bfloat16)

    def pack(step, carry):
        at = pl.multiple_of(step * 16, 16)
        groups = ((own,), (low, high), (left, right, corner_left, corner_right))
        for g, refs in enumerate(groups):
            parts = [ref[:, pl.ds(at, 16), :] for ref in refs]
            block = parts[0] if len(parts) == 1 else jnp.concatenate(parts, axis=0)
            moved = jnp.dot(
                swap_in[...], block.reshape(256, members), preferred_element_type=jnp.float32
            )
            packed[pl.ds(at + 1, 16), 16 * g : 16 * g + 16, :] = (
                moved.astype(jnp.bfloat16).reshape(16, 16, members)
            )
        return carry

    lax.fori_loop(0, lanes // 16, pack, 0)
    ones = ones_rows(members)
    read = jnp.broadcast_to(read_column[...], (read_column.shape[0], members))

    def some_cells(step, carry):
        for k in range(4):
            o = step * 4 + k
            cell = cells[o]
            row, y = cell // lanes, cell % lanes
            taps = jnp.concatenate(
                [packed[pl.ds(y, 3)].reshape(3 * count, members), ones], axis=0
            )
            half = jnp.dot(by_row[row], taps, preferred_element_type=jnp.float32)
            total = jnp.sum(read * (half * (1.0 + jnp.tanh(half))), axis=0, keepdims=True)
            found = (0.5 + 0.5 * jnp.tanh(total)) * mask[row, y].astype(jnp.float32)
            pred[pl.ds(o, 1), :] = found.astype(jnp.bfloat16).astype(jnp.float32)
        return carry

    lax.fori_loop(0, observed // 4, some_cells, 0)

    root_count = math.sqrt(members - 1)
    predicted = pred[...]
    center = jnp.mean(predicted, axis=1, keepdims=True)
    inverse_sigma = 1.0 / sigma[...]
    scaled = (predicted - center) * (inverse_sigma / root_count)
    innovation = (values[...] - center) * inverse_sigma
    coeff = jnp.sum(scaled * innovation, axis=0, keepdims=True) / root_count
    first = coeff.astype(jnp.bfloat16).astype(jnp.float32)
    second = (coeff - first).astype(jnp.bfloat16).astype(jnp.float32)
    third = coeff - first - second
    index = lax.broadcasted_iota(jnp.int32, (PAY_ROWS, members), 0)
    tail = jnp.where(index == 0, first, jnp.where(index == 1, second, jnp.where(index == 2, third, 0.0)))
    pay_out[0:observed, :] = scaled.astype(jnp.bfloat16)
    pay_out[observed : observed + PAY_ROWS, :] = tail.astype(jnp.bfloat16)


def saturate_kernel(start, packed, weights, swap_out, mask, read_half, sat_out, sat_rows):
    rows, span, members = sat_out.shape
    count = packed.shape[1]
    channels = read_half.shape[0]
    ones = ones_rows(members)
    lane_index = lax.broadcasted_iota(jnp.int32, mask.shape, 1)

    def two_rows(step, carry):
        found = []
        for k in range(2):
            y = start + step * 2 + k
            taps = jnp.concatenate(
                [packed[pl.ds(y, 3)].reshape(3 * count, members), ones], axis=0
            )
            half = jnp.dot(weights[...], taps, preferred_element_type=jnp.float32)
            total = jnp.zeros((rows, members), jnp.float32)
            for c in range(channels):
                part = half[rows * c : rows * c + rows]
                total = total + read_half[c] * (part * (1.0 + jnp.tanh(part)))
            here = jnp.sum(jnp.where(lane_index == y, mask[...], 0.0), axis=1, keepdims=True)
            found.append(here * (0.5 + 0.5 * jnp.tanh(total)))
        at = pl.multiple_of(step * 2 * rows, 2 * rows)
        sat_rows[pl.ds(at, 2 * rows), :] = jnp.concatenate(found, axis=0).astype(jnp.bfloat16)
        return carry

    lax.fori_loop(0, span // 2, two_rows, 0)
    moved = jnp.dot(swap_out[...], sat_rows[...], preferred_element_type=jnp.float32)
    sat_out[...] = moved.astype(jnp.bfloat16).reshape(rows, span, members)


def transposed_dot(a, b, precision):
    return lax.dot_general(
        a, b, (((0,), (0,)), ((), ())), preferred_element_type=jnp.float32, precision=precision
    )


def spread_row(part, p):
    return jnp.broadcast_to(part[p : p + 1, :], part.shape)


def spread_lane(part, q):
    return jnp.broadcast_to(part[:, q : q + 1], part.shape)


def inverse_root(value):
    guess = lax.rsqrt(value)
    return guess * (1.5 - (0.5 * value) * (guess * guess))


def inverse_factor_block(block):
    lane = lax.broadcasted_iota(jnp.int32, (8, 2 * BLOCK), 1)
    sub = lax.broadcasted_iota(jnp.int32, (8, 2 * BLOCK), 0)
    groups = BLOCK // 8
    parts = []
    for i in range(groups):
        unit = jnp.where(lane == sub + (BLOCK + 8 * i), 1.0, 0.0)
        known = jnp.concatenate(
            [block[8 * i : 8 * i + 8, :], jnp.zeros((8, BLOCK), jnp.float32)], axis=1
        )
        parts.append(known + unit)
    done = []
    for j in range(groups):
        corner = [spread_lane(parts[j], 8 * j + q) for q in range(8)]
        entry = {(p, q): spread_row(corner[q], p) for q in range(8) for p in range(q, 8)}
        line = [spread_row(parts[j], p) for p in range(8)]
        near = j + 1 < groups
        if near:
            beside = [spread_lane(parts[j + 1], 8 * j + q) for q in range(8)]
        factor, scale = {}, []
        for q in range(8):
            root = inverse_root(entry[q, q])
            scale.append(root)
            line[q] = line[q] * root
            for p in range(q + 1, 8):
                factor[p, q] = entry[p, q] * root
            for t in range(q + 1, 8):
                for p in range(t, 8):
                    entry[p, t] = entry[p, t] - factor[p, q] * factor[t, q]
            for p in range(q + 1, 8):
                line[p] = line[p] - factor[p, q] * line[q]
            if near:
                lead = beside[q] * root
                for t in range(q + 1, 8):
                    beside[t] = beside[t] - lead * factor[t, q]
                parts[j + 1] = parts[j + 1] - lead * line[q]
        if j + 2 < groups:
            weighted = [None] * 8
            for q in range(7, -1, -1):
                rest = line[q]
                for p in range(q + 1, 8):
                    rest = rest - factor[p, q] * weighted[p]
                weighted[q] = rest * scale[q]
            for i in range(j + 2, groups):
                change = spread_lane(parts[i], 8 * j) * weighted[0]
                for q in range(1, 8):
                    change = change + spread_lane(parts[i], 8 * j + q) * weighted[q]
                parts[i] = parts[i] - change
        merged = line[0]
        for q in range(1, 8):
            merged = jnp.where(sub == q, line[q], merged)
        done.append(merged[:, BLOCK:])
    return jnp.concatenate(done, axis=0)


def update_kernel(gathered, *refs):
    if gathered:
        pay, refs = refs[0], refs[1:]
    else:
        gram, coeff_in, refs = refs[0], refs[1], refs[2:]
    fields, sats, (out, joint, mixing) = refs[0], refs[1:-3], refs[-3:]
    members = fields.shape[2]
    sub = lax.broadcasted_iota(jnp.int32, (members, members), 0)
    lane = lax.broadcasted_iota(jnp.int32, (members, members), 1)
    identity = jnp.where(sub == lane, 1.0, 0.0)
    if gathered:
        devices, observed = pay.shape[0], pay.shape[1] - PAY_ROWS
        group = max(1, 256 // observed)
        total = identity
        for d in range(0, devices, group):
            block = pay[d : d + group, 0:observed, :].reshape(-1, members)
            total = total + transposed_dot(block, block, None)
        coeff = jnp.zeros((PAY_ROWS, members), jnp.float32)
        for d in range(devices):
            coeff = coeff + pay[d, observed:, :].astype(jnp.float32)
        coeff = jnp.sum(coeff, axis=0, keepdims=True)
    else:
        total = identity + gram[...]
        coeff = coeff_in[...]
    joint[:, 0:members] = total
    joint[:, members:] = identity
    for k in range(members // BLOCK):
        at = k * BLOCK
        inverse = inverse_factor_block(joint[at : at + BLOCK, at : at + BLOCK])
        rows = jnp.dot(
            inverse, joint[at : at + BLOCK, :], precision=HIGHEST, preferred_element_type=jnp.float32
        )
        joint[at : at + BLOCK, :] = rows
        if at + BLOCK < members:
            joint[at + BLOCK :, :] = joint[at + BLOCK :, :] - transposed_dot(
                rows[:, at + BLOCK : members], rows, HIGHEST
            )
    inverse = joint[:, members:]
    wide = jnp.broadcast_to(coeff, (8, members))
    half = lax.dot_general(
        wide, inverse, (((1,), (1,)), ((), ())), preferred_element_type=jnp.float32, precision=HIGHEST
    )
    weight = jnp.dot(half, inverse, preferred_element_type=jnp.float32, precision=HIGHEST)
    mixing[...] = jnp.transpose(inverse + weight[0:1, :]).astype(jnp.bfloat16)

    def blend(state):
        state = state.astype(jnp.float32)
        mean = jnp.mean(state, axis=1, keepdims=True)
        anomalies = (state - mean).astype(jnp.bfloat16)
        moved = jnp.dot(anomalies, mixing[...], preferred_element_type=jnp.float32)
        return (mean + moved).astype(jnp.bfloat16)

    field_rows, lanes = fields.shape[0], fields.shape[1]

    def step(n, carry):
        at = pl.multiple_of(2 * n, 2)
        block = fields[pl.ds(at, 2)].reshape(2 * lanes, members)
        out[pl.ds(at, 2)] = blend(block).reshape(2, lanes, members)
        return carry

    lax.fori_loop(0, field_rows // 2, step, 0)
    for n, sat in enumerate(sats):
        rows, span = sat.shape[0], sat.shape[1]
        out[field_rows:, n * span : (n + 1) * span, :] = blend(
            sat[...].reshape(rows * span, members)
        ).reshape(rows, span, members)


def shift(value, axis, by, closed):
    count = lax.axis_size(axis)
    if by > 0:
        pairs = [(i, (i + 1) % count) for i in range(count if closed else count - 1)]
    else:
        pairs = [((i + 1) % count, i) for i in range(count if closed else count - 1)]
    return lax.ppermute(value, axis, pairs)


def gather_rows(block, steps, packed, saturate):
    pieces = []
    for n, (axis, bit) in enumerate(steps):
        count = lax.axis_size(axis)
        if n < PIECES:
            block, packed = lax.optimization_barrier((block, packed))
        other = lax.ppermute(block, axis, [(i, i ^ bit) for i in range(count)])
        if n < PIECES:
            piece = saturate(n, packed)
        block = jnp.concatenate([block, other], axis=0)
        if n < PIECES:
            block, piece = lax.optimization_barrier((block, piece))
            pieces.append(piece)
    return block, pieces + [saturate(n, packed) for n in range(len(pieces), PIECES)]


def bits_of(axis, count):
    bits = []
    while (1 << len(bits)) < count:
        bits.append((axis, 1 << len(bits)))
    return bits


def vmem():
    return pl.BlockSpec(memory_space=pltpu.VMEM)


def smem():
    return pl.BlockSpec(memory_space=pltpu.SMEM)


def shards(
    fields, pore_mask, conv_kernel, conv_bias, read_weight, obs_cells, obs_values, obs_sigma
):
    _, planes, columns, lanes, members = fields.shape
    channels = conv_kernel.shape[1]
    rows = planes * columns
    observed = obs_cells.shape[0]

    low = shift(fields[:, -1:], "cores", 1, True)
    high = shift(fields[:, :1], "cores", -1, True)
    left = shift(fields[:, :, -1:], "face", 1, False)
    right = shift(fields[:, :, :1], "face", -1, False)
    corner_left = shift(
        jnp.concatenate([low[:, :, -1:], high[:, :, -1:]], axis=1), "face", 1, False
    )
    corner_right = shift(
        jnp.concatenate([low[:, :, :1], high[:, :, :1]], axis=1), "face", -1, False
    )

    selector = tap_selector(planes, columns)
    count = selector.shape[2] // 3
    taps = jnp.dot(
        jnp.transpose(conv_kernel),
        jnp.asarray(selector.reshape(54, -1), jnp.bfloat16),
        preferred_element_type=jnp.float32,
    ).reshape(channels, rows, 3 * count)
    bias = jnp.stack(three_pieces(0.5 * conv_bias), axis=1)
    bias = jnp.broadcast_to(bias[:, None, :], (channels, rows, 3))
    weights = jnp.concatenate(
        [0.5 * taps, bias, jnp.zeros((channels, rows, 13), jnp.float32)], axis=2
    ).astype(jnp.bfloat16)
    by_row = jnp.transpose(weights, (1, 0, 2))
    weights = weights.reshape(channels * rows, 3 * count + 16)
    flat = lambda a: a.reshape(-1, lanes, members)
    span = lanes // PIECES
    mask = pore_mask.reshape(rows, lanes)
    mask_float = mask.astype(jnp.float32)
    read_half = 0.5 * read_weight
    swap_in = jnp.asarray(swap_matrix(16, 16), jnp.bfloat16)
    swap_out = jnp.asarray(swap_matrix(span, rows), jnp.bfloat16)
    params = pltpu.CompilerParams(vmem_limit_bytes=VMEM_BYTES)
    packed, pay = pl.pallas_call(
        observe_kernel,
        out_shape=(
            jax.ShapeDtypeStruct((lanes + 2, count, members), jnp.bfloat16),
            jax.ShapeDtypeStruct((observed + PAY_ROWS, members), jnp.bfloat16),
        ),
        in_specs=[vmem()] * 12 + [smem()] * 2,
        out_specs=(vmem(), vmem()),
        scratch_shapes=[pltpu.VMEM((observed, members), jnp.float32)],
        compiler_params=params,
        name="observe",
    )(
        flat(fields), flat(low), flat(high), flat(left), flat(right), flat(corner_left),
        flat(corner_right), by_row, swap_in, read_half[:, None],
        obs_sigma[:, None], obs_values[:, None], obs_cells, mask,
    )

    def saturate(n, packed):
        return pl.pallas_call(
            functools.partial(saturate_kernel, n * span),
            out_shape=jax.ShapeDtypeStruct((rows, span, members), jnp.bfloat16),
            in_specs=[vmem()] * 4 + [smem()],
            out_specs=vmem(),
            scratch_shapes=[pltpu.VMEM((rows * span, members), jnp.bfloat16)],
            compiler_params=params,
            cost_estimate=pl.CostEstimate(
                flops=2 * 256 * 256 * span * members,
                bytes_accessed=4 * 1024 * 1024,
                transcendentals=channels * rows * span * members,
            ),
            name="saturate",
        )(packed, weights, swap_out, mask_float, read_half)

    core_count, face_count = lax.axis_size("cores"), lax.axis_size("face")
    devices = core_count * face_count
    gathered = devices <= GATHER_DEVICES and devices & (devices - 1) == 0
    if gathered:
        steps = bits_of("face", face_count)[::-1] + bits_of("cores", core_count)[1:]
        steps = steps + bits_of("cores", core_count)[:1]
        block, pieces = gather_rows(pay[None], steps, packed, saturate)
        terms = (block,)
    else:
        part = pay[:observed]
        gram = lax.dot_general(
            part, part, (((0,), (0,)), ((), ())), preferred_element_type=jnp.float32
        )
        coeff = jnp.sum(pay[observed:].astype(jnp.float32), axis=0, keepdims=True)
        terms = lax.psum((gram, coeff), ("cores", "face"))
        pieces = [saturate(n, packed) for n in range(PIECES)]
    out = pl.pallas_call(
        functools.partial(update_kernel, gathered),
        out_shape=jax.ShapeDtypeStruct((3 * rows, lanes, members), jnp.bfloat16),
        in_specs=[vmem()] * (len(terms) + 1 + PIECES),
        out_specs=vmem(),
        scratch_shapes=[
            pltpu.VMEM((members, 2 * members), jnp.float32),
            pltpu.VMEM((members, members), jnp.bfloat16),
        ],
        compiler_params=params,
        name="update",
    )(*terms, flat(fields), *pieces)
    return out.reshape(3, planes, columns, lanes, members)


def solution(mesh):
    return jax.shard_map(
        shards,
        mesh=mesh,
        in_specs=(
            P(None, "cores", "face", None, None),
            P("cores", "face", None),
            P(),
            P(),
            P(),
            P(("cores", "face")),
            P(("cores", "face")),
            P(("cores", "face")),
        ),
        out_specs=P(None, "cores", "face", None, None),
        check_vma=False,
    )
```

```python
import functools
import math

import jax
import jax.numpy as jnp
import numpy as np
from jax import lax
from jax.experimental import pallas as pl
from jax.experimental.pallas import tpu as pltpu
from jax.sharding import PartitionSpec as P

HIGHEST = lax.Precision.HIGHEST
PAY_ROWS = 16
GATHER_DEVICES = 64
BLOCK = 64
PIECES = 4
VMEM_BYTES = 32 * 1024 * 1024


def plane_places(planes, columns):
    own = [(f, z + 1, x + 1) for f in range(2) for z in range(planes) for x in range(columns)]
    low = [(f, 0, x + 1) for f in range(2) for x in range(columns)]
    high = [(f, planes + 1, x + 1) for f in range(2) for x in range(columns)]
    left = [(f, z + 1, 0) for f in range(2) for z in range(planes)]
    right = [(f, z + 1, columns + 1) for f in range(2) for z in range(planes)]
    corner_low = [(f, 0, x) for f in range(2) for x in (0, columns + 1)]
    corner_high = [(f, planes + 1, x) for f in range(2) for x in (0, columns + 1)]
    return own + low + high + left + right + corner_low + corner_high


def tap_selector(planes, columns):
    places = plane_places(planes, columns)
    chosen = np.zeros((54, planes * columns, 3 * len(places)), np.float32)
    for z in range(planes):
        for x in range(columns):
            for n, (f, zz, xx) in enumerate(places):
                a, b = zz - z, xx - x
                if 0 <= a <= 2 and 0 <= b <= 2:
                    for c in range(3):
                        chosen[27 * f + 9 * a + 3 * b + c, z * columns + x, c * len(places) + n] = 1.0
    return chosen


def swap_matrix(outer, inner):
    matrix = np.zeros((outer * inner, outer * inner), np.float32)
    for i in range(outer):
        for j in range(inner):
            matrix[j * outer + i, i * inner + j] = 1.0
    return matrix


def three_pieces(value):
    first = lax.reduce_precision(value, 8, 7)
    second = lax.reduce_precision(value - first, 8, 7)
    third = lax.reduce_precision(value - first - second, 8, 7)
    return first, second, third


def ones_rows(members):
    row_index = lax.broadcasted_iota(jnp.int32, (16, members), 0)
    return jnp.where(row_index < 3, 1.0, 0.0).astype(jnp.bfloat16)


def observe_kernel(
    own, low, high, left, right, corner_low, corner_high, by_row, swap_in, read_column,
    sigma, values, cells, mask, packed, pay_out, pred
):
    lanes, members = own.shape[1], own.shape[2]
    count = packed.shape[1]
    observed = cells.shape[0]
    packed[0] = jnp.zeros((count, members), jnp.bfloat16)
    packed[lanes + 1] = jnp.zeros((count, members), jnp.bfloat16)

    def pack(step, carry):
        at = pl.multiple_of(step * 16, 16)
        groups = ((own,), (low, high), (left, right, corner_low, corner_high))
        for g, refs in enumerate(groups):
            parts = [ref[:, pl.ds(at, 16), :] for ref in refs]
            block = parts[0] if len(parts) == 1 else jnp.concatenate(parts, axis=0)
            moved = jnp.dot(
                swap_in[...], block.reshape(256, members), preferred_element_type=jnp.float32
            )
            packed[pl.ds(at + 1, 16), 16 * g : 16 * g + 16, :] = (
                moved.astype(jnp.bfloat16).reshape(16, 16, members)
            )
        return carry

    lax.fori_loop(0, lanes // 16, pack, 0)
    ones = ones_rows(members)
    read = jnp.broadcast_to(read_column[...], (read_column.shape[0], members))

    def some_cells(step, carry):
        for k in range(4):
            o = step * 4 + k
            cell = cells[o]
            row, y = cell // lanes, cell % lanes
            taps = jnp.concatenate(
                [packed[pl.ds(y, 3)].reshape(3 * count, members), ones], axis=0
            )
            half = jnp.dot(by_row[row], taps, preferred_element_type=jnp.float32)
            total = jnp.sum(read * (half * (1.0 + jnp.tanh(half))), axis=0, keepdims=True)
            found = (0.5 + 0.5 * jnp.tanh(total)) * mask[row, y].astype(jnp.float32)
            pred[pl.ds(o, 1), :] = found.astype(jnp.bfloat16).astype(jnp.float32)
        return carry

    lax.fori_loop(0, observed // 4, some_cells, 0)

    root_count = math.sqrt(members - 1)
    predicted = pred[...]
    center = jnp.mean(predicted, axis=1, keepdims=True)
    inverse_sigma = 1.0 / sigma[...]
    scaled = (predicted - center) * (inverse_sigma / root_count)
    innovation = (values[...] - center) * inverse_sigma
    coeff = jnp.sum(scaled * innovation, axis=0, keepdims=True) / root_count
    first = coeff.astype(jnp.bfloat16).astype(jnp.float32)
    second = (coeff - first).astype(jnp.bfloat16).astype(jnp.float32)
    third = coeff - first - second
    index = lax.broadcasted_iota(jnp.int32, (PAY_ROWS, members), 0)
    tail = jnp.where(index == 0, first, jnp.where(index == 1, second, jnp.where(index == 2, third, 0.0)))
    pay_out[0:observed, :] = scaled.astype(jnp.bfloat16)
    pay_out[observed : observed + PAY_ROWS, :] = tail.astype(jnp.bfloat16)


def saturate_kernel(start, packed, weights, swap_out, mask, read_half, sat_out, sat_rows):
    rows, span, members = sat_out.shape
    count = packed.shape[1]
    channels = read_half.shape[0]
    ones = ones_rows(members)
    lane_index = lax.broadcasted_iota(jnp.int32, mask.shape, 1)

    def two_rows(step, carry):
        found = []
        for k in range(2):
            y = start + step * 2 + k
            taps = jnp.concatenate(
                [packed[pl.ds(y, 3)].reshape(3 * count, members), ones], axis=0
            )
            half = jnp.dot(weights[...], taps, preferred_element_type=jnp.float32)
            total = jnp.zeros((rows, members), jnp.float32)
            for c in range(channels):
                part = half[rows * c : rows * c + rows]
                total = total + read_half[c] * (part * (1.0 + jnp.tanh(part)))
            here = jnp.sum(jnp.where(lane_index == y, mask[...], 0.0), axis=1, keepdims=True)
            found.append(here * (0.5 + 0.5 * jnp.tanh(total)))
        at = pl.multiple_of(step * 2 * rows, 2 * rows)
        sat_rows[pl.ds(at, 2 * rows), :] = jnp.concatenate(found, axis=0).astype(jnp.bfloat16)
        return carry

    lax.fori_loop(0, span // 2, two_rows, 0)
    moved = jnp.dot(swap_out[...], sat_rows[...], preferred_element_type=jnp.float32)
    sat_out[...] = moved.astype(jnp.bfloat16).reshape(rows, span, members)


def transposed_dot(a, b, precision):
    return lax.dot_general(
        a, b, (((0,), (0,)), ((), ())), preferred_element_type=jnp.float32, precision=precision
    )


def spread_row(part, p):
    return jnp.broadcast_to(part[p : p + 1, :], part.shape)


def spread_lane(part, q):
    return jnp.broadcast_to(part[:, q : q + 1], part.shape)


def inverse_root(value):
    guess = lax.rsqrt(value)
    return guess * (1.5 - (0.5 * value) * (guess * guess))


def inverse_factor_block(block):
    lane = lax.broadcasted_iota(jnp.int32, (8, 2 * BLOCK), 1)
    sub = lax.broadcasted_iota(jnp.int32, (8, 2 * BLOCK), 0)
    groups = BLOCK // 8
    parts = []
    for i in range(groups):
        unit = jnp.where(lane == sub + (BLOCK + 8 * i), 1.0, 0.0)
        known = jnp.concatenate(
            [block[8 * i : 8 * i + 8, :], jnp.zeros((8, BLOCK), jnp.float32)], axis=1
        )
        parts.append(known + unit)
    done = []
    for j in range(groups):
        corner = [spread_lane(parts[j], 8 * j + q) for q in range(8)]
        entry = {(p, q): spread_row(corner[q], p) for q in range(8) for p in range(q, 8)}
        line = [spread_row(parts[j], p) for p in range(8)]
        near = j + 1 < groups
        if near:
            beside = [spread_lane(parts[j + 1], 8 * j + q) for q in range(8)]
        factor, scale = {}, []
        for q in range(8):
            root = inverse_root(entry[q, q])
            scale.append(root)
            line[q] = line[q] * root
            for p in range(q + 1, 8):
                factor[p, q] = entry[p, q] * root
            for t in range(q + 1, 8):
                for p in range(t, 8):
                    entry[p, t] = entry[p, t] - factor[p, q] * factor[t, q]
            for p in range(q + 1, 8):
                line[p] = line[p] - factor[p, q] * line[q]
            if near:
                lead = beside[q] * root
                for t in range(q + 1, 8):
                    beside[t] = beside[t] - lead * factor[t, q]
                parts[j + 1] = parts[j + 1] - lead * line[q]
        if j + 2 < groups:
            weighted = [None] * 8
            for q in range(7, -1, -1):
                rest = line[q]
                for p in range(q + 1, 8):
                    rest = rest - factor[p, q] * weighted[p]
                weighted[q] = rest * scale[q]
            for i in range(j + 2, groups):
                change = spread_lane(parts[i], 8 * j) * weighted[0]
                for q in range(1, 8):
                    change = change + spread_lane(parts[i], 8 * j + q) * weighted[q]
                parts[i] = parts[i] - change
        merged = line[0]
        for q in range(1, 8):
            merged = jnp.where(sub == q, line[q], merged)
        done.append(merged[:, BLOCK:])
    return jnp.concatenate(done, axis=0)


def update_kernel(gathered, *refs):
    if gathered:
        pay, refs = refs[0], refs[1:]
    else:
        gram, coeff_in, refs = refs[0], refs[1], refs[2:]
    fields, sats, (out, joint, mixing) = refs[0], refs[1:-3], refs[-3:]
    members = fields.shape[2]
    sub = lax.broadcasted_iota(jnp.int32, (members, members), 0)
    lane = lax.broadcasted_iota(jnp.int32, (members, members), 1)
    identity = jnp.where(sub == lane, 1.0, 0.0)
    if gathered:
        devices, observed = pay.shape[0], pay.shape[1] - PAY_ROWS
        group = max(1, 256 // observed)
        total = identity
        for d in range(0, devices, group):
            block = pay[d : d + group, 0:observed, :].reshape(-1, members)
            total = total + transposed_dot(block, block, None)
        coeff = jnp.zeros((PAY_ROWS, members), jnp.float32)
        for d in range(devices):
            coeff = coeff + pay[d, observed:, :].astype(jnp.float32)
        coeff = jnp.sum(coeff, axis=0, keepdims=True)
    else:
        total = identity + gram[...]
        coeff = coeff_in[...]
    joint[:, 0:members] = total
    joint[:, members:] = identity
    for k in range(members // BLOCK):
        at = k * BLOCK
        inverse = inverse_factor_block(joint[at : at + BLOCK, at : at + BLOCK])
        rows = jnp.dot(
            inverse, joint[at : at + BLOCK, :], precision=HIGHEST, preferred_element_type=jnp.float32
        )
        joint[at : at + BLOCK, :] = rows
        if at + BLOCK < members:
            joint[at + BLOCK :, :] = joint[at + BLOCK :, :] - transposed_dot(
                rows[:, at + BLOCK : members], rows, HIGHEST
            )
    inverse = joint[:, members:]
    wide = jnp.broadcast_to(coeff, (8, members))
    half = lax.dot_general(
        wide, inverse, (((1,), (1,)), ((), ())), preferred_element_type=jnp.float32, precision=HIGHEST
    )
    weight = jnp.dot(half, inverse, preferred_element_type=jnp.float32, precision=HIGHEST)
    mixing[...] = jnp.transpose(inverse + weight[0:1, :]).astype(jnp.bfloat16)

    def blend(state):
        state = state.astype(jnp.float32)
        mean = jnp.mean(state, axis=1, keepdims=True)
        anomalies = (state - mean).astype(jnp.bfloat16)
        moved = jnp.dot(anomalies, mixing[...], preferred_element_type=jnp.float32)
        return (mean + moved).astype(jnp.bfloat16)

    field_rows, lanes = fields.shape[0], fields.shape[1]

    def step(n, carry):
        at = pl.multiple_of(2 * n, 2)
        block = fields[pl.ds(at, 2)].reshape(2 * lanes, members)
        out[pl.ds(at, 2)] = blend(block).reshape(2, lanes, members)
        return carry

    lax.fori_loop(0, field_rows // 2, step, 0)
    for n, sat in enumerate(sats):
        rows, span = sat.shape[0], sat.shape[1]
        out[field_rows:, n * span : (n + 1) * span, :] = blend(
            sat[...].reshape(rows * span, members)
        ).reshape(rows, span, members)


def shift(value, axis, by, closed):
    count = lax.axis_size(axis)
    if by > 0:
        pairs = [(i, (i + 1) % count) for i in range(count if closed else count - 1)]
    else:
        pairs = [((i + 1) % count, i) for i in range(count if closed else count - 1)]
    return lax.ppermute(value, axis, pairs)


def vmem():
    return pl.BlockSpec(memory_space=pltpu.VMEM)


def smem():
    return pl.BlockSpec(memory_space=pltpu.SMEM)


def shards(
    fields, pore_mask, conv_kernel, conv_bias, read_weight, obs_cells, obs_values, obs_sigma
):
    _, planes, columns, lanes, members = fields.shape
    channels = conv_kernel.shape[1]
    rows = planes * columns
    observed = obs_cells.shape[0]

    left = shift(fields[:, :, -1:], "face", 1, False)
    right = shift(fields[:, :, :1], "face", -1, False)
    low = shift(fields[:, -1:], "cores", 1, True)
    high = shift(fields[:, :1], "cores", -1, True)
    corner_low = shift(
        jnp.concatenate([left[:, -1:], right[:, -1:]], axis=2), "cores", 1, True
    )
    corner_high = shift(
        jnp.concatenate([left[:, :1], right[:, :1]], axis=2), "cores", -1, True
    )

    selector = tap_selector(planes, columns)
    count = selector.shape[2] // 3
    taps = jnp.dot(
        jnp.transpose(conv_kernel),
        jnp.asarray(selector.reshape(54, -1), jnp.bfloat16),
        preferred_element_type=jnp.float32,
    ).reshape(channels, rows, 3 * count)
    bias = jnp.stack(three_pieces(0.5 * conv_bias), axis=1)
    bias = jnp.broadcast_to(bias[:, None, :], (channels, rows, 3))
    weights = jnp.concatenate(
        [0.5 * taps, bias, jnp.zeros((channels, rows, 13), jnp.float32)], axis=2
    ).astype(jnp.bfloat16)
    by_row = jnp.transpose(weights, (1, 0, 2))
    weights = weights.reshape(channels * rows, 3 * count + 16)
    flat = lambda a: a.reshape(-1, lanes, members)
    span = lanes // PIECES
    mask = pore_mask.reshape(rows, lanes)
    mask_float = mask.astype(jnp.float32)
    read_half = 0.5 * read_weight
    swap_in = jnp.asarray(swap_matrix(16, 16), jnp.bfloat16)
    swap_out = jnp.asarray(swap_matrix(span, rows), jnp.bfloat16)
    params = pltpu.CompilerParams(vmem_limit_bytes=VMEM_BYTES)
    packed, pay = pl.pallas_call(
        observe_kernel,
        out_shape=(
            jax.ShapeDtypeStruct((lanes + 2, count, members), jnp.bfloat16),
            jax.ShapeDtypeStruct((observed + PAY_ROWS, members), jnp.bfloat16),
        ),
        in_specs=[vmem()] * 12 + [smem()] * 2,
        out_specs=(vmem(), vmem()),
        scratch_shapes=[pltpu.VMEM((observed, members), jnp.float32)],
        compiler_params=params,
        name="observe",
    )(
        flat(fields), flat(low), flat(high), flat(left), flat(right), flat(corner_low),
        flat(corner_high), by_row, swap_in, read_half[:, None],
        obs_sigma[:, None], obs_values[:, None], obs_cells, mask,
    )

    def saturate(n, packed):
        return pl.pallas_call(
            functools.partial(saturate_kernel, n * span),
            out_shape=jax.ShapeDtypeStruct((rows, span, members), jnp.bfloat16),
            in_specs=[vmem()] * 4 + [smem()],
            out_specs=vmem(),
            scratch_shapes=[pltpu.VMEM((rows * span, members), jnp.bfloat16)],
            compiler_params=params,
            cost_estimate=pl.CostEstimate(
                flops=2 * 256 * 256 * span * members,
                bytes_accessed=4 * 1024 * 1024,
                transcendentals=channels * rows * span * members,
            ),
            name="saturate",
        )(packed, weights, swap_out, mask_float, read_half)

    core_count, face_count = lax.axis_size("cores"), lax.axis_size("face")
    devices = core_count * face_count
    gathered = devices <= GATHER_DEVICES and devices & (devices - 1) == 0
    if gathered:
        terms = (lax.all_gather(pay, ("cores", "face"), axis=0),)
    else:
        part = pay[:observed]
        gram = lax.dot_general(
            part, part, (((0,), (0,)), ((), ())), preferred_element_type=jnp.float32
        )
        coeff = jnp.sum(pay[observed:].astype(jnp.float32), axis=0, keepdims=True)
        terms = lax.psum((gram, coeff), ("cores", "face"))
    pieces = [saturate(n, packed) for n in range(PIECES)]
    out = pl.pallas_call(
        functools.partial(update_kernel, gathered),
        out_shape=jax.ShapeDtypeStruct((3 * rows, lanes, members), jnp.bfloat16),
        in_specs=[vmem()] * (len(terms) + 1 + PIECES),
        out_specs=vmem(),
        scratch_shapes=[
            pltpu.VMEM((members, 2 * members), jnp.float32),
            pltpu.VMEM((members, members), jnp.bfloat16),
        ],
        compiler_params=params,
        name="update",
    )(*terms, flat(fields), *pieces)
    return out.reshape(3, planes, columns, lanes, members)


def solution(mesh):
    return jax.shard_map(
        shards,
        mesh=mesh,
        in_specs=(
            P(None, "cores", "face", None, None),
            P("cores", "face", None),
            P(),
            P(),
            P(),
            P(("cores", "face")),
            P(("cores", "face")),
            P(("cores", "face")),
        ),
        out_specs=P(None, "cores", "face", None, None),
        check_vma=False,
    )
```

```python
import functools
import math

import jax
import jax.numpy as jnp
import numpy as np
from jax import lax
from jax.experimental import pallas as pl
from jax.experimental.pallas import tpu as pltpu
from jax.sharding import PartitionSpec as P

HIGHEST = lax.Precision.HIGHEST
PAY_ROWS = 16
GATHER_DEVICES = 64
BLOCK = 64
PIECES = 4
VMEM_BYTES = 32 * 1024 * 1024


def plane_places(planes, columns):
    own = [(f, z + 1, x + 1) for f in range(2) for z in range(planes) for x in range(columns)]
    low = [(f, 0, x + 1) for f in range(2) for x in range(columns)]
    high = [(f, planes + 1, x + 1) for f in range(2) for x in range(columns)]
    left = [(f, z + 1, 0) for f in range(2) for z in range(planes)]
    right = [(f, z + 1, columns + 1) for f in range(2) for z in range(planes)]
    corners = [
        (f, z, x) for x in (0, columns + 1) for z in (0, planes + 1) for f in range(2)
    ]
    return own + low + high + left + right + corners


def tap_selector(planes, columns):
    places = plane_places(planes, columns)
    chosen = np.zeros((54, planes * columns, 3 * len(places)), np.float32)
    for z in range(planes):
        for x in range(columns):
            for n, (f, zz, xx) in enumerate(places):
                a, b = zz - z, xx - x
                if 0 <= a <= 2 and 0 <= b <= 2:
                    for c in range(3):
                        chosen[27 * f + 9 * a + 3 * b + c, z * columns + x, c * len(places) + n] = 1.0
    return chosen


def swap_matrix(outer, inner):
    matrix = np.zeros((outer * inner, outer * inner), np.float32)
    for i in range(outer):
        for j in range(inner):
            matrix[j * outer + i, i * inner + j] = 1.0
    return matrix


def three_pieces(value):
    first = lax.reduce_precision(value, 8, 7)
    second = lax.reduce_precision(value - first, 8, 7)
    third = lax.reduce_precision(value - first - second, 8, 7)
    return first, second, third


def ones_rows(members):
    row_index = lax.broadcasted_iota(jnp.int32, (16, members), 0)
    return jnp.where(row_index < 3, 1.0, 0.0).astype(jnp.bfloat16)


def observe_kernel(
    own, low, high, left, right, low_left, high_left, low_right, high_right, by_row, swap_in, read_column,
    sigma, values, cells, mask, packed, pay_out, pred
):
    lanes, members = own.shape[1], own.shape[2]
    count = packed.shape[1]
    observed = cells.shape[0]
    packed[0] = jnp.zeros((count, members), jnp.bfloat16)
    packed[lanes + 1] = jnp.zeros((count, members), jnp.bfloat16)

    for step in range(lanes // 16):
        at = step * 16
        groups = ((own,), (low, high), (left, right, low_left, high_left, low_right, high_right))
        for g, refs in enumerate(groups):
            parts = [ref[:, pl.ds(at, 16), :] for ref in refs]
            block = parts[0] if len(parts) == 1 else jnp.concatenate(parts, axis=0)
            moved = jnp.dot(
                swap_in[...], block.reshape(256, members), preferred_element_type=jnp.float32
            )
            packed[pl.ds(at + 1, 16), 16 * g : 16 * g + 16, :] = (
                moved.astype(jnp.bfloat16).reshape(16, 16, members)
            )

    ones = ones_rows(members)
    read = jnp.broadcast_to(read_column[...], (read_column.shape[0], members))

    def some_cells(step, carry):
        for k in range(16):
            o = step * 16 + k
            cell = cells[o]
            row, y = cell // lanes, cell % lanes
            taps = jnp.concatenate(
                [packed[pl.ds(y, 3)].reshape(3 * count, members), ones], axis=0
            )
            half = jnp.dot(by_row[row], taps, preferred_element_type=jnp.float32)
            total = jnp.sum(read * (half * (1.0 + jnp.tanh(half))), axis=0, keepdims=True)
            found = (0.5 + 0.5 * jnp.tanh(total)) * mask[row, y].astype(jnp.float32)
            pred[pl.ds(o, 1), :] = found.astype(jnp.bfloat16).astype(jnp.float32)
        return carry

    lax.fori_loop(0, observed // 16, some_cells, 0)

    root_count = math.sqrt(members - 1)
    predicted = pred[...]
    center = jnp.mean(predicted, axis=1, keepdims=True)
    inverse_sigma = 1.0 / sigma[...]
    scaled = (predicted - center) * (inverse_sigma / root_count)
    innovation = (values[...] - center) * inverse_sigma
    coeff = jnp.sum(scaled * innovation, axis=0, keepdims=True) / root_count
    first = coeff.astype(jnp.bfloat16).astype(jnp.float32)
    second = (coeff - first).astype(jnp.bfloat16).astype(jnp.float32)
    third = coeff - first - second
    index = lax.broadcasted_iota(jnp.int32, (PAY_ROWS, members), 0)
    tail = jnp.where(index == 0, first, jnp.where(index == 1, second, jnp.where(index == 2, third, 0.0)))
    pay_out[0:observed, :] = scaled.astype(jnp.bfloat16)
    pay_out[observed : observed + PAY_ROWS, :] = tail.astype(jnp.bfloat16)


def saturate_kernel(
    start, packed, weights, swap_out, mask, read_half, anomaly_out, mean_out, sat_rows
):
    rows, span, members = anomaly_out.shape
    count = packed.shape[1]
    channels = read_half.shape[0]
    ones = ones_rows(members)
    lane_index = lax.broadcasted_iota(jnp.int32, mask.shape, 1)

    def some_rows(step, carry):
        found = []
        for k in range(8):
            y = start + step * 8 + k
            taps = jnp.concatenate(
                [packed[pl.ds(y, 3)].reshape(3 * count, members), ones], axis=0
            )
            half = jnp.dot(weights[...], taps, preferred_element_type=jnp.float32)
            total = jnp.zeros((rows, members), jnp.float32)
            for c in range(channels):
                part = half[rows * c : rows * c + rows]
                total = total + read_half[c] * (part * (1.0 + jnp.tanh(part)))
            here = jnp.sum(jnp.where(lane_index == y, mask[...], 0.0), axis=1, keepdims=True)
            found.append(here * (0.5 + 0.5 * jnp.tanh(total)))
        at = pl.multiple_of(step * 8 * rows, 8 * rows)
        sat_rows[pl.ds(at, 8 * rows), :] = jnp.concatenate(found, axis=0).astype(jnp.bfloat16)
        return carry

    lax.fori_loop(0, span // 8, some_rows, 0)
    moved = jnp.dot(swap_out[...], sat_rows[...], preferred_element_type=jnp.float32)
    mean = jnp.mean(moved, axis=1, keepdims=True)
    anomaly_out[...] = (moved - mean).astype(jnp.bfloat16).reshape(rows, span, members)
    mean_out[...] = mean.reshape(rows, span, 1)


def moments_kernel(fields, anomaly_out, mean_out):
    def step(n, carry):
        state = fields[pl.ds(2 * n, 2)].astype(jnp.float32)
        mean = jnp.mean(state, axis=2, keepdims=True)
        anomaly_out[pl.ds(2 * n, 2)] = (state - mean).astype(jnp.bfloat16)
        mean_out[pl.ds(2 * n, 2)] = mean
        return carry

    lax.fori_loop(0, fields.shape[0] // 2, step, 0)


def transposed_dot(a, b, precision):
    return lax.dot_general(
        a, b, (((0,), (0,)), ((), ())), preferred_element_type=jnp.float32, precision=precision
    )


def spread_row(part, p):
    return jnp.broadcast_to(part[p : p + 1, :], part.shape)


def spread_lane(part, q):
    return jnp.broadcast_to(part[:, q : q + 1], part.shape)


def inverse_root(value):
    guess = lax.rsqrt(value)
    return guess * (1.5 - (0.5 * value) * (guess * guess))


def inverse_factor_block(block):
    lane = lax.broadcasted_iota(jnp.int32, (8, 2 * BLOCK), 1)
    sub = lax.broadcasted_iota(jnp.int32, (8, 2 * BLOCK), 0)
    groups = BLOCK // 8
    parts = []
    for i in range(groups):
        unit = jnp.where(lane == sub + (BLOCK + 8 * i), 1.0, 0.0)
        known = jnp.concatenate(
            [block[8 * i : 8 * i + 8, :], jnp.zeros((8, BLOCK), jnp.float32)], axis=1
        )
        parts.append(known + unit)
    done = []
    for j in range(groups):
        corner = [spread_lane(parts[j], 8 * j + q) for q in range(8)]
        entry = {(p, q): spread_row(corner[q], p) for q in range(8) for p in range(q, 8)}
        line = [spread_row(parts[j], p) for p in range(8)]
        near = j + 1 < groups
        if near:
            beside = [spread_lane(parts[j + 1], 8 * j + q) for q in range(8)]
        factor, scale = {}, []
        for q in range(8):
            root = inverse_root(entry[q, q])
            scale.append(root)
            line[q] = line[q] * root
            for p in range(q + 1, 8):
                factor[p, q] = entry[p, q] * root
            for t in range(q + 1, 8):
                for p in range(t, 8):
                    entry[p, t] = entry[p, t] - factor[p, q] * factor[t, q]
            for p in range(q + 1, 8):
                line[p] = line[p] - factor[p, q] * line[q]
            if near:
                lead = beside[q] * root
                for t in range(q + 1, 8):
                    beside[t] = beside[t] - lead * factor[t, q]
                parts[j + 1] = parts[j + 1] - lead * line[q]
        if j + 2 < groups:
            weighted = [None] * 8
            for q in range(7, -1, -1):
                rest = line[q]
                for p in range(q + 1, 8):
                    rest = rest - factor[p, q] * weighted[p]
                weighted[q] = rest * scale[q]
            for i in range(j + 2, groups):
                change = spread_lane(parts[i], 8 * j) * weighted[0]
                for q in range(1, 8):
                    change = change + spread_lane(parts[i], 8 * j + q) * weighted[q]
                parts[i] = parts[i] - change
        merged = line[0]
        for q in range(1, 8):
            merged = jnp.where(sub == q, line[q], merged)
        done.append(merged[:, BLOCK:])
    return jnp.concatenate(done, axis=0)


def update_kernel(gathered, *refs):
    if gathered:
        pay, refs = refs[0], refs[1:]
    else:
        gram, coeff_in, refs = refs[0], refs[1], refs[2:]
    moments, (out, joint, mixing) = refs[:-3], refs[-3:]
    members = out.shape[2]
    sub = lax.broadcasted_iota(jnp.int32, (members, members), 0)
    lane = lax.broadcasted_iota(jnp.int32, (members, members), 1)
    identity = jnp.where(sub == lane, 1.0, 0.0)
    if gathered:
        devices, observed = pay.shape[0], pay.shape[1] - PAY_ROWS
        group = max(1, 256 // observed)
        total = identity
        for d in range(0, devices, group):
            block = pay[d : d + group, 0:observed, :].reshape(-1, members)
            total = total + transposed_dot(block, block, None)
        coeff = jnp.zeros((PAY_ROWS, members), jnp.float32)
        for d in range(devices):
            coeff = coeff + pay[d, observed:, :].astype(jnp.float32)
        coeff = jnp.sum(coeff, axis=0, keepdims=True)
    else:
        total = identity + gram[...]
        coeff = coeff_in[...]
    joint[:, 0:members] = total
    joint[:, members:] = identity
    for k in range(members // BLOCK):
        at = k * BLOCK
        inverse = inverse_factor_block(joint[at : at + BLOCK, at : at + BLOCK])
        rows = jnp.dot(
            inverse, joint[at : at + BLOCK, :], precision=HIGHEST, preferred_element_type=jnp.float32
        )
        joint[at : at + BLOCK, :] = rows
        if at + BLOCK < members:
            joint[at + BLOCK :, :] = joint[at + BLOCK :, :] - transposed_dot(
                rows[:, at + BLOCK : members], rows, HIGHEST
            )
    inverse = joint[:, members:]
    wide = jnp.broadcast_to(coeff, (8, members))
    half = lax.dot_general(
        wide, inverse, (((1,), (1,)), ((), ())), preferred_element_type=jnp.float32, precision=HIGHEST
    )
    weight = jnp.dot(half, inverse, preferred_element_type=jnp.float32, precision=HIGHEST)
    mixing[...] = jnp.transpose(inverse + weight[0:1, :]).astype(jnp.bfloat16)

    def blend(anomalies, mean):
        outer, inner = anomalies.shape[0], anomalies.shape[1]
        moved = jnp.dot(
            anomalies.reshape(outer * inner, members), mixing[...], preferred_element_type=jnp.float32
        )
        return (mean + moved.reshape(outer, inner, members)).astype(jnp.bfloat16)

    anomalies, mean = moments[:2]
    field_rows = anomalies.shape[0]

    def step(n, carry):
        for k in range(2):
            at = 4 * n + 2 * k
            out[pl.ds(at, 2)] = blend(anomalies[pl.ds(at, 2)], mean[pl.ds(at, 2)])
        return carry

    lax.fori_loop(0, field_rows // 4, step, 0)
    for n in range(1, len(moments) // 2):
        anomalies, mean = moments[2 * n : 2 * n + 2]
        span = anomalies.shape[1]
        out[field_rows:, (n - 1) * span : n * span, :] = blend(anomalies[...], mean[...])


def shift(value, axis, by, closed):
    count = lax.axis_size(axis)
    if by > 0:
        pairs = [(i, (i + 1) % count) for i in range(count if closed else count - 1)]
    else:
        pairs = [((i + 1) % count, i) for i in range(count if closed else count - 1)]
    return lax.ppermute(value, axis, pairs)


def shift_both(value, core_by, face_by):
    core_count, face_count = lax.axis_size("cores"), lax.axis_size("face")
    pairs = [
        (i * face_count + j, ((i + core_by) % core_count) * face_count + j + face_by)
        for i in range(core_count)
        for j in range(face_count)
        if 0 <= j + face_by < face_count
    ]
    return lax.ppermute(value, ("cores", "face"), pairs)


def gather_rows(block, steps, packed, saturate):
    pieces = []
    for n, (axis, bit) in enumerate(steps):
        count = lax.axis_size(axis)
        if n < PIECES:
            block, packed = lax.optimization_barrier((block, packed))
        other = lax.ppermute(block, axis, [(i, i ^ bit) for i in range(count)])
        if n < PIECES:
            piece = saturate(n, packed)
        block = jnp.concatenate([block, other], axis=0)
        if n < PIECES:
            block, piece = lax.optimization_barrier((block, piece))
            pieces.append(piece)
    return block, pieces + [saturate(n, packed) for n in range(len(pieces), PIECES)]


def bits_of(axis, count):
    bits = []
    while (1 << len(bits)) < count:
        bits.append((axis, 1 << len(bits)))
    return bits


def vmem():
    return pl.BlockSpec(memory_space=pltpu.VMEM)


def smem():
    return pl.BlockSpec(memory_space=pltpu.SMEM)


def moments_shape(outer, inner, members):
    return (
        jax.ShapeDtypeStruct((outer, inner, members), jnp.bfloat16),
        jax.ShapeDtypeStruct((outer, inner, 1), jnp.float32),
    )


def shards(
    fields, pore_mask, conv_kernel, conv_bias, read_weight, obs_cells, obs_values, obs_sigma
):
    _, planes, columns, lanes, members = fields.shape
    channels = conv_kernel.shape[1]
    rows = planes * columns
    observed = obs_cells.shape[0]

    low = shift(fields[:, -1:], "cores", 1, True)
    high = shift(fields[:, :1], "cores", -1, True)
    low_left = shift_both(fields[:, -1:, -1:], 1, 1)
    high_left = shift_both(fields[:, :1, -1:], -1, 1)
    low_right = shift_both(fields[:, -1:, :1], 1, -1)
    high_right = shift_both(fields[:, :1, :1], -1, -1)
    left = shift(fields[:, :, -1:], "face", 1, False)
    right = shift(fields[:, :, :1], "face", -1, False)

    selector = tap_selector(planes, columns)
    count = selector.shape[2] // 3
    taps = jnp.dot(
        jnp.transpose(conv_kernel),
        jnp.asarray(selector.reshape(54, -1), jnp.bfloat16),
        preferred_element_type=jnp.float32,
    ).reshape(channels, rows, 3 * count)
    bias = jnp.stack(three_pieces(0.5 * conv_bias), axis=1)
    bias = jnp.broadcast_to(bias[:, None, :], (channels, rows, 3))
    weights = jnp.concatenate(
        [0.5 * taps, bias, jnp.zeros((channels, rows, 13), jnp.float32)], axis=2
    ).astype(jnp.bfloat16)
    by_row = jnp.transpose(weights, (1, 0, 2))
    weights = weights.reshape(channels * rows, 3 * count + 16)
    flat = lambda a: a.reshape(-1, lanes, members)
    span = lanes // PIECES
    mask = pore_mask.reshape(rows, lanes)
    mask_float = mask.astype(jnp.float32)
    read_half = 0.5 * read_weight
    swap_in = jnp.asarray(swap_matrix(16, 16), jnp.bfloat16)
    swap_out = jnp.asarray(swap_matrix(span, rows), jnp.bfloat16)
    params = pltpu.CompilerParams(vmem_limit_bytes=VMEM_BYTES)
    packed, pay = pl.pallas_call(
        observe_kernel,
        out_shape=(
            jax.ShapeDtypeStruct((lanes + 2, count, members), jnp.bfloat16),
            jax.ShapeDtypeStruct((observed + PAY_ROWS, members), jnp.bfloat16),
        ),
        in_specs=[vmem()] * 14 + [smem()] * 2,
        out_specs=(vmem(), vmem()),
        scratch_shapes=[pltpu.VMEM((observed, members), jnp.float32)],
        compiler_params=params,
        name="observe",
    )(
        flat(fields), flat(low), flat(high), flat(left), flat(right), flat(low_left),
        flat(high_left), flat(low_right), flat(high_right), by_row, swap_in, read_half[:, None],
        obs_sigma[:, None], obs_values[:, None], obs_cells, mask,
    )

    def saturate(n, packed):
        return pl.pallas_call(
            functools.partial(saturate_kernel, n * span),
            out_shape=moments_shape(rows, span, members),
            in_specs=[vmem()] * 4 + [smem()],
            out_specs=(vmem(), vmem()),
            scratch_shapes=[pltpu.VMEM((rows * span, members), jnp.bfloat16)],
            compiler_params=params,
            cost_estimate=pl.CostEstimate(
                flops=2 * 256 * 256 * span * members,
                bytes_accessed=4 * 1024 * 1024,
                transcendentals=channels * rows * span * members,
            ),
            name="saturate",
        )(packed, weights, swap_out, mask_float, read_half)

    field_moments = pl.pallas_call(
        moments_kernel,
        out_shape=moments_shape(2 * rows, lanes, members),
        in_specs=[vmem()],
        out_specs=(vmem(), vmem()),
        compiler_params=params,
        name="moments",
    )(flat(fields))
    core_count, face_count = lax.axis_size("cores"), lax.axis_size("face")
    devices = core_count * face_count
    gathered = devices <= GATHER_DEVICES and devices & (devices - 1) == 0
    if gathered:
        steps = bits_of("face", face_count)[::-1] + bits_of("cores", core_count)[1:]
        steps = steps + bits_of("cores", core_count)[:1]
        block, pieces = gather_rows(pay[None], steps, packed, saturate)
        terms = (block,)
    else:
        part = pay[:observed]
        gram = lax.dot_general(
            part, part, (((0,), (0,)), ((), ())), preferred_element_type=jnp.float32
        )
        coeff = jnp.sum(pay[observed:].astype(jnp.float32), axis=0, keepdims=True)
        terms = lax.psum((gram, coeff), ("cores", "face"))
        pieces = [saturate(n, packed) for n in range(PIECES)]
    out = pl.pallas_call(
        functools.partial(update_kernel, gathered),
        out_shape=jax.ShapeDtypeStruct((3 * rows, lanes, members), jnp.bfloat16),
        in_specs=[vmem()] * (len(terms) + 2 + 2 * PIECES),
        out_specs=vmem(),
        scratch_shapes=[
            pltpu.VMEM((members, 2 * members), jnp.float32),
            pltpu.VMEM((members, members), jnp.bfloat16),
        ],
        compiler_params=params,
        name="update",
    )(*terms, *field_moments, *(part for piece in pieces for part in piece))
    return out.reshape(3, planes, columns, lanes, members)


def solution(mesh):
    return jax.shard_map(
        shards,
        mesh=mesh,
        in_specs=(
            P(None, "cores", "face", None, None),
            P("cores", "face", None),
            P(),
            P(),
            P(),
            P(("cores", "face")),
            P(("cores", "face")),
            P(("cores", "face")),
        ),
        out_specs=P(None, "cores", "face", None, None),
        check_vma=False,
    )
```

```python
import functools
import math

import jax
import jax.numpy as jnp
import numpy as np
from jax import lax
from jax.experimental import pallas as pl
from jax.experimental.pallas import tpu as pltpu
from jax.sharding import PartitionSpec as P

HIGHEST = lax.Precision.HIGHEST
PAY_ROWS = 16
GATHER_DEVICES = 64
BLOCK = 64
SPANS = (16, 32, 32, 48)
VMEM_BYTES = 32 * 1024 * 1024


def plane_places(planes, columns):
    own = [(f, z + 1, x + 1) for f in range(2) for z in range(planes) for x in range(columns)]
    low = [(f, 0, x + 1) for f in range(2) for x in range(columns)]
    high = [(f, planes + 1, x + 1) for f in range(2) for x in range(columns)]
    left = [(f, z + 1, 0) for f in range(2) for z in range(planes)]
    right = [(f, z + 1, columns + 1) for f in range(2) for z in range(planes)]
    corners = [
        (f, z, x) for z in (0, planes + 1) for x in (0, columns + 1) for f in range(2)
    ]
    return own + low + high + left + right + corners


def tap_selector(planes, columns):
    places = plane_places(planes, columns)
    chosen = np.zeros((54, planes * columns, 3 * len(places)), np.float32)
    for z in range(planes):
        for x in range(columns):
            for n, (f, zz, xx) in enumerate(places):
                a, b = zz - z, xx - x
                if 0 <= a <= 2 and 0 <= b <= 2:
                    for c in range(3):
                        chosen[27 * f + 9 * a + 3 * b + c, z * columns + x, c * len(places) + n] = 1.0
    return chosen


def swap_matrix(outer, inner):
    matrix = np.zeros((outer * inner, outer * inner), np.float32)
    for i in range(outer):
        for j in range(inner):
            matrix[j * outer + i, i * inner + j] = 1.0
    return matrix


def three_pieces(value):
    first = lax.reduce_precision(value, 8, 7)
    second = lax.reduce_precision(value - first, 8, 7)
    third = lax.reduce_precision(value - first - second, 8, 7)
    return first, second, third


def ones_rows(members):
    row_index = lax.broadcasted_iota(jnp.int32, (16, members), 0)
    return jnp.where(row_index < 3, 1.0, 0.0).astype(jnp.bfloat16)


def ordered(odd, far, near):
    return jnp.where(odd == 0, far, near), jnp.where(odd == 0, near, far)


def observe_kernel(
    own, far, near, left, right, far_left, far_right, near_corner, by_row, swap_in, read_column,
    sigma, values, cells, mask, odd, packed, pay_out, pred
):
    lanes, members = own.shape[1], own.shape[2]
    count = packed.shape[1]
    observed = cells.shape[0]
    packed[0] = jnp.zeros((count, members), jnp.bfloat16)
    packed[lanes + 1] = jnp.zeros((count, members), jnp.bfloat16)

    for step in range(lanes // 16):
        at = step * 16
        part = lambda ref: ref[:, pl.ds(at, 16), :]
        far_block, near_block = part(far), part(near)
        far_sides = jnp.concatenate([part(far_left), part(far_right)], axis=0)
        near_sides = part(near_corner)
        blocks = (
            part(own),
            jnp.concatenate(ordered(odd[0], far_block, near_block), axis=0),
            jnp.concatenate(
                [part(left), part(right), *ordered(odd[0], far_sides, near_sides)], axis=0
            ),
        )
        for g, block in enumerate(blocks):
            moved = jnp.dot(
                swap_in[...], block.reshape(256, members), preferred_element_type=jnp.float32
            )
            packed[pl.ds(at + 1, 16), 16 * g : 16 * g + 16, :] = (
                moved.astype(jnp.bfloat16).reshape(16, 16, members)
            )

    ones = ones_rows(members)
    read = jnp.broadcast_to(read_column[...], (read_column.shape[0], members))

    def some_cells(step, carry):
        for k in range(16):
            o = step * 16 + k
            cell = cells[o]
            row, y = cell // lanes, cell % lanes
            taps = jnp.concatenate(
                [packed[pl.ds(y, 3)].reshape(3 * count, members), ones], axis=0
            )
            half = jnp.dot(by_row[row], taps, preferred_element_type=jnp.float32)
            total = jnp.sum(read * (half * (1.0 + jnp.tanh(half))), axis=0, keepdims=True)
            found = (0.5 + 0.5 * jnp.tanh(total)) * mask[row, y].astype(jnp.float32)
            pred[pl.ds(o, 1), :] = found.astype(jnp.bfloat16).astype(jnp.float32)
        return carry

    lax.fori_loop(0, observed // 16, some_cells, 0)

    root_count = math.sqrt(members - 1)
    predicted = pred[...]
    center = jnp.mean(predicted, axis=1, keepdims=True)
    inverse_sigma = 1.0 / sigma[...]
    scaled = (predicted - center) * (inverse_sigma / root_count)
    innovation = (values[...] - center) * inverse_sigma
    coeff = jnp.sum(scaled * innovation, axis=0, keepdims=True) / root_count
    first = coeff.astype(jnp.bfloat16).astype(jnp.float32)
    second = (coeff - first).astype(jnp.bfloat16).astype(jnp.float32)
    third = coeff - first - second
    index = lax.broadcasted_iota(jnp.int32, (PAY_ROWS, members), 0)
    tail = jnp.where(index == 0, first, jnp.where(index == 1, second, jnp.where(index == 2, third, 0.0)))
    pay_out[0:observed, :] = scaled.astype(jnp.bfloat16)
    pay_out[observed : observed + PAY_ROWS, :] = tail.astype(jnp.bfloat16)


def saturate_kernel(
    start, packed, weights, swap_out, mask, read_half, anomaly_out, mean_out, sat_rows
):
    rows, span, members = anomaly_out.shape
    count = packed.shape[1]
    channels = read_half.shape[0]
    ones = ones_rows(members)
    lane_index = lax.broadcasted_iota(jnp.int32, mask.shape, 1)

    def some_rows(step, carry):
        found = []
        for k in range(8):
            y = start + step * 8 + k
            taps = jnp.concatenate(
                [packed[pl.ds(y, 3)].reshape(3 * count, members), ones], axis=0
            )
            half = jnp.dot(weights[...], taps, preferred_element_type=jnp.float32)
            total = jnp.zeros((rows, members), jnp.float32)
            for c in range(channels):
                part = half[rows * c : rows * c + rows]
                total = total + read_half[c] * (part * (1.0 + jnp.tanh(part)))
            here = jnp.sum(jnp.where(lane_index == y, mask[...], 0.0), axis=1, keepdims=True)
            found.append(here * (0.5 + 0.5 * jnp.tanh(total)))
        at = pl.multiple_of(step * 8 * rows, 8 * rows)
        sat_rows[pl.ds(at, 8 * rows), :] = jnp.concatenate(found, axis=0).astype(jnp.bfloat16)
        return carry

    lax.fori_loop(0, span // 8, some_rows, 0)
    for n in range(span // 16):
        block = sat_rows[n * 16 * rows : (n + 1) * 16 * rows, :]
        moved = jnp.dot(swap_out[...], block, preferred_element_type=jnp.float32)
        mean = jnp.mean(moved, axis=1, keepdims=True)
        anomalies = (moved - mean).astype(jnp.bfloat16)
        anomaly_out[:, n * 16 : n * 16 + 16, :] = anomalies.reshape(rows, 16, members)
        mean_out[:, n * 16 : n * 16 + 16, :] = mean.reshape(rows, 16, 1)


def moments_kernel(fields, anomaly_out, mean_out):
    def step(n, carry):
        state = fields[pl.ds(2 * n, 2)].astype(jnp.float32)
        mean = jnp.mean(state, axis=2, keepdims=True)
        anomaly_out[pl.ds(2 * n, 2)] = (state - mean).astype(jnp.bfloat16)
        mean_out[pl.ds(2 * n, 2)] = mean
        return carry

    lax.fori_loop(0, fields.shape[0] // 2, step, 0)


def transposed_dot(a, b, precision):
    return lax.dot_general(
        a, b, (((0,), (0,)), ((), ())), preferred_element_type=jnp.float32, precision=precision
    )


def spread_row(part, p):
    return jnp.broadcast_to(part[p : p + 1, :], part.shape)


def spread_lane(part, q):
    return jnp.broadcast_to(part[:, q : q + 1], part.shape)


def inverse_factor_block(block):
    lane = lax.broadcasted_iota(jnp.int32, (8, 2 * BLOCK), 1)
    sub = lax.broadcasted_iota(jnp.int32, (8, 2 * BLOCK), 0)
    groups = BLOCK // 8
    parts = []
    for i in range(groups):
        unit = jnp.where(lane == sub + (BLOCK + 8 * i), 1.0, 0.0)
        known = jnp.concatenate(
            [block[8 * i : 8 * i + 8, :], jnp.zeros((8, BLOCK), jnp.float32)], axis=1
        )
        parts.append(known + unit)
    done = []
    for j in range(groups):
        corner = [spread_lane(parts[j], 8 * j + q) for q in range(8)]
        entry = {(p, q): spread_row(corner[q], p) for q in range(8) for p in range(q, 8)}
        line = [spread_row(parts[j], p) for p in range(8)]
        near = j + 1 < groups
        if near:
            beside = [spread_lane(parts[j + 1], 8 * j + q) for q in range(8)]
        factor, scale = {}, []
        for q in range(8):
            root = lax.rsqrt(entry[q, q])
            scale.append(root)
            line[q] = line[q] * root
            for p in range(q + 1, 8):
                factor[p, q] = entry[p, q] * root
            for t in range(q + 1, 8):
                for p in range(t, 8):
                    entry[p, t] = entry[p, t] - factor[p, q] * factor[t, q]
            for p in range(q + 1, 8):
                line[p] = line[p] - factor[p, q] * line[q]
            if near:
                lead = beside[q] * root
                for t in range(q + 1, 8):
                    beside[t] = beside[t] - lead * factor[t, q]
                parts[j + 1] = parts[j + 1] - lead * line[q]
        if j + 2 < groups:
            weighted = [None] * 8
            for q in range(7, -1, -1):
                rest = line[q]
                for p in range(q + 1, 8):
                    rest = rest - factor[p, q] * weighted[p]
                weighted[q] = rest * scale[q]
            for i in range(j + 2, groups):
                change = spread_lane(parts[i], 8 * j) * weighted[0]
                for q in range(1, 8):
                    change = change + spread_lane(parts[i], 8 * j + q) * weighted[q]
                parts[i] = parts[i] - change
        merged = line[0]
        for q in range(1, 8):
            merged = jnp.where(sub == q, line[q], merged)
        done.append(merged[:, BLOCK:])
    return jnp.concatenate(done, axis=0)


def update_kernel(gathered, *refs):
    if gathered:
        pay, refs = refs[0], refs[1:]
    else:
        gram, coeff_in, refs = refs[0], refs[1], refs[2:]
    moments, (out, joint, mixing) = refs[:-3], refs[-3:]
    members = out.shape[2]
    sub = lax.broadcasted_iota(jnp.int32, (members, members), 0)
    lane = lax.broadcasted_iota(jnp.int32, (members, members), 1)
    identity = jnp.where(sub == lane, 1.0, 0.0)
    if gathered:
        devices, observed = pay.shape[0], pay.shape[1] - PAY_ROWS
        group = max(1, 256 // observed)
        total = identity
        for d in range(0, devices, group):
            block = pay[d : d + group, 0:observed, :].reshape(-1, members)
            total = total + transposed_dot(block, block, None)
        coeff = jnp.zeros((PAY_ROWS, members), jnp.float32)
        for d in range(devices):
            coeff = coeff + pay[d, observed:, :].astype(jnp.float32)
        coeff = jnp.sum(coeff, axis=0, keepdims=True)
    else:
        total = identity + gram[...]
        coeff = coeff_in[...]
    joint[:, 0:members] = total
    joint[:, members:] = identity
    for k in range(members // BLOCK):
        at = k * BLOCK
        inverse = inverse_factor_block(joint[at : at + BLOCK, at : at + BLOCK])
        rows = jnp.dot(
            inverse, joint[at : at + BLOCK, :], precision=HIGHEST, preferred_element_type=jnp.float32
        )
        joint[at : at + BLOCK, :] = rows
        if at + BLOCK < members:
            joint[at + BLOCK :, :] = joint[at + BLOCK :, :] - transposed_dot(
                rows[:, at + BLOCK : members], rows, HIGHEST
            )
    inverse = joint[:, members:]
    wide = jnp.broadcast_to(coeff, (8, members))
    half = lax.dot_general(
        wide, inverse, (((1,), (1,)), ((), ())), preferred_element_type=jnp.float32, precision=HIGHEST
    )
    weight = jnp.dot(half, inverse, preferred_element_type=jnp.float32, precision=HIGHEST)
    mixing[...] = jnp.transpose(inverse + weight[0:1, :]).astype(jnp.bfloat16)

    def blend(anomalies, mean):
        outer, inner = anomalies.shape[0], anomalies.shape[1]
        moved = jnp.dot(
            anomalies.reshape(outer * inner, members), mixing[...], preferred_element_type=jnp.float32
        )
        return (mean + moved.reshape(outer, inner, members)).astype(jnp.bfloat16)

    anomalies, mean = moments[:2]
    field_rows = anomalies.shape[0]

    def step(n, carry):
        for k in range(2):
            at = 4 * n + 2 * k
            out[pl.ds(at, 2)] = blend(anomalies[pl.ds(at, 2)], mean[pl.ds(at, 2)])
        return carry

    lax.fori_loop(0, field_rows // 4, step, 0)
    at = 0
    for n in range(1, len(moments) // 2):
        anomalies, mean = moments[2 * n : 2 * n + 2]
        span = anomalies.shape[1]
        out[field_rows:, at : at + span, :] = blend(anomalies[...], mean[...])
        at += span


def shift(value, axis, by, closed):
    count = lax.axis_size(axis)
    if by > 0:
        pairs = [(i, (i + 1) % count) for i in range(count if closed else count - 1)]
    else:
        pairs = [((i + 1) % count, i) for i in range(count if closed else count - 1)]
    return lax.ppermute(value, axis, pairs)


def swap_cores(value, inside):
    count = lax.axis_size("cores")
    pairs = []
    for i in range(count):
        step = 1 if (i % 2 == 0) == inside else -1
        pairs.append((i, (i + step) % count))
    return lax.ppermute(value, "cores", pairs)


def gather_rows(block, steps, packed, saturate):
    pieces = []
    for n, (axis, bit) in enumerate(steps):
        count = lax.axis_size(axis)
        if n < len(SPANS):
            block, packed = lax.optimization_barrier((block, packed))
        other = lax.ppermute(block, axis, [(i, i ^ bit) for i in range(count)])
        if n < len(SPANS):
            piece = saturate(n, packed)
        block = jnp.concatenate([block, other], axis=0)
        if n < len(SPANS):
            block, piece = lax.optimization_barrier((block, piece))
            pieces.append(piece)
    return block, pieces + [saturate(n, packed) for n in range(len(pieces), len(SPANS))]


def bits_of(axis, count):
    bits = []
    while (1 << len(bits)) < count:
        bits.append((axis, 1 << len(bits)))
    return bits


def vmem():
    return pl.BlockSpec(memory_space=pltpu.VMEM)


def smem():
    return pl.BlockSpec(memory_space=pltpu.SMEM)


def moments_shape(outer, inner, members):
    return (
        jax.ShapeDtypeStruct((outer, inner, members), jnp.bfloat16),
        jax.ShapeDtypeStruct((outer, inner, 1), jnp.float32),
    )


def shards(
    fields, pore_mask, conv_kernel, conv_bias, read_weight, obs_cells, obs_values, obs_sigma
):
    _, planes, columns, lanes, members = fields.shape
    channels = conv_kernel.shape[1]
    rows = planes * columns
    observed = obs_cells.shape[0]

    odd = lax.axis_index("cores") % 2
    near_plane = (1 - odd) * (planes - 1)
    far = lax.dynamic_slice_in_dim(fields, odd * (planes - 1), 1, axis=1)
    near = lax.dynamic_slice_in_dim(fields, near_plane, 1, axis=1)
    far, near, tied = lax.optimization_barrier((far, near, fields))
    far = swap_cores(far, False)
    near = swap_cores(near, True)
    left = shift(tied[:, :, -1:], "face", 1, False)
    right = shift(tied[:, :, :1], "face", -1, False)
    far_left = shift(far[:, :, -1:], "face", 1, False)
    far_right = shift(far[:, :, :1], "face", -1, False)
    near_sides = [lax.dynamic_slice_in_dim(side, near_plane, 1, axis=1) for side in (left, right)]
    near_corner = swap_cores(jnp.concatenate(near_sides, axis=0), True)

    selector = tap_selector(planes, columns)
    count = selector.shape[2] // 3
    taps = jnp.dot(
        jnp.transpose(conv_kernel),
        jnp.asarray(selector.reshape(54, -1), jnp.bfloat16),
        preferred_element_type=jnp.float32,
    ).reshape(channels, rows, 3 * count)
    bias = jnp.stack(three_pieces(0.5 * conv_bias), axis=1)
    bias = jnp.broadcast_to(bias[:, None, :], (channels, rows, 3))
    weights = jnp.concatenate(
        [0.5 * taps, bias, jnp.zeros((channels, rows, 13), jnp.float32)], axis=2
    ).astype(jnp.bfloat16)
    by_row = jnp.transpose(weights, (1, 0, 2))
    weights = weights.reshape(channels * rows, 3 * count + 16)
    flat = lambda a: a.reshape(-1, lanes, members)
    starts = [sum(SPANS[:n]) for n in range(len(SPANS))]
    mask = pore_mask.reshape(rows, lanes)
    mask_float = mask.astype(jnp.float32)
    read_half = 0.5 * read_weight
    swap_in = jnp.asarray(swap_matrix(16, 16), jnp.bfloat16)
    swap_out = jnp.asarray(swap_matrix(16, rows), jnp.bfloat16)
    params = pltpu.CompilerParams(vmem_limit_bytes=VMEM_BYTES)
    packed, pay = pl.pallas_call(
        observe_kernel,
        out_shape=(
            jax.ShapeDtypeStruct((lanes + 2, count, members), jnp.bfloat16),
            jax.ShapeDtypeStruct((observed + PAY_ROWS, members), jnp.bfloat16),
        ),
        in_specs=[vmem()] * 13 + [smem()] * 3,
        out_specs=(vmem(), vmem()),
        scratch_shapes=[pltpu.VMEM((observed, members), jnp.float32)],
        compiler_params=params,
        name="observe",
    )(
        flat(fields), flat(far), flat(near), flat(left), flat(right), flat(far_left),
        flat(far_right), flat(near_corner), by_row, swap_in, read_half[:, None],
        obs_sigma[:, None], obs_values[:, None], obs_cells, mask, odd.astype(jnp.int32)[None],
    )

    def saturate(n, packed):
        span = SPANS[n]
        return pl.pallas_call(
            functools.partial(saturate_kernel, starts[n]),
            out_shape=moments_shape(rows, span, members),
            in_specs=[vmem()] * 4 + [smem()],
            out_specs=(vmem(), vmem()),
            scratch_shapes=[pltpu.VMEM((rows * span, members), jnp.bfloat16)],
            compiler_params=params,
            cost_estimate=pl.CostEstimate(
                flops=2 * 256 * 256 * span * members,
                bytes_accessed=4 * 1024 * 1024,
                transcendentals=channels * rows * span * members,
            ),
            name="saturate",
        )(packed, weights, swap_out, mask_float, read_half)

    field_moments = pl.pallas_call(
        moments_kernel,
        out_shape=moments_shape(2 * rows, lanes, members),
        in_specs=[vmem()],
        out_specs=(vmem(), vmem()),
        compiler_params=params,
        name="moments",
    )(flat(fields))
    core_count, face_count = lax.axis_size("cores"), lax.axis_size("face")
    devices = core_count * face_count
    gathered = devices <= GATHER_DEVICES and devices & (devices - 1) == 0
    if gathered:
        steps = bits_of("face", face_count)[::-1] + bits_of("cores", core_count)[1:]
        steps = steps + bits_of("cores", core_count)[:1]
        block, pieces = gather_rows(pay[None], steps, packed, saturate)
        terms = (block,)
    else:
        part = pay[:observed]
        gram = lax.dot_general(
            part, part, (((0,), (0,)), ((), ())), preferred_element_type=jnp.float32
        )
        coeff = jnp.sum(pay[observed:].astype(jnp.float32), axis=0, keepdims=True)
        terms = lax.psum((gram, coeff), ("cores", "face"))
        pieces = [saturate(n, packed) for n in range(len(SPANS))]
    out = pl.pallas_call(
        functools.partial(update_kernel, gathered),
        out_shape=jax.ShapeDtypeStruct((3 * rows, lanes, members), jnp.bfloat16),
        in_specs=[vmem()] * (len(terms) + 2 + 2 * len(SPANS)),
        out_specs=vmem(),
        scratch_shapes=[
            pltpu.VMEM((members, 2 * members), jnp.float32),
            pltpu.VMEM((members, members), jnp.bfloat16),
        ],
        compiler_params=params,
        name="update",
    )(*terms, *field_moments, *(part for piece in pieces for part in piece))
    return out.reshape(3, planes, columns, lanes, members)


def solution(mesh):
    return jax.shard_map(
        shards,
        mesh=mesh,
        in_specs=(
            P(None, "cores", "face", None, None),
            P("cores", "face", None),
            P(),
            P(),
            P(),
            P(("cores", "face")),
            P(("cores", "face")),
            P(("cores", "face")),
        ),
        out_specs=P(None, "cores", "face", None, None),
        check_vma=False,
    )
```

```python
import functools
import math

import jax
import jax.numpy as jnp
import numpy as np
from jax import lax
from jax.experimental import pallas as pl
from jax.experimental.pallas import tpu as pltpu
from jax.sharding import PartitionSpec as P

HIGHEST = lax.Precision.HIGHEST
PAY_ROWS = 16
GATHER_DEVICES = 64
BLOCK = 64
SPANS = (16, 32, 32, 48)
VMEM_BYTES = 32 * 1024 * 1024


def plane_places(planes, columns):
    own = [(f, z + 1, x + 1) for f in range(2) for z in range(planes) for x in range(columns)]
    low = [(f, 0, x + 1) for f in range(2) for x in range(columns)]
    high = [(f, planes + 1, x + 1) for f in range(2) for x in range(columns)]
    left = [(f, z + 1, 0) for f in range(2) for z in range(planes)]
    right = [(f, z + 1, columns + 1) for f in range(2) for z in range(planes)]
    corners = [
        (f, z, x) for z in (0, planes + 1) for x in (0, columns + 1) for f in range(2)
    ]
    return own + low + high + left + right + corners


def tap_selector(planes, columns):
    places = plane_places(planes, columns)
    chosen = np.zeros((54, planes * columns, 3 * len(places)), np.float32)
    for z in range(planes):
        for x in range(columns):
            for n, (f, zz, xx) in enumerate(places):
                a, b = zz - z, xx - x
                if 0 <= a <= 2 and 0 <= b <= 2:
                    for c in range(3):
                        chosen[27 * f + 9 * a + 3 * b + c, z * columns + x, c * len(places) + n] = 1.0
    return chosen


def swap_matrix(outer, inner):
    matrix = np.zeros((outer * inner, outer * inner), np.float32)
    for i in range(outer):
        for j in range(inner):
            matrix[j * outer + i, i * inner + j] = 1.0
    return matrix


def three_pieces(value):
    first = lax.reduce_precision(value, 8, 7)
    second = lax.reduce_precision(value - first, 8, 7)
    third = lax.reduce_precision(value - first - second, 8, 7)
    return first, second, third


def ones_rows(members):
    row_index = lax.broadcasted_iota(jnp.int32, (16, members), 0)
    return jnp.where(row_index < 3, 1.0, 0.0).astype(jnp.bfloat16)


def ordered(odd, far, near):
    return jnp.where(odd == 0, far, near), jnp.where(odd == 0, near, far)


def observe_kernel(
    own, far, near, left, right, far_left, far_right, near_corner, by_row, swap_in, read_column,
    sigma, values, cells, mask, odd, packed, pay_out, pred
):
    lanes, members = own.shape[1], own.shape[2]
    count = packed.shape[1]
    observed = cells.shape[0]
    packed[0] = jnp.zeros((count, members), jnp.bfloat16)
    packed[lanes + 1] = jnp.zeros((count, members), jnp.bfloat16)

    for step in range(lanes // 16):
        at = step * 16
        part = lambda ref: ref[:, pl.ds(at, 16), :]
        far_block, near_block = part(far), part(near)
        far_sides = jnp.concatenate([part(far_left), part(far_right)], axis=0)
        near_sides = part(near_corner)
        blocks = (
            part(own),
            jnp.concatenate(ordered(odd[0], far_block, near_block), axis=0),
            jnp.concatenate(
                [part(left), part(right), *ordered(odd[0], far_sides, near_sides)], axis=0
            ),
        )
        for g, block in enumerate(blocks):
            moved = jnp.dot(
                swap_in[...], block.reshape(256, members), preferred_element_type=jnp.float32
            )
            packed[pl.ds(at + 1, 16), 16 * g : 16 * g + 16, :] = (
                moved.astype(jnp.bfloat16).reshape(16, 16, members)
            )

    ones = ones_rows(members)
    read = jnp.broadcast_to(read_column[...], (read_column.shape[0], members))

    def some_cells(step, carry):
        for k in range(16):
            o = step * 16 + k
            cell = cells[o]
            row, y = cell // lanes, cell % lanes
            taps = jnp.concatenate(
                [packed[pl.ds(y, 3)].reshape(3 * count, members), ones], axis=0
            )
            half = jnp.dot(by_row[row], taps, preferred_element_type=jnp.float32)
            total = jnp.sum(read * (half * (1.0 + jnp.tanh(half))), axis=0, keepdims=True)
            found = (0.5 + 0.5 * jnp.tanh(total)) * mask[row, y].astype(jnp.float32)
            pred[pl.ds(o, 1), :] = found.astype(jnp.bfloat16).astype(jnp.float32)
        return carry

    lax.fori_loop(0, observed // 16, some_cells, 0)

    root_count = math.sqrt(members - 1)
    predicted = pred[...]
    center = jnp.mean(predicted, axis=1, keepdims=True)
    inverse_sigma = 1.0 / sigma[...]
    scaled = (predicted - center) * (inverse_sigma / root_count)
    innovation = (values[...] - center) * inverse_sigma
    coeff = jnp.sum(scaled * innovation, axis=0, keepdims=True) / root_count
    first = coeff.astype(jnp.bfloat16).astype(jnp.float32)
    second = (coeff - first).astype(jnp.bfloat16).astype(jnp.float32)
    third = coeff - first - second
    index = lax.broadcasted_iota(jnp.int32, (PAY_ROWS, members), 0)
    tail = jnp.where(index == 0, first, jnp.where(index == 1, second, jnp.where(index == 2, third, 0.0)))
    pay_out[0:observed, :] = scaled.astype(jnp.bfloat16)
    pay_out[observed : observed + PAY_ROWS, :] = tail.astype(jnp.bfloat16)


def saturate_kernel(
    start, packed, weights, swap_out, mask, read_half, anomaly_out, mean_out, sat_rows
):
    rows, span, members = anomaly_out.shape
    count = packed.shape[1]
    channels = read_half.shape[0]
    ones = ones_rows(members)
    lane_index = lax.broadcasted_iota(jnp.int32, mask.shape, 1)

    def some_rows(step, carry):
        found = []
        for k in range(8):
            y = start + step * 8 + k
            taps = jnp.concatenate(
                [packed[pl.ds(y, 3)].reshape(3 * count, members), ones], axis=0
            )
            half = jnp.dot(weights[...], taps, preferred_element_type=jnp.float32)
            total = jnp.zeros((rows, members), jnp.float32)
            for c in range(channels):
                part = half[rows * c : rows * c + rows]
                total = total + read_half[c] * (part * (1.0 + jnp.tanh(part)))
            here = jnp.sum(jnp.where(lane_index == y, mask[...], 0.0), axis=1, keepdims=True)
            found.append(here * (0.5 + 0.5 * jnp.tanh(total)))
        at = pl.multiple_of(step * 8 * rows, 8 * rows)
        sat_rows[pl.ds(at, 8 * rows), :] = jnp.concatenate(found, axis=0).astype(jnp.bfloat16)
        return carry

    lax.fori_loop(0, span // 8, some_rows, 0)
    for n in range(span // 16):
        block = sat_rows[n * 16 * rows : (n + 1) * 16 * rows, :]
        moved = jnp.dot(swap_out[...], block, preferred_element_type=jnp.float32)
        mean = jnp.mean(moved, axis=1, keepdims=True)
        anomalies = (moved - mean).astype(jnp.bfloat16)
        anomaly_out[:, n * 16 : n * 16 + 16, :] = anomalies.reshape(rows, 16, members)
        mean_out[:, n * 16 : n * 16 + 16, :] = mean.reshape(rows, 16, 1)


def moments_kernel(fields, anomaly_out, mean_out):
    def step(n, carry):
        state = fields[pl.ds(2 * n, 2)].astype(jnp.float32)
        mean = jnp.mean(state, axis=2, keepdims=True)
        anomaly_out[pl.ds(2 * n, 2)] = (state - mean).astype(jnp.bfloat16)
        mean_out[pl.ds(2 * n, 2)] = mean
        return carry

    lax.fori_loop(0, fields.shape[0] // 2, step, 0)


def transposed_dot(a, b, precision):
    return lax.dot_general(
        a, b, (((0,), (0,)), ((), ())), preferred_element_type=jnp.float32, precision=precision
    )


def spread_row(part, p):
    return jnp.broadcast_to(part[p : p + 1, :], part.shape)


def spread_lane(part, q):
    return jnp.broadcast_to(part[:, q : q + 1], part.shape)


def inverse_factor_block(block):
    lane = lax.broadcasted_iota(jnp.int32, (8, 2 * BLOCK), 1)
    sub = lax.broadcasted_iota(jnp.int32, (8, 2 * BLOCK), 0)
    groups = BLOCK // 8
    parts = []
    for i in range(groups):
        unit = jnp.where(lane == sub + (BLOCK + 8 * i), 1.0, 0.0)
        known = jnp.concatenate(
            [block[8 * i : 8 * i + 8, :], jnp.zeros((8, BLOCK), jnp.float32)], axis=1
        )
        parts.append(known + unit)
    done = []
    for j in range(groups):
        corner = [spread_lane(parts[j], 8 * j + q) for q in range(8)]
        entry = {(p, q): spread_row(corner[q], p) for q in range(8) for p in range(q, 8)}
        line = [spread_row(parts[j], p) for p in range(8)]
        near = j + 1 < groups
        if near:
            beside = [spread_lane(parts[j + 1], 8 * j + q) for q in range(8)]
        factor, scale = {}, []
        for q in range(8):
            root = lax.rsqrt(entry[q, q])
            scale.append(root)
            line[q] = line[q] * root
            for p in range(q + 1, 8):
                factor[p, q] = entry[p, q] * root
            for t in range(q + 1, 8):
                for p in range(t, 8):
                    entry[p, t] = entry[p, t] - factor[p, q] * factor[t, q]
            for p in range(q + 1, 8):
                line[p] = line[p] - factor[p, q] * line[q]
            if near:
                lead = beside[q] * root
                for t in range(q + 1, 8):
                    beside[t] = beside[t] - lead * factor[t, q]
                parts[j + 1] = parts[j + 1] - lead * line[q]
        if j + 2 < groups:
            weighted = [None] * 8
            for q in range(7, -1, -1):
                rest = line[q]
                for p in range(q + 1, 8):
                    rest = rest - factor[p, q] * weighted[p]
                weighted[q] = rest * scale[q]
            for i in range(j + 2, groups):
                change = spread_lane(parts[i], 8 * j) * weighted[0]
                for q in range(1, 8):
                    change = change + spread_lane(parts[i], 8 * j + q) * weighted[q]
                parts[i] = parts[i] - change
        merged = line[0]
        for q in range(1, 8):
            merged = jnp.where(sub == q, line[q], merged)
        done.append(merged[:, BLOCK:])
    return jnp.concatenate(done, axis=0)


def update_kernel(gathered, *refs):
    if gathered:
        pay, refs = refs[0], refs[1:]
    else:
        gram, coeff_in, refs = refs[0], refs[1], refs[2:]
    moments, (out, joint, mixing) = refs[:-3], refs[-3:]
    members = out.shape[2]
    sub = lax.broadcasted_iota(jnp.int32, (members, members), 0)
    lane = lax.broadcasted_iota(jnp.int32, (members, members), 1)
    identity = jnp.where(sub == lane, 1.0, 0.0)
    if gathered:
        devices, observed = pay.shape[0], pay.shape[1] - PAY_ROWS
        group = max(1, 256 // observed)
        total = identity
        for d in range(0, devices, group):
            block = pay[d : d + group, 0:observed, :].reshape(-1, members)
            total = total + transposed_dot(block, block, None)
        coeff = jnp.zeros((PAY_ROWS, members), jnp.float32)
        for d in range(devices):
            coeff = coeff + pay[d, observed:, :].astype(jnp.float32)
        coeff = jnp.sum(coeff, axis=0, keepdims=True)
    else:
        total = identity + gram[...]
        coeff = coeff_in[...]
    joint[...] = total
    for k in range(members // BLOCK):
        at = k * BLOCK
        below = at + BLOCK
        wide_sub, wide_lane = sub[0:BLOCK, :], lane[0:BLOCK, :]
        inside = jnp.logical_and(wide_lane >= at, wide_lane < below)
        row = joint[at:below, :]
        inverse = inverse_factor_block(row[:, at:below])
        unit = jnp.where(wide_lane == wide_sub + at, 1.0, 0.0)
        row = jnp.dot(
            inverse,
            jnp.where(inside, unit, row),
            precision=HIGHEST,
            preferred_element_type=jnp.float32,
        )
        joint[at:below, :] = row
        if below < members:
            ahead = jnp.where(wide_lane >= below, row, 0.0)
            change = transposed_dot(ahead, row, HIGHEST)
            rest_lane = lane[below:, :]
            inside = jnp.logical_and(rest_lane >= at, rest_lane < below)
            joint[below:, :] = jnp.where(inside, 0.0, joint[below:, :]) - change[below:, :]
    inverse = jnp.where(lane <= sub, joint[...], 0.0)
    half = jnp.sum(inverse * coeff, axis=1, keepdims=True)
    weight = jnp.sum(inverse * half, axis=0, keepdims=True)
    mixing[...] = jnp.transpose((inverse + weight).astype(jnp.bfloat16))

    def blend(anomalies, mean):
        outer, inner = anomalies.shape[0], anomalies.shape[1]
        moved = jnp.dot(
            anomalies.reshape(outer * inner, members), mixing[...], preferred_element_type=jnp.float32
        )
        return (mean + moved.reshape(outer, inner, members)).astype(jnp.bfloat16)

    anomalies, mean = moments[:2]
    field_rows = anomalies.shape[0]

    def step(n, carry):
        for k in range(2):
            at = 4 * n + 2 * k
            out[pl.ds(at, 2)] = blend(anomalies[pl.ds(at, 2)], mean[pl.ds(at, 2)])
        return carry

    lax.fori_loop(0, field_rows // 4, step, 0)
    at = 0
    for n in range(1, len(moments) // 2):
        anomalies, mean = moments[2 * n : 2 * n + 2]
        span = anomalies.shape[1]
        out[field_rows:, at : at + span, :] = blend(anomalies[...], mean[...])
        at += span


def shift(value, axis, by, closed):
    count = lax.axis_size(axis)
    if by > 0:
        pairs = [(i, (i + 1) % count) for i in range(count if closed else count - 1)]
    else:
        pairs = [((i + 1) % count, i) for i in range(count if closed else count - 1)]
    return lax.ppermute(value, axis, pairs)


def core_pairs(inside):
    count = lax.axis_size("cores")
    steps = [1 if (i % 2 == 0) == inside else -1 for i in range(count)]
    return [(i, (i + step) % count) for i, step in enumerate(steps)]


def swap_cores(value, inside):
    return lax.ppermute(value, "cores", core_pairs(inside))


def swap_far_corner(value, face_by):
    face_count = lax.axis_size("face")
    pairs = [
        (i * face_count + j, other * face_count + j + face_by)
        for i, other in core_pairs(False)
        for j in range(face_count)
        if 0 <= j + face_by < face_count
    ]
    return lax.ppermute(value, ("cores", "face"), pairs)


def gather_rows(block, steps, packed, saturate):
    pieces = []
    for n, (axis, bit) in enumerate(steps):
        count = lax.axis_size(axis)
        if n < len(SPANS):
            block, packed = lax.optimization_barrier((block, packed))
        other = lax.ppermute(block, axis, [(i, i ^ bit) for i in range(count)])
        if n < len(SPANS):
            piece = saturate(n, packed)
        block = jnp.concatenate([block, other], axis=0)
        if n < len(SPANS):
            block, piece = lax.optimization_barrier((block, piece))
            pieces.append(piece)
    return block, pieces + [saturate(n, packed) for n in range(len(pieces), len(SPANS))]


def bits_of(axis, count):
    bits = []
    while (1 << len(bits)) < count:
        bits.append((axis, 1 << len(bits)))
    return bits


def vmem():
    return pl.BlockSpec(memory_space=pltpu.VMEM)


def smem():
    return pl.BlockSpec(memory_space=pltpu.SMEM)


def moments_shape(outer, inner, members):
    return (
        jax.ShapeDtypeStruct((outer, inner, members), jnp.bfloat16),
        jax.ShapeDtypeStruct((outer, inner, 1), jnp.float32),
    )


def shards(
    fields, pore_mask, conv_kernel, conv_bias, read_weight, obs_cells, obs_values, obs_sigma
):
    _, planes, columns, lanes, members = fields.shape
    channels = conv_kernel.shape[1]
    rows = planes * columns
    observed = obs_cells.shape[0]

    odd = lax.axis_index("cores") % 2
    near_plane = (1 - odd) * (planes - 1)
    far = lax.dynamic_slice_in_dim(fields, odd * (planes - 1), 1, axis=1)
    near = lax.dynamic_slice_in_dim(fields, near_plane, 1, axis=1)
    far, near = lax.optimization_barrier((far, near))
    far_left = swap_far_corner(far[:, :, -1:], 1)
    far_right = swap_far_corner(far[:, :, :1], -1)
    far = swap_cores(far, False)
    near, tied = lax.optimization_barrier((swap_cores(near, True), fields))
    left = shift(tied[:, :, -1:], "face", 1, False)
    right = shift(tied[:, :, :1], "face", -1, False)
    near_sides = [lax.dynamic_slice_in_dim(side, near_plane, 1, axis=1) for side in (left, right)]
    near_corner = swap_cores(jnp.concatenate(near_sides, axis=0), True)

    selector = tap_selector(planes, columns)
    count = selector.shape[2] // 3
    taps = jnp.dot(
        jnp.transpose(conv_kernel),
        jnp.asarray(selector.reshape(54, -1), jnp.bfloat16),
        preferred_element_type=jnp.float32,
    ).reshape(channels, rows, 3 * count)
    bias = jnp.stack(three_pieces(0.5 * conv_bias), axis=1)
    bias = jnp.broadcast_to(bias[:, None, :], (channels, rows, 3))
    weights = jnp.concatenate(
        [0.5 * taps, bias, jnp.zeros((channels, rows, 13), jnp.float32)], axis=2
    ).astype(jnp.bfloat16)
    by_row = jnp.transpose(weights, (1, 0, 2))
    weights = weights.reshape(channels * rows, 3 * count + 16)
    flat = lambda a: a.reshape(-1, lanes, members)
    starts = [sum(SPANS[:n]) for n in range(len(SPANS))]
    mask = pore_mask.reshape(rows, lanes)
    mask_float = mask.astype(jnp.float32)
    read_half = 0.5 * read_weight
    swap_in = jnp.asarray(swap_matrix(16, 16), jnp.bfloat16)
    swap_out = jnp.asarray(swap_matrix(16, rows), jnp.bfloat16)
    params = pltpu.CompilerParams(vmem_limit_bytes=VMEM_BYTES)
    field_moments = pl.pallas_call(
        moments_kernel,
        out_shape=moments_shape(2 * rows, lanes, members),
        in_specs=[vmem()],
        out_specs=(vmem(), vmem()),
        compiler_params=params,
        name="moments",
    )(flat(fields))
    by_row, field_moments = lax.optimization_barrier((by_row, tuple(field_moments)))
    packed, pay = pl.pallas_call(
        observe_kernel,
        out_shape=(
            jax.ShapeDtypeStruct((lanes + 2, count, members), jnp.bfloat16),
            jax.ShapeDtypeStruct((observed + PAY_ROWS, members), jnp.bfloat16),
        ),
        in_specs=[vmem()] * 13 + [smem()] * 3,
        out_specs=(vmem(), vmem()),
        scratch_shapes=[pltpu.VMEM((observed, members), jnp.float32)],
        compiler_params=params,
        name="observe",
    )(
        flat(fields), flat(far), flat(near), flat(left), flat(right), flat(far_left),
        flat(far_right), flat(near_corner), by_row, swap_in, read_half[:, None],
        obs_sigma[:, None], obs_values[:, None], obs_cells, mask, odd.astype(jnp.int32)[None],
    )

    def saturate(n, packed):
        span = SPANS[n]
        return pl.pallas_call(
            functools.partial(saturate_kernel, starts[n]),
            out_shape=moments_shape(rows, span, members),
            in_specs=[vmem()] * 4 + [smem()],
            out_specs=(vmem(), vmem()),
            scratch_shapes=[pltpu.VMEM((rows * span, members), jnp.bfloat16)],
            compiler_params=params,
            cost_estimate=pl.CostEstimate(
                flops=2 * 256 * 256 * span * members,
                bytes_accessed=4 * 1024 * 1024,
                transcendentals=channels * rows * span * members,
            ),
            name="saturate",
        )(packed, weights, swap_out, mask_float, read_half)

    core_count, face_count = lax.axis_size("cores"), lax.axis_size("face")
    devices = core_count * face_count
    gathered = devices <= GATHER_DEVICES and devices & (devices - 1) == 0
    if gathered:
        steps = bits_of("face", face_count)[::-1] + bits_of("cores", core_count)[1:]
        steps = steps + bits_of("cores", core_count)[:1]
        block, pieces = gather_rows(pay[None], steps, packed, saturate)
        terms = (block,)
    else:
        part = pay[:observed]
        gram = lax.dot_general(
            part, part, (((0,), (0,)), ((), ())), preferred_element_type=jnp.float32
        )
        coeff = jnp.sum(pay[observed:].astype(jnp.float32), axis=0, keepdims=True)
        terms = lax.psum((gram, coeff), ("cores", "face"))
        pieces = [saturate(n, packed) for n in range(len(SPANS))]
    out = pl.pallas_call(
        functools.partial(update_kernel, gathered),
        out_shape=jax.ShapeDtypeStruct((3 * rows, lanes, members), jnp.bfloat16),
        in_specs=[vmem()] * (len(terms) + 2 + 2 * len(SPANS)),
        out_specs=vmem(),
        scratch_shapes=[
            pltpu.VMEM((members, members), jnp.float32),
            pltpu.VMEM((members, members), jnp.bfloat16),
        ],
        compiler_params=params,
        name="update",
    )(*terms, *field_moments, *(part for piece in pieces for part in piece))
    return out.reshape(3, planes, columns, lanes, members)


def solution(mesh):
    return jax.shard_map(
        shards,
        mesh=mesh,
        in_specs=(
            P(None, "cores", "face", None, None),
            P("cores", "face", None),
            P(),
            P(),
            P(),
            P(("cores", "face")),
            P(("cores", "face")),
            P(("cores", "face")),
        ),
        out_specs=P(None, "cores", "face", None, None),
        check_vma=False,
    )
```

```python
import functools
import math

import jax
import jax.numpy as jnp
import numpy as np
from jax import lax
from jax.experimental import pallas as pl
from jax.experimental.pallas import tpu as pltpu
from jax.sharding import PartitionSpec as P

HIGHEST = lax.Precision.HIGHEST
PAY_ROWS = 16
GATHER_DEVICES = 64
BLOCK = 64
SPANS = (16, 32, 32, 48)
VMEM_BYTES = 32 * 1024 * 1024


def plane_places(planes, columns):
    own = [(f, z + 1, x + 1) for f in range(2) for z in range(planes) for x in range(columns)]
    low = [(f, 0, x + 1) for f in range(2) for x in range(columns)]
    high = [(f, planes + 1, x + 1) for f in range(2) for x in range(columns)]
    left = [(f, z + 1, 0) for f in range(2) for z in range(planes)]
    right = [(f, z + 1, columns + 1) for f in range(2) for z in range(planes)]
    corners = [
        (f, z, x) for z in (0, planes + 1) for x in (0, columns + 1) for f in range(2)
    ]
    return own + low + high + left + right + corners


def tap_selector(planes, columns):
    places = plane_places(planes, columns)
    chosen = np.zeros((54, planes * columns, 3 * len(places)), np.float32)
    for z in range(planes):
        for x in range(columns):
            for n, (f, zz, xx) in enumerate(places):
                a, b = zz - z, xx - x
                if 0 <= a <= 2 and 0 <= b <= 2:
                    for c in range(3):
                        chosen[27 * f + 9 * a + 3 * b + c, z * columns + x, c * len(places) + n] = 1.0
    return chosen


def swap_matrix(outer, inner):
    matrix = np.zeros((outer * inner, outer * inner), np.float32)
    for i in range(outer):
        for j in range(inner):
            matrix[j * outer + i, i * inner + j] = 1.0
    return matrix


def three_pieces(value):
    first = lax.reduce_precision(value, 8, 7)
    second = lax.reduce_precision(value - first, 8, 7)
    third = lax.reduce_precision(value - first - second, 8, 7)
    return first, second, third


def ones_rows(members):
    row_index = lax.broadcasted_iota(jnp.int32, (16, members), 0)
    return jnp.where(row_index < 3, 1.0, 0.0).astype(jnp.bfloat16)


def ordered(odd, far, near):
    return jnp.where(odd == 0, far, near), jnp.where(odd == 0, near, far)


def observe_kernel(
    own, far, near, left, right, far_left, far_right, near_corner, by_row, swap_in, read_column,
    observations, cells, mask, odd, packed, pay_out, pred
):
    lanes, members = own.shape[1], own.shape[2]
    count = packed.shape[1]
    observed = cells.shape[0]
    packed[0] = jnp.zeros((count, members), jnp.bfloat16)
    packed[lanes + 1] = jnp.zeros((count, members), jnp.bfloat16)

    for step in range(lanes // 16):
        at = step * 16
        part = lambda ref: ref[:, pl.ds(at, 16), :]
        far_block, near_block = part(far), part(near)
        far_sides = jnp.concatenate([part(far_left), part(far_right)], axis=0)
        near_sides = part(near_corner)
        blocks = (
            part(own),
            jnp.concatenate(ordered(odd[0], far_block, near_block), axis=0),
            jnp.concatenate(
                [part(left), part(right), *ordered(odd[0], far_sides, near_sides)], axis=0
            ),
        )
        for g, block in enumerate(blocks):
            moved = jnp.dot(
                swap_in[...], block.reshape(256, members), preferred_element_type=jnp.float32
            )
            packed[pl.ds(at + 1, 16), 16 * g : 16 * g + 16, :] = (
                moved.astype(jnp.bfloat16).reshape(16, 16, members)
            )

    ones = ones_rows(members)
    read = jnp.broadcast_to(read_column[...], (read_column.shape[0], members))

    def some_cells(step, carry):
        for k in range(16):
            o = step * 16 + k
            cell = cells[o]
            row, y = cell // lanes, cell % lanes
            taps = jnp.concatenate(
                [packed[pl.ds(y, 3)].reshape(3 * count, members), ones], axis=0
            )
            half = jnp.dot(by_row[row], taps, preferred_element_type=jnp.float32)
            total = jnp.sum(read * (half * (1.0 + jnp.tanh(half))), axis=0, keepdims=True)
            found = (0.5 + 0.5 * jnp.tanh(total)) * mask[row, y].astype(jnp.float32)
            pred[pl.ds(o, 1), :] = found.astype(jnp.bfloat16).astype(jnp.float32)
        return carry

    lax.fori_loop(0, observed // 16, some_cells, 0)

    root_count = math.sqrt(members - 1)
    predicted = pred[...]
    center = jnp.mean(predicted, axis=1, keepdims=True)
    inverse_sigma = 1.0 / observations[:, 0:1]
    scaled = (predicted - center) * (inverse_sigma / root_count)
    innovation = (observations[:, 1:2] - center) * inverse_sigma
    coeff = jnp.sum(scaled * innovation, axis=0, keepdims=True) / root_count
    first = coeff.astype(jnp.bfloat16).astype(jnp.float32)
    second = (coeff - first).astype(jnp.bfloat16).astype(jnp.float32)
    third = coeff - first - second
    index = lax.broadcasted_iota(jnp.int32, (PAY_ROWS, members), 0)
    tail = jnp.where(index == 0, first, jnp.where(index == 1, second, jnp.where(index == 2, third, 0.0)))
    pay_out[0:observed, :] = scaled.astype(jnp.bfloat16)
    pay_out[observed : observed + PAY_ROWS, :] = tail.astype(jnp.bfloat16)


def saturate_kernel(
    start, packed, weights, swap_out, mask, read_half, anomaly_out, mean_out, sat_rows
):
    rows, span, members = anomaly_out.shape
    count = packed.shape[1]
    channels = read_half.shape[0]
    ones = ones_rows(members)
    lane_index = lax.broadcasted_iota(jnp.int32, mask.shape, 1)

    def some_rows(step, carry):
        found = []
        for k in range(8):
            y = start + step * 8 + k
            taps = jnp.concatenate(
                [packed[pl.ds(y, 3)].reshape(3 * count, members), ones], axis=0
            )
            half = jnp.dot(weights[...], taps, preferred_element_type=jnp.float32)
            total = jnp.zeros((rows, members), jnp.float32)
            for c in range(channels):
                part = half[rows * c : rows * c + rows]
                total = total + read_half[c] * (part * (1.0 + jnp.tanh(part)))
            here = jnp.sum(jnp.where(lane_index == y, mask[...], 0.0), axis=1, keepdims=True)
            found.append(here * (0.5 + 0.5 * jnp.tanh(total)))
        at = pl.multiple_of(step * 8 * rows, 8 * rows)
        sat_rows[pl.ds(at, 8 * rows), :] = jnp.concatenate(found, axis=0).astype(jnp.bfloat16)
        return carry

    lax.fori_loop(0, span // 8, some_rows, 0)
    for n in range(span // 16):
        block = sat_rows[n * 16 * rows : (n + 1) * 16 * rows, :]
        moved = jnp.dot(swap_out[...], block, preferred_element_type=jnp.float32)
        mean = jnp.mean(moved, axis=1, keepdims=True)
        anomalies = (moved - mean).astype(jnp.bfloat16)
        anomaly_out[:, n * 16 : n * 16 + 16, :] = anomalies.reshape(rows, 16, members)
        mean_out[:, n * 16 : n * 16 + 16, :] = mean.reshape(rows, 16, 1)


def moments_kernel(fields, anomaly_out, mean_out):
    def step(n, carry):
        state = fields[pl.ds(2 * n, 2)].astype(jnp.float32)
        mean = jnp.mean(state, axis=2, keepdims=True)
        anomaly_out[pl.ds(2 * n, 2)] = (state - mean).astype(jnp.bfloat16)
        mean_out[pl.ds(2 * n, 2)] = mean
        return carry

    lax.fori_loop(0, fields.shape[0] // 2, step, 0)


def transposed_dot(a, b, precision):
    return lax.dot_general(
        a, b, (((0,), (0,)), ((), ())), preferred_element_type=jnp.float32, precision=precision
    )


def spread_row(part, p):
    return jnp.broadcast_to(part[p : p + 1, :], part.shape)


def spread_lane(part, q):
    return jnp.broadcast_to(part[:, q : q + 1], part.shape)


def inverse_factor_block(block):
    lane = lax.broadcasted_iota(jnp.int32, (8, 2 * BLOCK), 1)
    sub = lax.broadcasted_iota(jnp.int32, (8, 2 * BLOCK), 0)
    groups = BLOCK // 8
    parts = []
    for i in range(groups):
        unit = jnp.where(lane == sub + (BLOCK + 8 * i), 1.0, 0.0)
        known = jnp.concatenate(
            [block[8 * i : 8 * i + 8, :], jnp.zeros((8, BLOCK), jnp.float32)], axis=1
        )
        parts.append(known + unit)
    done = []
    for j in range(groups):
        corner = [spread_lane(parts[j], 8 * j + q) for q in range(8)]
        entry = {(p, q): spread_row(corner[q], p) for q in range(8) for p in range(q, 8)}
        line = [spread_row(parts[j], p) for p in range(8)]
        near = j + 1 < groups
        if near:
            beside = [spread_lane(parts[j + 1], 8 * j + q) for q in range(8)]
        factor, scale = {}, []
        for q in range(8):
            root = lax.rsqrt(entry[q, q])
            scale.append(root)
            line[q] = line[q] * root
            for p in range(q + 1, 8):
                factor[p, q] = entry[p, q] * root
            for t in range(q + 1, 8):
                for p in range(t, 8):
                    entry[p, t] = entry[p, t] - factor[p, q] * factor[t, q]
            for p in range(q + 1, 8):
                line[p] = line[p] - factor[p, q] * line[q]
            if near:
                lead = beside[q] * root
                for t in range(q + 1, 8):
                    beside[t] = beside[t] - lead * factor[t, q]
                parts[j + 1] = parts[j + 1] - lead * line[q]
        if j + 2 < groups:
            weighted = [None] * 8
            for q in range(7, -1, -1):
                rest = line[q]
                for p in range(q + 1, 8):
                    rest = rest - factor[p, q] * weighted[p]
                weighted[q] = rest * scale[q]
            for i in range(j + 2, groups):
                change = spread_lane(parts[i], 8 * j) * weighted[0]
                for q in range(1, 8):
                    change = change + spread_lane(parts[i], 8 * j + q) * weighted[q]
                parts[i] = parts[i] - change
        merged = line[0]
        for q in range(1, 8):
            merged = jnp.where(sub == q, line[q], merged)
        done.append(merged[:, BLOCK:])
    return jnp.concatenate(done, axis=0)


def update_kernel(gathered, *refs):
    if gathered:
        pay, refs = refs[0], refs[1:]
    else:
        gram, coeff_in, refs = refs[0], refs[1], refs[2:]
    moments, (out, joint, mixing) = refs[:-3], refs[-3:]
    members = out.shape[2]
    sub = lax.broadcasted_iota(jnp.int32, (members, members), 0)
    lane = lax.broadcasted_iota(jnp.int32, (members, members), 1)
    identity = jnp.where(sub == lane, 1.0, 0.0)
    if gathered:
        devices, observed = pay.shape[0], pay.shape[1] - PAY_ROWS
        group = max(1, 256 // observed)
        total = identity
        for d in range(0, devices, group):
            block = pay[d : d + group, 0:observed, :].reshape(-1, members)
            total = total + transposed_dot(block, block, None)
        coeff = jnp.zeros((PAY_ROWS, members), jnp.float32)
        for d in range(devices):
            coeff = coeff + pay[d, observed:, :].astype(jnp.float32)
        coeff = jnp.sum(coeff, axis=0, keepdims=True)
    else:
        total = identity + gram[...]
        coeff = coeff_in[...]
    joint[...] = total
    for k in range(members // BLOCK):
        at = k * BLOCK
        below = at + BLOCK
        wide_sub, wide_lane = sub[0:BLOCK, :], lane[0:BLOCK, :]
        inside = jnp.logical_and(wide_lane >= at, wide_lane < below)
        row = joint[at:below, :]
        inverse = inverse_factor_block(row[:, at:below])
        unit = jnp.where(wide_lane == wide_sub + at, 1.0, 0.0)
        row = jnp.dot(
            inverse,
            jnp.where(inside, unit, row),
            precision=HIGHEST,
            preferred_element_type=jnp.float32,
        )
        joint[at:below, :] = row
        if below < members:
            ahead = jnp.where(wide_lane >= below, row, 0.0)
            change = transposed_dot(ahead, row, HIGHEST)
            rest_lane = lane[below:, :]
            inside = jnp.logical_and(rest_lane >= at, rest_lane < below)
            joint[below:, :] = jnp.where(inside, 0.0, joint[below:, :]) - change[below:, :]
    inverse = jnp.where(lane <= sub, joint[...], 0.0)
    half = jnp.sum(inverse * coeff, axis=1, keepdims=True)
    weight = jnp.sum(inverse * half, axis=0, keepdims=True)
    mixing[...] = jnp.transpose((inverse + weight).astype(jnp.bfloat16))

    def blend(anomalies, mean):
        outer, inner = anomalies.shape[0], anomalies.shape[1]
        moved = jnp.dot(
            anomalies.reshape(outer * inner, members), mixing[...], preferred_element_type=jnp.float32
        )
        return (mean + moved.reshape(outer, inner, members)).astype(jnp.bfloat16)

    anomalies, mean = moments[:2]
    field_rows = anomalies.shape[0]

    def step(n, carry):
        for k in range(2):
            at = 4 * n + 2 * k
            out[pl.ds(at, 2)] = blend(anomalies[pl.ds(at, 2)], mean[pl.ds(at, 2)])
        return carry

    lax.fori_loop(0, field_rows // 4, step, 0)
    at = 0
    for n in range(1, len(moments) // 2):
        anomalies, mean = moments[2 * n : 2 * n + 2]
        span = anomalies.shape[1]
        out[field_rows:, at : at + span, :] = blend(anomalies[...], mean[...])
        at += span


def shift(value, axis, by, closed):
    count = lax.axis_size(axis)
    if by > 0:
        pairs = [(i, (i + 1) % count) for i in range(count if closed else count - 1)]
    else:
        pairs = [((i + 1) % count, i) for i in range(count if closed else count - 1)]
    return lax.ppermute(value, axis, pairs)


def core_pairs(inside):
    count = lax.axis_size("cores")
    steps = [1 if (i % 2 == 0) == inside else -1 for i in range(count)]
    return [(i, (i + step) % count) for i, step in enumerate(steps)]


def swap_cores(value, inside):
    return lax.ppermute(value, "cores", core_pairs(inside))


def swap_far_corner(value, face_by):
    face_count = lax.axis_size("face")
    pairs = [
        (i * face_count + j, other * face_count + j + face_by)
        for i, other in core_pairs(False)
        for j in range(face_count)
        if 0 <= j + face_by < face_count
    ]
    return lax.ppermute(value, ("cores", "face"), pairs)


def gather_rows(block, steps, packed, saturate):
    pieces = []
    for n, (axis, bit) in enumerate(steps):
        count = lax.axis_size(axis)
        if n < len(SPANS):
            block, packed = lax.optimization_barrier((block, packed))
        other = lax.ppermute(block, axis, [(i, i ^ bit) for i in range(count)])
        if n < len(SPANS):
            piece = saturate(n, packed)
        block = jnp.concatenate([block, other], axis=0)
        if n < len(SPANS):
            block, piece = lax.optimization_barrier((block, piece))
            pieces.append(piece)
    return block, pieces + [saturate(n, packed) for n in range(len(pieces), len(SPANS))]


def bits_of(axis, count):
    bits = []
    while (1 << len(bits)) < count:
        bits.append((axis, 1 << len(bits)))
    return bits


def vmem():
    return pl.BlockSpec(memory_space=pltpu.VMEM)


def smem():
    return pl.BlockSpec(memory_space=pltpu.SMEM)


def moments_shape(outer, inner, members):
    return (
        jax.ShapeDtypeStruct((outer, inner, members), jnp.bfloat16),
        jax.ShapeDtypeStruct((outer, inner, 1), jnp.float32),
    )


def shards(
    fields, pore_mask, conv_kernel, conv_bias, read_weight, obs_cells, obs_values, obs_sigma
):
    _, planes, columns, lanes, members = fields.shape
    channels = conv_kernel.shape[1]
    rows = planes * columns
    observed = obs_cells.shape[0]

    odd = lax.axis_index("cores") % 2
    far_plane, near_plane = odd * (planes - 1), (1 - odd) * (planes - 1)
    plane = lambda at: lax.dynamic_index_in_dim(fields, at, 1, keepdims=False)
    cell_row = lambda at, column: lax.dynamic_slice(
        fields, (0, at, column, 0, 0), (2, 1, 1, lanes, members)
    ).reshape(2, lanes, members)
    sent = (
        plane(near_plane), plane(far_plane), cell_row(far_plane, columns - 1), cell_row(far_plane, 0)
    )
    near, far, far_left, far_right = lax.optimization_barrier(sent)
    far_left = swap_far_corner(far_left, 1)
    far_right = swap_far_corner(far_right, -1)
    far = swap_cores(far, False)
    near, tied = lax.optimization_barrier((swap_cores(near, True), fields))
    left = shift(tied[:, :, -1], "face", 1, False)
    right = shift(tied[:, :, 0], "face", -1, False)

    selector = tap_selector(planes, columns)
    count = selector.shape[2] // 3
    taps = jnp.dot(
        jnp.transpose(conv_kernel),
        jnp.asarray(selector.reshape(54, -1), jnp.bfloat16),
        preferred_element_type=jnp.float32,
    ).reshape(channels, rows, 3 * count)
    bias = jnp.stack(three_pieces(0.5 * conv_bias), axis=1)
    bias = jnp.broadcast_to(bias[:, None, :], (channels, rows, 3))
    weights = jnp.concatenate(
        [0.5 * taps, bias, jnp.zeros((channels, rows, 13), jnp.float32)], axis=2
    ).astype(jnp.bfloat16)
    by_row = jnp.transpose(weights, (1, 0, 2))
    weights = weights.reshape(channels * rows, 3 * count + 16)
    flat = lambda a: a.reshape(-1, lanes, members)
    starts = [sum(SPANS[:n]) for n in range(len(SPANS))]
    mask = pore_mask.reshape(rows, lanes)
    mask_float = mask.astype(jnp.float32)
    read_half = 0.5 * read_weight
    swap_in = jnp.asarray(swap_matrix(16, 16), jnp.bfloat16)
    swap_out = jnp.asarray(swap_matrix(16, rows), jnp.bfloat16)
    params = pltpu.CompilerParams(vmem_limit_bytes=VMEM_BYTES)
    field_moments = pl.pallas_call(
        moments_kernel,
        out_shape=moments_shape(2 * rows, lanes, members),
        in_specs=[vmem()],
        out_specs=(vmem(), vmem()),
        compiler_params=params,
        name="moments",
    )(flat(fields))
    near_sides = jnp.concatenate(
        [lax.dynamic_index_in_dim(side, near_plane, 1, keepdims=False) for side in (left, right)]
    )
    read_column = read_half[:, None]
    observations = jnp.stack([obs_sigma, obs_values], axis=1)
    prepared = (by_row, weights, mask_float, read_column, observations, *field_moments)
    near_sides, far_left, far_right, prepared = lax.optimization_barrier(
        (near_sides, far_left, far_right, prepared)
    )
    by_row, weights, mask_float, read_column, observations, *field_moments = prepared
    near_corner = swap_cores(near_sides, True)
    packed, pay = pl.pallas_call(
        observe_kernel,
        out_shape=(
            jax.ShapeDtypeStruct((lanes + 2, count, members), jnp.bfloat16),
            jax.ShapeDtypeStruct((observed + PAY_ROWS, members), jnp.bfloat16),
        ),
        in_specs=[vmem()] * 12 + [smem()] * 3,
        out_specs=(vmem(), vmem()),
        scratch_shapes=[pltpu.VMEM((observed, members), jnp.float32)],
        compiler_params=params,
        name="observe",
    )(
        flat(fields), flat(far), flat(near), flat(left), flat(right), flat(far_left),
        flat(far_right), flat(near_corner), by_row, swap_in, read_column, observations,
        obs_cells, mask, odd.astype(jnp.int32)[None],
    )

    def saturate(n, packed):
        span = SPANS[n]
        return pl.pallas_call(
            functools.partial(saturate_kernel, starts[n]),
            out_shape=moments_shape(rows, span, members),
            in_specs=[vmem()] * 4 + [smem()],
            out_specs=(vmem(), vmem()),
            scratch_shapes=[pltpu.VMEM((rows * span, members), jnp.bfloat16)],
            compiler_params=params,
            cost_estimate=pl.CostEstimate(
                flops=2 * 256 * 256 * span * members,
                bytes_accessed=4 * 1024 * 1024,
                transcendentals=channels * rows * span * members,
            ),
            name="saturate",
        )(packed, weights, swap_out, mask_float, read_half)

    core_count, face_count = lax.axis_size("cores"), lax.axis_size("face")
    devices = core_count * face_count
    gathered = devices <= GATHER_DEVICES and devices & (devices - 1) == 0
    if gathered:
        steps = bits_of("face", face_count)[::-1] + bits_of("cores", core_count)[1:]
        steps = steps + bits_of("cores", core_count)[:1]
        block, pieces = gather_rows(pay[None], steps, packed, saturate)
        terms = (block,)
    else:
        part = pay[:observed]
        gram = lax.dot_general(
            part, part, (((0,), (0,)), ((), ())), preferred_element_type=jnp.float32
        )
        coeff = jnp.sum(pay[observed:].astype(jnp.float32), axis=0, keepdims=True)
        terms = lax.psum((gram, coeff), ("cores", "face"))
        pieces = [saturate(n, packed) for n in range(len(SPANS))]
    out = pl.pallas_call(
        functools.partial(update_kernel, gathered),
        out_shape=jax.ShapeDtypeStruct((3 * rows, lanes, members), jnp.bfloat16),
        in_specs=[vmem()] * (len(terms) + 2 + 2 * len(SPANS)),
        out_specs=vmem(),
        scratch_shapes=[
            pltpu.VMEM((members, members), jnp.float32),
            pltpu.VMEM((members, members), jnp.bfloat16),
        ],
        compiler_params=params,
        name="update",
    )(*terms, *field_moments, *(part for piece in pieces for part in piece))
    return out.reshape(3, planes, columns, lanes, members)


def solution(mesh):
    return jax.shard_map(
        shards,
        mesh=mesh,
        in_specs=(
            P(None, "cores", "face", None, None),
            P("cores", "face", None),
            P(),
            P(),
            P(),
            P(("cores", "face")),
            P(("cores", "face")),
            P(("cores", "face")),
        ),
        out_specs=P(None, "cores", "face", None, None),
        check_vma=False,
    )
```

```python
import functools
import math

import jax
import jax.numpy as jnp
import numpy as np
from jax import lax
from jax.experimental import pallas as pl
from jax.experimental.pallas import tpu as pltpu
from jax.sharding import PartitionSpec as P

HIGHEST = lax.Precision.HIGHEST
PAY_ROWS = 16
GATHER_DEVICES = 64
BLOCK = 64
SPANS = (16, 32, 32, 48)
VMEM_BYTES = 8 * 1024 * 1024


def plane_places(planes, columns):
    own = [(f, z + 1, x + 1) for f in range(2) for z in range(planes) for x in range(columns)]
    low = [(f, 0, x + 1) for f in range(2) for x in range(columns)]
    high = [(f, planes + 1, x + 1) for f in range(2) for x in range(columns)]
    left = [(f, z + 1, 0) for f in range(2) for z in range(planes)]
    right = [(f, z + 1, columns + 1) for f in range(2) for z in range(planes)]
    corners = [
        (f, z, x) for z in (0, planes + 1) for f in range(2) for x in (0, columns + 1)
    ]
    return own + low + high + left + right + corners


def tap_selector(planes, columns):
    places = plane_places(planes, columns)
    chosen = np.zeros((54, planes * columns, 3 * len(places)), np.float32)
    for z in range(planes):
        for x in range(columns):
            for n, (f, zz, xx) in enumerate(places):
                a, b = zz - z, xx - x
                if 0 <= a <= 2 and 0 <= b <= 2:
                    for c in range(3):
                        chosen[27 * f + 9 * a + 3 * b + c, z * columns + x, c * len(places) + n] = 1.0
    return chosen


def swap_matrix(outer, inner):
    matrix = np.zeros((outer * inner, outer * inner), np.float32)
    for i in range(outer):
        for j in range(inner):
            matrix[j * outer + i, i * inner + j] = 1.0
    return matrix


def three_pieces(value):
    first = lax.reduce_precision(value, 8, 7)
    second = lax.reduce_precision(value - first, 8, 7)
    third = lax.reduce_precision(value - first - second, 8, 7)
    return first, second, third


def ones_rows(members):
    row_index = lax.broadcasted_iota(jnp.int32, (16, members), 0)
    return jnp.where(row_index < 3, 1.0, 0.0).astype(jnp.bfloat16)


def observe_kernel(
    own, low, high, left, right, corner_low, corner_high, by_row, swap_in, read_column,
    observations, cells, mask, packed, pay_out, pred
):
    lanes, members = own.shape[1], own.shape[2]
    count = packed.shape[1]
    observed = cells.shape[0]
    packed[0] = jnp.zeros((count, members), jnp.bfloat16)
    packed[lanes + 1] = jnp.zeros((count, members), jnp.bfloat16)

    for step in range(lanes // 16):
        at = step * 16
        part = lambda ref: ref[:, pl.ds(at, 16), :]
        sides = (left, right, corner_low, corner_high)
        blocks = (
            part(own),
            jnp.concatenate([part(low), part(high)], axis=0),
            jnp.concatenate([part(side) for side in sides], axis=0),
        )
        for g, block in enumerate(blocks):
            moved = jnp.dot(
                swap_in[...], block.reshape(256, members), preferred_element_type=jnp.float32
            )
            packed[pl.ds(at + 1, 16), 16 * g : 16 * g + 16, :] = (
                moved.astype(jnp.bfloat16).reshape(16, 16, members)
            )

    ones = ones_rows(members)
    read = jnp.broadcast_to(read_column[...], (read_column.shape[0], members))

    def some_cells(step, carry):
        for k in range(16):
            o = step * 16 + k
            cell = cells[o]
            row, y = cell // lanes, cell % lanes
            taps = jnp.concatenate(
                [packed[pl.ds(y, 3)].reshape(3 * count, members), ones], axis=0
            )
            half = jnp.dot(by_row[row], taps, preferred_element_type=jnp.float32)
            total = jnp.sum(read * (half * (1.0 + jnp.tanh(half))), axis=0, keepdims=True)
            found = (0.5 + 0.5 * jnp.tanh(total)) * mask[row, y].astype(jnp.float32)
            pred[pl.ds(o, 1), :] = found.astype(jnp.bfloat16).astype(jnp.float32)
        return carry

    lax.fori_loop(0, observed // 16, some_cells, 0)

    root_count = math.sqrt(members - 1)
    predicted = pred[...]
    center = jnp.mean(predicted, axis=1, keepdims=True)
    inverse_sigma = 1.0 / observations[:, 0:1]
    scaled = (predicted - center) * (inverse_sigma / root_count)
    innovation = (observations[:, 1:2] - center) * inverse_sigma
    coeff = jnp.sum(scaled * innovation, axis=0, keepdims=True) / root_count
    first = coeff.astype(jnp.bfloat16).astype(jnp.float32)
    second = (coeff - first).astype(jnp.bfloat16).astype(jnp.float32)
    third = coeff - first - second
    index = lax.broadcasted_iota(jnp.int32, (PAY_ROWS, members), 0)
    tail = jnp.where(index == 0, first, jnp.where(index == 1, second, jnp.where(index == 2, third, 0.0)))
    pay_out[0:observed, :] = scaled.astype(jnp.bfloat16)
    pay_out[observed : observed + PAY_ROWS, :] = tail.astype(jnp.bfloat16)


def saturate_kernel(
    start, packed, weights, swap_out, mask, read_half, anomaly_out, mean_out, sat_rows
):
    rows, span, members = anomaly_out.shape
    count = packed.shape[1]
    channels = read_half.shape[0]
    ones = ones_rows(members)
    lane_index = lax.broadcasted_iota(jnp.int32, mask.shape, 1)

    def some_rows(step, carry):
        found = []
        for k in range(8):
            y = start + step * 8 + k
            taps = jnp.concatenate(
                [packed[pl.ds(y, 3)].reshape(3 * count, members), ones], axis=0
            )
            half = jnp.dot(weights[...], taps, preferred_element_type=jnp.float32)
            total = jnp.zeros((rows, members), jnp.float32)
            for c in range(channels):
                part = half[rows * c : rows * c + rows]
                total = total + read_half[c] * (part * (1.0 + jnp.tanh(part)))
            here = jnp.sum(jnp.where(lane_index == y, mask[...], 0.0), axis=1, keepdims=True)
            found.append(here * (0.5 + 0.5 * jnp.tanh(total)))
        at = pl.multiple_of(step * 8 * rows, 8 * rows)
        sat_rows[pl.ds(at, 8 * rows), :] = jnp.concatenate(found, axis=0).astype(jnp.bfloat16)
        return carry

    lax.fori_loop(0, span // 8, some_rows, 0)
    for n in range(span // 16):
        block = sat_rows[n * 16 * rows : (n + 1) * 16 * rows, :]
        moved = jnp.dot(swap_out[...], block, preferred_element_type=jnp.float32)
        mean = jnp.mean(moved, axis=1, keepdims=True)
        anomalies = (moved - mean).astype(jnp.bfloat16)
        anomaly_out[:, n * 16 : n * 16 + 16, :] = anomalies.reshape(rows, 16, members)
        mean_out[:, n * 16 : n * 16 + 16, :] = mean.reshape(rows, 16, 1)


def moments_kernel(fields, anomaly_out, mean_out):
    def step(n, carry):
        state = fields[pl.ds(2 * n, 2)].astype(jnp.float32)
        mean = jnp.mean(state, axis=2, keepdims=True)
        anomaly_out[pl.ds(2 * n, 2)] = (state - mean).astype(jnp.bfloat16)
        mean_out[pl.ds(2 * n, 2)] = mean
        return carry

    lax.fori_loop(0, fields.shape[0] // 2, step, 0)


def transposed_dot(a, b, precision):
    return lax.dot_general(
        a, b, (((0,), (0,)), ((), ())), preferred_element_type=jnp.float32, precision=precision
    )


def spread_row(part, p):
    return jnp.broadcast_to(part[p : p + 1, :], part.shape)


def spread_lane(part, q):
    return jnp.broadcast_to(part[:, q : q + 1], part.shape)


def inverse_factor_block(block):
    lane = lax.broadcasted_iota(jnp.int32, (8, 2 * BLOCK), 1)
    sub = lax.broadcasted_iota(jnp.int32, (8, 2 * BLOCK), 0)
    groups = BLOCK // 8
    parts = []
    for i in range(groups):
        unit = jnp.where(lane == sub + (BLOCK + 8 * i), 1.0, 0.0)
        known = jnp.concatenate(
            [block[8 * i : 8 * i + 8, :], jnp.zeros((8, BLOCK), jnp.float32)], axis=1
        )
        parts.append(known + unit)
    done = []
    for j in range(groups):
        corner = [spread_lane(parts[j], 8 * j + q) for q in range(8)]
        entry = {(p, q): spread_row(corner[q], p) for q in range(8) for p in range(q, 8)}
        line = [spread_row(parts[j], p) for p in range(8)]
        near = j + 1 < groups
        if near:
            beside = [spread_lane(parts[j + 1], 8 * j + q) for q in range(8)]
        factor, scale = {}, []
        for q in range(8):
            root = lax.rsqrt(entry[q, q])
            scale.append(root)
            line[q] = line[q] * root
            for p in range(q + 1, 8):
                factor[p, q] = entry[p, q] * root
            for t in range(q + 1, 8):
                for p in range(t, 8):
                    entry[p, t] = entry[p, t] - factor[p, q] * factor[t, q]
            for p in range(q + 1, 8):
                line[p] = line[p] - factor[p, q] * line[q]
            if near:
                lead = beside[q] * root
                for t in range(q + 1, 8):
                    beside[t] = beside[t] - lead * factor[t, q]
                parts[j + 1] = parts[j + 1] - lead * line[q]
        if j + 2 < groups:
            weighted = [None] * 8
            for q in range(7, -1, -1):
                rest = line[q]
                for p in range(q + 1, 8):
                    rest = rest - factor[p, q] * weighted[p]
                weighted[q] = rest * scale[q]
            for i in range(j + 2, groups):
                change = spread_lane(parts[i], 8 * j) * weighted[0]
                for q in range(1, 8):
                    change = change + spread_lane(parts[i], 8 * j + q) * weighted[q]
                parts[i] = parts[i] - change
        merged = line[0]
        for q in range(1, 8):
            merged = jnp.where(sub == q, line[q], merged)
        done.append(merged[:, BLOCK:])
    return jnp.concatenate(done, axis=0)


def update_kernel(gathered, *refs):
    if gathered:
        pay, refs = refs[0], refs[1:]
    else:
        gram, coeff_in, refs = refs[0], refs[1], refs[2:]
    moments, (out, joint, mixing) = refs[:-3], refs[-3:]
    members = out.shape[2]
    sub = lax.broadcasted_iota(jnp.int32, (members, members), 0)
    lane = lax.broadcasted_iota(jnp.int32, (members, members), 1)
    identity = jnp.where(sub == lane, 1.0, 0.0)
    if gathered:
        devices, observed = pay.shape[0], pay.shape[1] - PAY_ROWS
        group = max(1, 256 // observed)
        total = identity
        for d in range(0, devices, group):
            block = pay[d : d + group, 0:observed, :].reshape(-1, members)
            total = total + transposed_dot(block, block, None)
        coeff = jnp.zeros((PAY_ROWS, members), jnp.float32)
        for d in range(devices):
            coeff = coeff + pay[d, observed:, :].astype(jnp.float32)
        coeff = jnp.sum(coeff, axis=0, keepdims=True)
    else:
        total = identity + gram[...]
        coeff = coeff_in[...]
    joint[...] = total
    for k in range(members // BLOCK):
        at = k * BLOCK
        below = at + BLOCK
        wide_sub, wide_lane = sub[0:BLOCK, :], lane[0:BLOCK, :]
        inside = jnp.logical_and(wide_lane >= at, wide_lane < below)
        row = joint[at:below, :]
        inverse = inverse_factor_block(row[:, at:below])
        unit = jnp.where(wide_lane == wide_sub + at, 1.0, 0.0)
        row = jnp.dot(
            inverse,
            jnp.where(inside, unit, row),
            precision=HIGHEST,
            preferred_element_type=jnp.float32,
        )
        joint[at:below, :] = row
        if below < members:
            ahead = jnp.where(wide_lane >= below, row, 0.0)
            change = transposed_dot(ahead, row, HIGHEST)
            rest_lane = lane[below:, :]
            inside = jnp.logical_and(rest_lane >= at, rest_lane < below)
            joint[below:, :] = jnp.where(inside, 0.0, joint[below:, :]) - change[below:, :]
    inverse = jnp.where(lane <= sub, joint[...], 0.0)
    half = jnp.sum(inverse * coeff, axis=1, keepdims=True)
    weight = jnp.sum(inverse * half, axis=0, keepdims=True)
    mixing[...] = jnp.transpose((inverse + weight).astype(jnp.bfloat16))

    def blend(anomalies, mean):
        outer, inner = anomalies.shape[0], anomalies.shape[1]
        moved = jnp.dot(
            anomalies.reshape(outer * inner, members), mixing[...], preferred_element_type=jnp.float32
        )
        return (mean + moved.reshape(outer, inner, members)).astype(jnp.bfloat16)

    anomalies, mean = moments[:2]
    field_rows = anomalies.shape[0]

    def step(n, carry):
        for k in range(2):
            at = 4 * n + 2 * k
            out[pl.ds(at, 2)] = blend(anomalies[pl.ds(at, 2)], mean[pl.ds(at, 2)])
        return carry

    lax.fori_loop(0, field_rows // 4, step, 0)
    at = 0
    for n in range(1, len(moments) // 2):
        anomalies, mean = moments[2 * n : 2 * n + 2]
        span = anomalies.shape[1]
        out[field_rows:, at : at + span, :] = blend(anomalies[...], mean[...])
        at += span


def shift(value, axis, by, closed):
    count = lax.axis_size(axis)
    if by > 0:
        pairs = [(i, (i + 1) % count) for i in range(count if closed else count - 1)]
    else:
        pairs = [((i + 1) % count, i) for i in range(count if closed else count - 1)]
    return lax.ppermute(value, axis, pairs)


def gather_rows(block, steps, packed, saturate):
    pieces = []
    for n, (axis, bit) in enumerate(steps):
        count = lax.axis_size(axis)
        if n < len(SPANS):
            block, packed = lax.optimization_barrier((block, packed))
        other = lax.ppermute(block, axis, [(i, i ^ bit) for i in range(count)])
        if n < len(SPANS):
            piece = saturate(n, packed)
        block = jnp.concatenate([block, other], axis=0)
        if n < len(SPANS):
            block, piece = lax.optimization_barrier((block, piece))
            pieces.append(piece)
    return block, pieces + [saturate(n, packed) for n in range(len(pieces), len(SPANS))]


def bits_of(axis, count):
    bits = []
    while (1 << len(bits)) < count:
        bits.append((axis, 1 << len(bits)))
    return bits


def vmem():
    return pl.BlockSpec(memory_space=pltpu.VMEM)


def smem():
    return pl.BlockSpec(memory_space=pltpu.SMEM)


def moments_shape(outer, inner, members):
    return (
        jax.ShapeDtypeStruct((outer, inner, members), jnp.bfloat16),
        jax.ShapeDtypeStruct((outer, inner, 1), jnp.float32),
    )


def shards(
    fields, pore_mask, conv_kernel, conv_bias, read_weight, obs_cells, obs_values, obs_sigma
):
    _, planes, columns, lanes, members = fields.shape
    channels = conv_kernel.shape[1]
    rows = planes * columns
    observed = obs_cells.shape[0]

    left = shift(fields[:, :, -1:], "face", 1, False)
    right = shift(fields[:, :, :1], "face", -1, False)
    low = shift(fields[:, -1:], "cores", 1, True)
    high = shift(fields[:, :1], "cores", -1, True)
    low_sides = jnp.concatenate([left[:, -1:], right[:, -1:]], axis=2)
    high_sides = jnp.concatenate([left[:, :1], right[:, :1]], axis=2)
    corner_low = shift(low_sides, "cores", 1, True)
    corner_high = shift(high_sides, "cores", -1, True)

    selector = tap_selector(planes, columns)
    count = selector.shape[2] // 3
    taps = jnp.dot(
        jnp.transpose(conv_kernel),
        jnp.asarray(selector.reshape(54, -1), jnp.bfloat16),
        preferred_element_type=jnp.float32,
    ).reshape(channels, rows, 3 * count)
    bias = jnp.stack(three_pieces(0.5 * conv_bias), axis=1)
    bias = jnp.broadcast_to(bias[:, None, :], (channels, rows, 3))
    weights = jnp.concatenate(
        [0.5 * taps, bias, jnp.zeros((channels, rows, 13), jnp.float32)], axis=2
    ).astype(jnp.bfloat16)
    by_row = jnp.transpose(weights, (1, 0, 2))
    weights = weights.reshape(channels * rows, 3 * count + 16)
    flat = lambda a: a.reshape(-1, lanes, members)
    starts = [sum(SPANS[:n]) for n in range(len(SPANS))]
    mask = pore_mask.reshape(rows, lanes)
    mask_float = mask.astype(jnp.float32)
    read_half = 0.5 * read_weight
    swap_in = jnp.asarray(swap_matrix(16, 16), jnp.bfloat16)
    swap_out = jnp.asarray(swap_matrix(16, rows), jnp.bfloat16)
    params = pltpu.CompilerParams(vmem_limit_bytes=VMEM_BYTES)
    field_moments = pl.pallas_call(
        moments_kernel,
        out_shape=moments_shape(2 * rows, lanes, members),
        in_specs=[vmem()],
        out_specs=(vmem(), vmem()),
        compiler_params=params,
        name="moments",
    )(flat(fields))
    read_column = read_half[:, None]
    observations = jnp.stack([obs_sigma, obs_values], axis=1)
    packed, pay = pl.pallas_call(
        observe_kernel,
        out_shape=(
            jax.ShapeDtypeStruct((lanes + 2, count, members), jnp.bfloat16),
            jax.ShapeDtypeStruct((observed + PAY_ROWS, members), jnp.bfloat16),
        ),
        in_specs=[vmem()] * 11 + [smem()] * 2,
        out_specs=(vmem(), vmem()),
        scratch_shapes=[pltpu.VMEM((observed, members), jnp.float32)],
        compiler_params=params,
        name="observe",
    )(
        flat(fields), flat(low), flat(high), flat(left), flat(right), flat(corner_low),
        flat(corner_high), by_row, swap_in, read_column, observations, obs_cells, mask,
    )

    def saturate(n, packed):
        span = SPANS[n]
        return pl.pallas_call(
            functools.partial(saturate_kernel, starts[n]),
            out_shape=moments_shape(rows, span, members),
            in_specs=[vmem()] * 4 + [smem()],
            out_specs=(vmem(), vmem()),
            scratch_shapes=[pltpu.VMEM((rows * span, members), jnp.bfloat16)],
            compiler_params=params,
            cost_estimate=pl.CostEstimate(
                flops=2 * 256 * 256 * span * members,
                bytes_accessed=4 * 1024 * 1024,
                transcendentals=channels * rows * span * members,
            ),
            name="saturate",
        )(packed, weights, swap_out, mask_float, read_half)

    core_count, face_count = lax.axis_size("cores"), lax.axis_size("face")
    devices = core_count * face_count
    gathered = devices <= GATHER_DEVICES and devices & (devices - 1) == 0
    if gathered:
        steps = bits_of("face", face_count)[::-1] + bits_of("cores", core_count)[1:]
        steps = steps + bits_of("cores", core_count)[:1]
        block, pieces = gather_rows(pay[None], steps, packed, saturate)
        terms = (block,)
    else:
        part = pay[:observed]
        gram = lax.dot_general(
            part, part, (((0,), (0,)), ((), ())), preferred_element_type=jnp.float32
        )
        coeff = jnp.sum(pay[observed:].astype(jnp.float32), axis=0, keepdims=True)
        terms = lax.psum((gram, coeff), ("cores", "face"))
        pieces = [saturate(n, packed) for n in range(len(SPANS))]
    out = pl.pallas_call(
        functools.partial(update_kernel, gathered),
        out_shape=jax.ShapeDtypeStruct((3 * rows, lanes, members), jnp.bfloat16),
        in_specs=[vmem()] * (len(terms) + 2 + 2 * len(SPANS)),
        out_specs=vmem(),
        scratch_shapes=[
            pltpu.VMEM((members, members), jnp.float32),
            pltpu.VMEM((members, members), jnp.bfloat16),
        ],
        compiler_params=params,
        name="update",
    )(*terms, *field_moments, *(part for piece in pieces for part in piece))
    return out.reshape(3, planes, columns, lanes, members)


def solution(mesh):
    return jax.shard_map(
        shards,
        mesh=mesh,
        in_specs=(
            P(None, "cores", "face", None, None),
            P("cores", "face", None),
            P(),
            P(),
            P(),
            P(("cores", "face")),
            P(("cores", "face")),
            P(("cores", "face")),
        ),
        out_specs=P(None, "cores", "face", None, None),
        check_vma=False,
    )
```

```python
import functools
import math

import jax
import jax.numpy as jnp
import numpy as np
from jax import lax
from jax.experimental import pallas as pl
from jax.experimental.pallas import tpu as pltpu
from jax.sharding import PartitionSpec as P

HIGHEST = lax.Precision.HIGHEST
PAY_ROWS = 16
GATHER_DEVICES = 64
BLOCK = 64
SPANS = (16, 32, 32, 48)
VMEM_BYTES = 8 * 1024 * 1024


def plane_places(planes, columns):
    own = [(f, z + 1, x + 1) for f in range(2) for z in range(planes) for x in range(columns)]
    low = [(f, 0, x + 1) for f in range(2) for x in range(columns)]
    high = [(f, planes + 1, x + 1) for f in range(2) for x in range(columns)]
    left = [(f, z + 1, 0) for f in range(2) for z in range(planes)]
    right = [(f, z + 1, columns + 1) for f in range(2) for z in range(planes)]
    corners = [
        (f, z, x) for z in (0, planes + 1) for f in range(2) for x in (0, columns + 1)
    ]
    return own + low + high + left + right + corners


def tap_selector(planes, columns):
    places = plane_places(planes, columns)
    chosen = np.zeros((54, planes * columns, 3 * len(places)), np.float32)
    for z in range(planes):
        for x in range(columns):
            for n, (f, zz, xx) in enumerate(places):
                a, b = zz - z, xx - x
                if 0 <= a <= 2 and 0 <= b <= 2:
                    for c in range(3):
                        chosen[27 * f + 9 * a + 3 * b + c, z * columns + x, c * len(places) + n] = 1.0
    return chosen


def swap_matrix(outer, inner):
    matrix = np.zeros((outer * inner, outer * inner), np.float32)
    for i in range(outer):
        for j in range(inner):
            matrix[j * outer + i, i * inner + j] = 1.0
    return matrix


def three_pieces(value):
    first = lax.reduce_precision(value, 8, 7)
    second = lax.reduce_precision(value - first, 8, 7)
    third = lax.reduce_precision(value - first - second, 8, 7)
    return first, second, third


def ones_rows(members):
    row_index = lax.broadcasted_iota(jnp.int32, (16, members), 0)
    return jnp.where(row_index < 3, 1.0, 0.0).astype(jnp.bfloat16)


def observe_kernel(
    own, low, high, left, right, corner_low, corner_high, by_row, swap_in, read_column,
    observations, cells, mask, packed, pay_out, pred
):
    lanes, members = own.shape[1], own.shape[2]
    count = packed.shape[1]
    observed = cells.shape[0]
    packed[0] = jnp.zeros((count, members), jnp.bfloat16)
    packed[lanes + 1] = jnp.zeros((count, members), jnp.bfloat16)

    for step in range(lanes // 16):
        at = step * 16
        part = lambda ref: ref[:, pl.ds(at, 16), :]
        sides = (left, right, corner_low, corner_high)
        blocks = (
            part(own),
            jnp.concatenate([part(low), part(high)], axis=0),
            jnp.concatenate([part(side) for side in sides], axis=0),
        )
        for g, block in enumerate(blocks):
            moved = jnp.dot(
                swap_in[...], block.reshape(256, members), preferred_element_type=jnp.float32
            )
            packed[pl.ds(at + 1, 16), 16 * g : 16 * g + 16, :] = (
                moved.astype(jnp.bfloat16).reshape(16, 16, members)
            )

    ones = ones_rows(members)
    read = jnp.broadcast_to(read_column[...], (read_column.shape[0], members))

    def some_cells(step, carry):
        for k in range(16):
            o = step * 16 + k
            cell = cells[o]
            row, y = cell // lanes, cell % lanes
            taps = jnp.concatenate(
                [packed[pl.ds(y, 3)].reshape(3 * count, members), ones], axis=0
            )
            half = jnp.dot(by_row[row], taps, preferred_element_type=jnp.float32)
            total = jnp.sum(read * (half * (1.0 + jnp.tanh(half))), axis=0, keepdims=True)
            found = (0.5 + 0.5 * jnp.tanh(total)) * mask[row, y].astype(jnp.float32)
            pred[pl.ds(o, 1), :] = found.astype(jnp.bfloat16).astype(jnp.float32)
        return carry

    lax.fori_loop(0, observed // 16, some_cells, 0)

    root_count = math.sqrt(members - 1)
    predicted = pred[...]
    center = jnp.mean(predicted, axis=1, keepdims=True)
    inverse_sigma = 1.0 / observations[:, 0:1]
    scaled = (predicted - center) * (inverse_sigma / root_count)
    innovation = (observations[:, 1:2] - center) * inverse_sigma
    coeff = jnp.sum(scaled * innovation, axis=0, keepdims=True) / root_count
    first = coeff.astype(jnp.bfloat16).astype(jnp.float32)
    second = (coeff - first).astype(jnp.bfloat16).astype(jnp.float32)
    third = coeff - first - second
    index = lax.broadcasted_iota(jnp.int32, (PAY_ROWS, members), 0)
    tail = jnp.where(index == 0, first, jnp.where(index == 1, second, jnp.where(index == 2, third, 0.0)))
    pay_out[0:observed, :] = scaled.astype(jnp.bfloat16)
    pay_out[observed : observed + PAY_ROWS, :] = tail.astype(jnp.bfloat16)


def saturate_kernel(
    start, packed, weights, swap_out, mask, read_half, anomaly_out, mean_out, sat_rows
):
    rows, span, members = anomaly_out.shape
    count = packed.shape[1]
    channels = read_half.shape[0]
    ones = ones_rows(members)
    lane_index = lax.broadcasted_iota(jnp.int32, mask.shape, 1)

    def some_rows(step, carry):
        found = []
        for k in range(8):
            y = start + step * 8 + k
            taps = jnp.concatenate(
                [packed[pl.ds(y, 3)].reshape(3 * count, members), ones], axis=0
            )
            half = jnp.dot(weights[...], taps, preferred_element_type=jnp.float32)
            total = jnp.zeros((rows, members), jnp.float32)
            for c in range(channels):
                part = half[rows * c : rows * c + rows]
                total = total + read_half[c] * (part * (1.0 + jnp.tanh(part)))
            here = jnp.sum(jnp.where(lane_index == y, mask[...], 0.0), axis=1, keepdims=True)
            found.append(here * (0.5 + 0.5 * jnp.tanh(total)))
        at = pl.multiple_of(step * 8 * rows, 8 * rows)
        sat_rows[pl.ds(at, 8 * rows), :] = jnp.concatenate(found, axis=0).astype(jnp.bfloat16)
        return carry

    lax.fori_loop(0, span // 8, some_rows, 0)
    for n in range(span // 16):
        block = sat_rows[n * 16 * rows : (n + 1) * 16 * rows, :]
        moved = jnp.dot(swap_out[...], block, preferred_element_type=jnp.float32)
        mean = jnp.mean(moved, axis=1, keepdims=True)
        anomalies = (moved - mean).astype(jnp.bfloat16)
        anomaly_out[:, n * 16 : n * 16 + 16, :] = anomalies.reshape(rows, 16, members)
        mean_out[:, n * 16 : n * 16 + 16, :] = mean.reshape(rows, 16, 1)


def moments_kernel(fields, anomaly_out, mean_out):
    def step(n, carry):
        state = fields[pl.ds(2 * n, 2)].astype(jnp.float32)
        mean = jnp.mean(state, axis=2, keepdims=True)
        anomaly_out[pl.ds(2 * n, 2)] = (state - mean).astype(jnp.bfloat16)
        mean_out[pl.ds(2 * n, 2)] = mean
        return carry

    lax.fori_loop(0, fields.shape[0] // 2, step, 0)


def transposed_dot(a, b, precision):
    return lax.dot_general(
        a, b, (((0,), (0,)), ((), ())), preferred_element_type=jnp.float32, precision=precision
    )


def spread_row(part, p):
    return jnp.broadcast_to(part[p : p + 1, :], part.shape)


def spread_lane(part, q):
    return jnp.broadcast_to(part[:, q : q + 1], part.shape)


def inverse_factor_block(block):
    lane = lax.broadcasted_iota(jnp.int32, (8, 2 * BLOCK), 1)
    sub = lax.broadcasted_iota(jnp.int32, (8, 2 * BLOCK), 0)
    groups = BLOCK // 8
    parts = []
    for i in range(groups):
        unit = jnp.where(lane == sub + (BLOCK + 8 * i), 1.0, 0.0)
        known = jnp.concatenate(
            [block[8 * i : 8 * i + 8, :], jnp.zeros((8, BLOCK), jnp.float32)], axis=1
        )
        parts.append(known + unit)
    done = []
    upcoming = [spread_lane(parts[0], q) for q in range(8)]
    for j in range(groups):
        corner = upcoming
        entry = {(p, q): spread_row(corner[q], p) for q in range(8) for p in range(q, 8)}
        line = [spread_row(parts[j], p) for p in range(8)]
        near = j + 1 < groups
        if near:
            beside = [spread_lane(parts[j + 1], 8 * j + q) for q in range(8)]
            upcoming = [spread_lane(parts[j + 1], 8 * j + 8 + q) for q in range(8)]
        factor, scale = {}, []
        for q in range(8):
            root = lax.rsqrt(entry[q, q])
            scale.append(root)
            line[q] = line[q] * root
            for p in range(q + 1, 8):
                factor[p, q] = entry[p, q] * root
            for t in range(q + 1, 8):
                for p in range(t, 8):
                    entry[p, t] = entry[p, t] - factor[p, q] * factor[t, q]
            for p in range(q + 1, 8):
                line[p] = line[p] - factor[p, q] * line[q]
            if near:
                lead = beside[q] * root
                upcoming = [
                    column - lead * spread_row(lead, p) for p, column in enumerate(upcoming)
                ]
                for t in range(q + 1, 8):
                    beside[t] = beside[t] - lead * factor[t, q]
                parts[j + 1] = parts[j + 1] - lead * line[q]
        if j + 2 < groups:
            weighted = [None] * 8
            for q in range(7, -1, -1):
                rest = line[q]
                for p in range(q + 1, 8):
                    rest = rest - factor[p, q] * weighted[p]
                weighted[q] = rest * scale[q]
            for i in range(j + 2, groups):
                change = spread_lane(parts[i], 8 * j) * weighted[0]
                for q in range(1, 8):
                    change = change + spread_lane(parts[i], 8 * j + q) * weighted[q]
                parts[i] = parts[i] - change
        merged = line[0]
        for q in range(1, 8):
            merged = jnp.where(sub == q, line[q], merged)
        done.append(merged[:, BLOCK:])
    return jnp.concatenate(done, axis=0)


def update_kernel(gathered, *refs):
    if gathered:
        pay, refs = refs[0], refs[1:]
    else:
        gram, coeff_in, refs = refs[0], refs[1], refs[2:]
    moments, (out, joint, mixing) = refs[:-3], refs[-3:]
    members = out.shape[2]
    sub = lax.broadcasted_iota(jnp.int32, (members, members), 0)
    lane = lax.broadcasted_iota(jnp.int32, (members, members), 1)
    identity = jnp.where(sub == lane, 1.0, 0.0)
    if gathered:
        devices, observed = pay.shape[0], pay.shape[1] - PAY_ROWS
        group = max(1, 256 // observed)
        total = identity
        for d in range(0, devices, group):
            block = pay[d : d + group, 0:observed, :].reshape(-1, members)
            total = total + transposed_dot(block, block, None)
        coeff = jnp.zeros((PAY_ROWS, members), jnp.float32)
        for d in range(devices):
            coeff = coeff + pay[d, observed:, :].astype(jnp.float32)
        coeff = jnp.sum(coeff, axis=0, keepdims=True)
    else:
        total = identity + gram[...]
        coeff = coeff_in[...]
    joint[...] = total
    for k in range(members // BLOCK):
        at = k * BLOCK
        below = at + BLOCK
        wide_sub, wide_lane = sub[0:BLOCK, :], lane[0:BLOCK, :]
        inside = jnp.logical_and(wide_lane >= at, wide_lane < below)
        row = joint[at:below, :]
        inverse = inverse_factor_block(row[:, at:below])
        unit = jnp.where(wide_lane == wide_sub + at, 1.0, 0.0)
        row = jnp.dot(
            inverse,
            jnp.where(inside, unit, row),
            precision=HIGHEST,
            preferred_element_type=jnp.float32,
        )
        joint[at:below, :] = row
        if below < members:
            ahead = jnp.where(wide_lane >= below, row, 0.0)
            change = transposed_dot(ahead, row, HIGHEST)
            rest_lane = lane[below:, :]
            inside = jnp.logical_and(rest_lane >= at, rest_lane < below)
            joint[below:, :] = jnp.where(inside, 0.0, joint[below:, :]) - change[below:, :]
    inverse = jnp.where(lane <= sub, joint[...], 0.0)
    half = jnp.sum(inverse * coeff, axis=1, keepdims=True)
    weight = jnp.sum(inverse * half, axis=0, keepdims=True)
    mixing[...] = jnp.transpose((inverse + weight).astype(jnp.bfloat16))

    def blend(anomalies, mean):
        outer, inner = anomalies.shape[0], anomalies.shape[1]
        moved = jnp.dot(
            anomalies.reshape(outer * inner, members), mixing[...], preferred_element_type=jnp.float32
        )
        return (mean + moved.reshape(outer, inner, members)).astype(jnp.bfloat16)

    anomalies, mean = moments[:2]
    field_rows = anomalies.shape[0]

    def step(n, carry):
        for k in range(2):
            at = 4 * n + 2 * k
            out[pl.ds(at, 2)] = blend(anomalies[pl.ds(at, 2)], mean[pl.ds(at, 2)])
        return carry

    lax.fori_loop(0, field_rows // 4, step, 0)
    at = 0
    for n in range(1, len(moments) // 2):
        anomalies, mean = moments[2 * n : 2 * n + 2]
        span = anomalies.shape[1]
        out[field_rows:, at : at + span, :] = blend(anomalies[...], mean[...])
        at += span


def shift(value, axis, by, closed):
    count = lax.axis_size(axis)
    if by > 0:
        pairs = [(i, (i + 1) % count) for i in range(count if closed else count - 1)]
    else:
        pairs = [((i + 1) % count, i) for i in range(count if closed else count - 1)]
    return lax.ppermute(value, axis, pairs)


def gather_rows(block, steps, packed, saturate):
    pieces = []
    for n, (axis, bit) in enumerate(steps):
        count = lax.axis_size(axis)
        if n < len(SPANS):
            block, packed = lax.optimization_barrier((block, packed))
        other = lax.ppermute(block, axis, [(i, i ^ bit) for i in range(count)])
        if n < len(SPANS):
            piece = saturate(n, packed)
        block = jnp.concatenate([block, other], axis=0)
        if n < len(SPANS):
            block, piece = lax.optimization_barrier((block, piece))
            pieces.append(piece)
    return block, pieces + [saturate(n, packed) for n in range(len(pieces), len(SPANS))]


def bits_of(axis, count):
    bits = []
    while (1 << len(bits)) < count:
        bits.append((axis, 1 << len(bits)))
    return bits


def vmem():
    return pl.BlockSpec(memory_space=pltpu.VMEM)


def smem():
    return pl.BlockSpec(memory_space=pltpu.SMEM)


def moments_shape(outer, inner, members):
    return (
        jax.ShapeDtypeStruct((outer, inner, members), jnp.bfloat16),
        jax.ShapeDtypeStruct((outer, inner, 1), jnp.float32),
    )


def shards(
    fields, pore_mask, conv_kernel, conv_bias, read_weight, obs_cells, obs_values, obs_sigma
):
    _, planes, columns, lanes, members = fields.shape
    channels = conv_kernel.shape[1]
    rows = planes * columns
    observed = obs_cells.shape[0]

    left = shift(fields[:, :, -1:], "face", 1, False)
    right = shift(fields[:, :, :1], "face", -1, False)
    low = shift(fields[:, -1:], "cores", 1, True)
    high = shift(fields[:, :1], "cores", -1, True)
    low_sides = jnp.concatenate([left[:, -1:], right[:, -1:]], axis=2)
    high_sides = jnp.concatenate([left[:, :1], right[:, :1]], axis=2)
    corner_low = shift(low_sides, "cores", 1, True)
    corner_high = shift(high_sides, "cores", -1, True)

    selector = tap_selector(planes, columns)
    count = selector.shape[2] // 3
    taps = jnp.dot(
        jnp.transpose(conv_kernel),
        jnp.asarray(selector.reshape(54, -1), jnp.bfloat16),
        preferred_element_type=jnp.float32,
    ).reshape(channels, rows, 3 * count)
    bias = jnp.stack(three_pieces(0.5 * conv_bias), axis=1)
    bias = jnp.broadcast_to(bias[:, None, :], (channels, rows, 3))
    weights = jnp.concatenate(
        [0.5 * taps, bias, jnp.zeros((channels, rows, 13), jnp.float32)], axis=2
    ).astype(jnp.bfloat16)
    by_row = jnp.transpose(weights, (1, 0, 2))
    weights = weights.reshape(channels * rows, 3 * count + 16)
    flat = lambda a: a.reshape(-1, lanes, members)
    starts = [sum(SPANS[:n]) for n in range(len(SPANS))]
    mask = pore_mask.reshape(rows, lanes)
    mask_float = mask.astype(jnp.float32)
    read_half = 0.5 * read_weight
    swap_in = jnp.asarray(swap_matrix(16, 16), jnp.bfloat16)
    swap_out = jnp.asarray(swap_matrix(16, rows), jnp.bfloat16)
    params = pltpu.CompilerParams(vmem_limit_bytes=VMEM_BYTES)
    field_moments = pl.pallas_call(
        moments_kernel,
        out_shape=moments_shape(2 * rows, lanes, members),
        in_specs=[vmem()],
        out_specs=(vmem(), vmem()),
        compiler_params=params,
        name="moments",
    )(flat(fields))
    read_column = read_half[:, None]
    observations = jnp.stack([obs_sigma, obs_values], axis=1)
    packed, pay = pl.pallas_call(
        observe_kernel,
        out_shape=(
            jax.ShapeDtypeStruct((lanes + 2, count, members), jnp.bfloat16),
            jax.ShapeDtypeStruct((observed + PAY_ROWS, members), jnp.bfloat16),
        ),
        in_specs=[vmem()] * 11 + [smem()] * 2,
        out_specs=(vmem(), vmem()),
        scratch_shapes=[pltpu.VMEM((observed, members), jnp.float32)],
        compiler_params=params,
        name="observe",
    )(
        flat(fields), flat(low), flat(high), flat(left), flat(right), flat(corner_low),
        flat(corner_high), by_row, swap_in, read_column, observations, obs_cells, mask,
    )

    def saturate(n, packed):
        span = SPANS[n]
        return pl.pallas_call(
            functools.partial(saturate_kernel, starts[n]),
            out_shape=moments_shape(rows, span, members),
            in_specs=[vmem()] * 4 + [smem()],
            out_specs=(vmem(), vmem()),
            scratch_shapes=[pltpu.VMEM((rows * span, members), jnp.bfloat16)],
            compiler_params=params,
            cost_estimate=pl.CostEstimate(
                flops=2 * 256 * 256 * span * members,
                bytes_accessed=4 * 1024 * 1024,
                transcendentals=channels * rows * span * members,
            ),
            name="saturate",
        )(packed, weights, swap_out, mask_float, read_half)

    core_count, face_count = lax.axis_size("cores"), lax.axis_size("face")
    devices = core_count * face_count
    gathered = devices <= GATHER_DEVICES and devices & (devices - 1) == 0
    if gathered:
        steps = bits_of("face", face_count)[::-1] + bits_of("cores", core_count)[1:]
        steps = steps + bits_of("cores", core_count)[:1]
        block, pieces = gather_rows(pay[None], steps, packed, saturate)
        terms = (block,)
    else:
        part = pay[:observed]
        gram = lax.dot_general(
            part, part, (((0,), (0,)), ((), ())), preferred_element_type=jnp.float32
        )
        coeff = jnp.sum(pay[observed:].astype(jnp.float32), axis=0, keepdims=True)
        terms = lax.psum((gram, coeff), ("cores", "face"))
        pieces = [saturate(n, packed) for n in range(len(SPANS))]
    out = pl.pallas_call(
        functools.partial(update_kernel, gathered),
        out_shape=jax.ShapeDtypeStruct((3 * rows, lanes, members), jnp.bfloat16),
        in_specs=[vmem()] * (len(terms) + 2 + 2 * len(SPANS)),
        out_specs=vmem(),
        scratch_shapes=[
            pltpu.VMEM((members, members), jnp.float32),
            pltpu.VMEM((members, members), jnp.bfloat16),
        ],
        compiler_params=params,
        name="update",
    )(*terms, *field_moments, *(part for piece in pieces for part in piece))
    return out.reshape(3, planes, columns, lanes, members)


def solution(mesh):
    return jax.shard_map(
        shards,
        mesh=mesh,
        in_specs=(
            P(None, "cores", "face", None, None),
            P("cores", "face", None),
            P(),
            P(),
            P(),
            P(("cores", "face")),
            P(("cores", "face")),
            P(("cores", "face")),
        ),
        out_specs=P(None, "cores", "face", None, None),
        check_vma=False,
    )
```

```python
import functools
import math

import jax
import jax.numpy as jnp
import numpy as np
from jax import lax
from jax.experimental import pallas as pl
from jax.experimental.pallas import tpu as pltpu
from jax.sharding import PartitionSpec as P

HIGHEST = lax.Precision.HIGHEST
PAY_ROWS = 16
GATHER_DEVICES = 64
BLOCK = 128
SPANS = (16, 16, 48, 48)
VMEM_BYTES = 8 * 1024 * 1024


def plane_places(planes, columns):
    own = [(f, z + 1, x + 1) for f in range(2) for z in range(planes) for x in range(columns)]
    low = [(f, 0, x + 1) for f in range(2) for x in range(columns)]
    high = [(f, planes + 1, x + 1) for f in range(2) for x in range(columns)]
    left = [(f, z + 1, 0) for f in range(2) for z in range(planes)]
    right = [(f, z + 1, columns + 1) for f in range(2) for z in range(planes)]
    corners = [
        (f, z, x) for z in (0, planes + 1) for f in range(2) for x in (0, columns + 1)
    ]
    return own + low + high + left + right + corners


def tap_selector(planes, columns):
    places = plane_places(planes, columns)
    chosen = np.zeros((54, planes * columns, 3 * len(places)), np.float32)
    for z in range(planes):
        for x in range(columns):
            for n, (f, zz, xx) in enumerate(places):
                a, b = zz - z, xx - x
                if 0 <= a <= 2 and 0 <= b <= 2:
                    for c in range(3):
                        chosen[27 * f + 9 * a + 3 * b + c, z * columns + x, c * len(places) + n] = 1.0
    return chosen


def swap_matrix(outer, inner):
    matrix = np.zeros((outer * inner, outer * inner), np.float32)
    for i in range(outer):
        for j in range(inner):
            matrix[j * outer + i, i * inner + j] = 1.0
    return matrix


def three_pieces(value):
    first = lax.reduce_precision(value, 8, 7)
    second = lax.reduce_precision(value - first, 8, 7)
    third = lax.reduce_precision(value - first - second, 8, 7)
    return first, second, third


def ones_rows(members):
    row_index = lax.broadcasted_iota(jnp.int32, (16, members), 0)
    return jnp.where(row_index < 3, 1.0, 0.0).astype(jnp.bfloat16)


def observe_kernel(
    own, low, high, left, right, corner_low, corner_high, by_row, swap_in, read_column,
    observations, cells, mask, packed, pay_out, pred
):
    lanes, members = own.shape[1], own.shape[2]
    count = packed.shape[1]
    observed = cells.shape[0]
    packed[0] = jnp.zeros((count, members), jnp.bfloat16)
    packed[lanes + 1] = jnp.zeros((count, members), jnp.bfloat16)

    for step in range(lanes // 16):
        at = step * 16
        part = lambda ref: ref[:, pl.ds(at, 16), :]
        sides = (left, right, corner_low, corner_high)
        blocks = (
            part(own),
            jnp.concatenate([part(low), part(high)], axis=0),
            jnp.concatenate([part(side) for side in sides], axis=0),
        )
        for g, block in enumerate(blocks):
            moved = jnp.dot(
                swap_in[...], block.reshape(256, members), preferred_element_type=jnp.float32
            )
            packed[pl.ds(at + 1, 16), 16 * g : 16 * g + 16, :] = (
                moved.astype(jnp.bfloat16).reshape(16, 16, members)
            )

    ones = ones_rows(members)
    read = jnp.broadcast_to(read_column[...], (read_column.shape[0], members))

    def some_cells(step, carry):
        for k in range(16):
            o = step * 16 + k
            cell = cells[o]
            row, y = cell // lanes, cell % lanes
            taps = jnp.concatenate(
                [packed[pl.ds(y, 3)].reshape(3 * count, members), ones], axis=0
            )
            half = jnp.dot(by_row[row], taps, preferred_element_type=jnp.float32)
            total = jnp.sum(read * (half * (1.0 + jnp.tanh(half))), axis=0, keepdims=True)
            found = (0.5 + 0.5 * jnp.tanh(total)) * mask[row, y].astype(jnp.float32)
            pred[pl.ds(o, 1), :] = found.astype(jnp.bfloat16).astype(jnp.float32)
        return carry

    lax.fori_loop(0, observed // 16, some_cells, 0)

    root_count = math.sqrt(members - 1)
    predicted = pred[...]
    center = jnp.mean(predicted, axis=1, keepdims=True)
    inverse_sigma = 1.0 / observations[:, 0:1]
    scaled = (predicted - center) * (inverse_sigma / root_count)
    innovation = (observations[:, 1:2] - center) * inverse_sigma
    coeff = jnp.sum(scaled * innovation, axis=0, keepdims=True) / root_count
    first = coeff.astype(jnp.bfloat16).astype(jnp.float32)
    second = (coeff - first).astype(jnp.bfloat16).astype(jnp.float32)
    third = coeff - first - second
    index = lax.broadcasted_iota(jnp.int32, (PAY_ROWS, members), 0)
    tail = jnp.where(index == 0, first, jnp.where(index == 1, second, jnp.where(index == 2, third, 0.0)))
    pay_out[0:observed, :] = scaled.astype(jnp.bfloat16)
    pay_out[observed : observed + PAY_ROWS, :] = tail.astype(jnp.bfloat16)


def saturate_kernel(
    start, packed, weights, swap_out, mask, read_half, anomaly_out, mean_out, sat_rows
):
    rows, span, members = anomaly_out.shape
    count = packed.shape[1]
    channels = read_half.shape[0]
    ones = ones_rows(members)
    lane_index = lax.broadcasted_iota(jnp.int32, mask.shape, 1)

    def some_rows(step, carry):
        found = []
        for k in range(8):
            y = start + step * 8 + k
            taps = jnp.concatenate(
                [packed[pl.ds(y, 3)].reshape(3 * count, members), ones], axis=0
            )
            half = jnp.dot(weights[...], taps, preferred_element_type=jnp.float32)
            total = jnp.zeros((rows, members), jnp.float32)
            for c in range(channels):
                part = half[rows * c : rows * c + rows]
                total = total + read_half[c] * (part * (1.0 + jnp.tanh(part)))
            here = jnp.sum(jnp.where(lane_index == y, mask[...], 0.0), axis=1, keepdims=True)
            found.append(here * (0.5 + 0.5 * jnp.tanh(total)))
        at = pl.multiple_of(step * 8 * rows, 8 * rows)
        sat_rows[pl.ds(at, 8 * rows), :] = jnp.concatenate(found, axis=0).astype(jnp.bfloat16)
        return carry

    lax.fori_loop(0, span // 8, some_rows, 0)
    for n in range(span // 16):
        block = sat_rows[n * 16 * rows : (n + 1) * 16 * rows, :]
        moved = jnp.dot(swap_out[...], block, preferred_element_type=jnp.float32)
        mean = jnp.mean(moved, axis=1, keepdims=True)
        anomalies = (moved - mean).astype(jnp.bfloat16)
        anomaly_out[:, n * 16 : n * 16 + 16, :] = anomalies.reshape(rows, 16, members)
        mean_out[:, n * 16 : n * 16 + 16, :] = mean.reshape(rows, 16, 1)


def moments_kernel(fields, anomaly_out, mean_out):
    def step(n, carry):
        state = fields[pl.ds(2 * n, 2)].astype(jnp.float32)
        mean = jnp.mean(state, axis=2, keepdims=True)
        anomaly_out[pl.ds(2 * n, 2)] = (state - mean).astype(jnp.bfloat16)
        mean_out[pl.ds(2 * n, 2)] = mean
        return carry

    lax.fori_loop(0, fields.shape[0] // 2, step, 0)


def transposed_dot(a, b, precision):
    return lax.dot_general(
        a, b, (((0,), (0,)), ((), ())), preferred_element_type=jnp.float32, precision=precision
    )


def spread_row(part, p):
    return jnp.broadcast_to(part[p : p + 1, :], part.shape)


def spread_lane(part, q):
    return jnp.broadcast_to(part[:, q : q + 1], part.shape)


def inverse_factor_block(block):
    lane = lax.broadcasted_iota(jnp.int32, (8, 2 * BLOCK), 1)
    sub = lax.broadcasted_iota(jnp.int32, (8, 2 * BLOCK), 0)
    groups = BLOCK // 8
    parts = []
    for i in range(groups):
        unit = jnp.where(lane == sub + (BLOCK + 8 * i), 1.0, 0.0)
        known = jnp.concatenate(
            [block[8 * i : 8 * i + 8, :], jnp.zeros((8, BLOCK), jnp.float32)], axis=1
        )
        parts.append(known + unit)
    done = []
    upcoming = [spread_lane(parts[0], q) for q in range(8)]
    for j in range(groups):
        corner = upcoming
        entry = {(p, q): spread_row(corner[q], p) for q in range(8) for p in range(q, 8)}
        line = [spread_row(parts[j], p) for p in range(8)]
        near = j + 1 < groups
        if near:
            beside = [spread_lane(parts[j + 1], 8 * j + q) for q in range(8)]
            upcoming = [spread_lane(parts[j + 1], 8 * j + 8 + q) for q in range(8)]
        factor, scale = {}, []
        for q in range(8):
            root = lax.rsqrt(entry[q, q])
            scale.append(root)
            line[q] = line[q] * root
            for p in range(q + 1, 8):
                factor[p, q] = entry[p, q] * root
            for t in range(q + 1, 8):
                for p in range(t, 8):
                    entry[p, t] = entry[p, t] - factor[p, q] * factor[t, q]
            for p in range(q + 1, 8):
                line[p] = line[p] - factor[p, q] * line[q]
            if near:
                lead = beside[q] * root
                upcoming = [
                    column - lead * spread_row(lead, p) for p, column in enumerate(upcoming)
                ]
                for t in range(q + 1, 8):
                    beside[t] = beside[t] - lead * factor[t, q]
                parts[j + 1] = parts[j + 1] - lead * line[q]
        if j + 2 < groups:
            weighted = [None] * 8
            for q in range(7, -1, -1):
                rest = line[q]
                for p in range(q + 1, 8):
                    rest = rest - factor[p, q] * weighted[p]
                weighted[q] = rest * scale[q]
            for i in range(j + 2, groups):
                change = spread_lane(parts[i], 8 * j) * weighted[0]
                for q in range(1, 8):
                    change = change + spread_lane(parts[i], 8 * j + q) * weighted[q]
                parts[i] = parts[i] - change
        merged = line[0]
        for q in range(1, 8):
            merged = jnp.where(sub == q, line[q], merged)
        done.append(merged[:, BLOCK:])
    return jnp.concatenate(done, axis=0)


def update_kernel(gathered, *refs):
    if gathered:
        pay, refs = refs[0], refs[1:]
    else:
        gram, coeff_in, refs = refs[0], refs[1], refs[2:]
    moments, (out, joint, mixing) = refs[:-3], refs[-3:]
    members = out.shape[2]
    sub = lax.broadcasted_iota(jnp.int32, (members, members), 0)
    lane = lax.broadcasted_iota(jnp.int32, (members, members), 1)
    identity = jnp.where(sub == lane, 1.0, 0.0)
    if gathered:
        devices, observed = pay.shape[0], pay.shape[1] - PAY_ROWS
        group = max(1, 256 // observed)
        total = identity
        for d in range(0, devices, group):
            block = pay[d : d + group, 0:observed, :].reshape(-1, members)
            total = total + transposed_dot(block, block, None)
        coeff = jnp.zeros((PAY_ROWS, members), jnp.float32)
        for d in range(devices):
            coeff = coeff + pay[d, observed:, :].astype(jnp.float32)
        coeff = jnp.sum(coeff, axis=0, keepdims=True)
    else:
        total = identity + gram[...]
        coeff = coeff_in[...]
    joint[...] = total
    for k in range(members // BLOCK):
        at = k * BLOCK
        below = at + BLOCK
        wide_sub, wide_lane = sub[0:BLOCK, :], lane[0:BLOCK, :]
        inside = jnp.logical_and(wide_lane >= at, wide_lane < below)
        row = joint[at:below, :]
        inverse = inverse_factor_block(row[:, at:below])
        unit = jnp.where(wide_lane == wide_sub + at, 1.0, 0.0)
        row = jnp.dot(
            inverse,
            jnp.where(inside, unit, row),
            precision=HIGHEST,
            preferred_element_type=jnp.float32,
        )
        joint[at:below, :] = row
        if below < members:
            ahead = jnp.where(wide_lane >= below, row, 0.0)
            change = transposed_dot(ahead, row, HIGHEST)
            rest_lane = lane[below:, :]
            inside = jnp.logical_and(rest_lane >= at, rest_lane < below)
            joint[below:, :] = jnp.where(inside, 0.0, joint[below:, :]) - change[below:, :]
    inverse = jnp.where(lane <= sub, joint[...], 0.0)
    half = jnp.sum(inverse * coeff, axis=1, keepdims=True)
    weight = jnp.sum(inverse * half, axis=0, keepdims=True)
    mixing[...] = jnp.transpose((inverse + weight).astype(jnp.bfloat16))

    def blend(anomalies, mean):
        outer, inner = anomalies.shape[0], anomalies.shape[1]
        moved = jnp.dot(
            anomalies.reshape(outer * inner, members), mixing[...], preferred_element_type=jnp.float32
        )
        return (mean + moved.reshape(outer, inner, members)).astype(jnp.bfloat16)

    anomalies, mean = moments[:2]
    field_rows = anomalies.shape[0]

    def step(n, carry):
        for k in range(2):
            at = 4 * n + 2 * k
            out[pl.ds(at, 2)] = blend(anomalies[pl.ds(at, 2)], mean[pl.ds(at, 2)])
        return carry

    lax.fori_loop(0, field_rows // 4, step, 0)
    at = 0
    for n in range(1, len(moments) // 2):
        anomalies, mean = moments[2 * n : 2 * n + 2]
        span = anomalies.shape[1]
        out[field_rows:, at : at + span, :] = blend(anomalies[...], mean[...])
        at += span


def shift(value, axis, by, closed):
    count = lax.axis_size(axis)
    if by > 0:
        pairs = [(i, (i + 1) % count) for i in range(count if closed else count - 1)]
    else:
        pairs = [((i + 1) % count, i) for i in range(count if closed else count - 1)]
    return lax.ppermute(value, axis, pairs)


def gather_rows(block, steps, packed, saturate):
    pieces = []
    for n, (axis, bit) in enumerate(steps):
        count = lax.axis_size(axis)
        if n < len(SPANS):
            block, packed = lax.optimization_barrier((block, packed))
        other = lax.ppermute(block, axis, [(i, i ^ bit) for i in range(count)])
        if n < len(SPANS):
            piece = saturate(n, packed)
        block = jnp.concatenate([block, other], axis=0)
        if n < len(SPANS):
            block, piece = lax.optimization_barrier((block, piece))
            pieces.append(piece)
    return block, pieces + [saturate(n, packed) for n in range(len(pieces), len(SPANS))]


def bits_of(axis, count):
    bits = []
    while (1 << len(bits)) < count:
        bits.append((axis, 1 << len(bits)))
    return bits


def vmem():
    return pl.BlockSpec(memory_space=pltpu.VMEM)


def smem():
    return pl.BlockSpec(memory_space=pltpu.SMEM)


def moments_shape(outer, inner, members):
    return (
        jax.ShapeDtypeStruct((outer, inner, members), jnp.bfloat16),
        jax.ShapeDtypeStruct((outer, inner, 1), jnp.float32),
    )


def shards(
    fields, pore_mask, conv_kernel, conv_bias, read_weight, obs_cells, obs_values, obs_sigma
):
    _, planes, columns, lanes, members = fields.shape
    channels = conv_kernel.shape[1]
    rows = planes * columns
    observed = obs_cells.shape[0]

    left = shift(fields[:, :, -1:], "face", 1, False)
    right = shift(fields[:, :, :1], "face", -1, False)
    low = shift(fields[:, -1:], "cores", 1, True)
    high = shift(fields[:, :1], "cores", -1, True)
    low_sides = jnp.concatenate([left[:, -1:], right[:, -1:]], axis=2)
    high_sides = jnp.concatenate([left[:, :1], right[:, :1]], axis=2)
    corner_low = shift(low_sides, "cores", 1, True)
    corner_high = shift(high_sides, "cores", -1, True)

    selector = tap_selector(planes, columns)
    count = selector.shape[2] // 3
    taps = jnp.dot(
        jnp.transpose(conv_kernel),
        jnp.asarray(selector.reshape(54, -1), jnp.bfloat16),
        preferred_element_type=jnp.float32,
    ).reshape(channels, rows, 3 * count)
    bias = jnp.stack(three_pieces(0.5 * conv_bias), axis=1)
    bias = jnp.broadcast_to(bias[:, None, :], (channels, rows, 3))
    weights = jnp.concatenate(
        [0.5 * taps, bias, jnp.zeros((channels, rows, 13), jnp.float32)], axis=2
    ).astype(jnp.bfloat16)
    by_row = jnp.transpose(weights, (1, 0, 2))
    weights = weights.reshape(channels * rows, 3 * count + 16)
    flat = lambda a: a.reshape(-1, lanes, members)
    starts = [sum(SPANS[:n]) for n in range(len(SPANS))]
    mask = pore_mask.reshape(rows, lanes)
    mask_float = mask.astype(jnp.float32)
    read_half = 0.5 * read_weight
    swap_in = jnp.asarray(swap_matrix(16, 16), jnp.bfloat16)
    swap_out = jnp.asarray(swap_matrix(16, rows), jnp.bfloat16)
    params = pltpu.CompilerParams(vmem_limit_bytes=VMEM_BYTES)
    field_moments = pl.pallas_call(
        moments_kernel,
        out_shape=moments_shape(2 * rows, lanes, members),
        in_specs=[vmem()],
        out_specs=(vmem(), vmem()),
        compiler_params=params,
        name="moments",
    )(flat(fields))
    read_column = read_half[:, None]
    observations = jnp.stack([obs_sigma, obs_values], axis=1)
    packed, pay = pl.pallas_call(
        observe_kernel,
        out_shape=(
            jax.ShapeDtypeStruct((lanes + 2, count, members), jnp.bfloat16),
            jax.ShapeDtypeStruct((observed + PAY_ROWS, members), jnp.bfloat16),
        ),
        in_specs=[vmem()] * 11 + [smem()] * 2,
        out_specs=(vmem(), vmem()),
        scratch_shapes=[pltpu.VMEM((observed, members), jnp.float32)],
        compiler_params=params,
        name="observe",
    )(
        flat(fields), flat(low), flat(high), flat(left), flat(right), flat(corner_low),
        flat(corner_high), by_row, swap_in, read_column, observations, obs_cells, mask,
    )

    def saturate(n, packed):
        span = SPANS[n]
        return pl.pallas_call(
            functools.partial(saturate_kernel, starts[n]),
            out_shape=moments_shape(rows, span, members),
            in_specs=[vmem()] * 4 + [smem()],
            out_specs=(vmem(), vmem()),
            scratch_shapes=[pltpu.VMEM((rows * span, members), jnp.bfloat16)],
            compiler_params=params,
            cost_estimate=pl.CostEstimate(
                flops=2 * 256 * 256 * span * members,
                bytes_accessed=4 * 1024 * 1024,
                transcendentals=channels * rows * span * members,
            ),
            name="saturate",
        )(packed, weights, swap_out, mask_float, read_half)

    core_count, face_count = lax.axis_size("cores"), lax.axis_size("face")
    devices = core_count * face_count
    gathered = devices <= GATHER_DEVICES and devices & (devices - 1) == 0
    if gathered:
        steps = bits_of("face", face_count)[::-1] + bits_of("cores", core_count)[1:]
        steps = steps + bits_of("cores", core_count)[:1]
        block, pieces = gather_rows(pay[None], steps, packed, saturate)
        terms = (block,)
    else:
        part = pay[:observed]
        gram = lax.dot_general(
            part, part, (((0,), (0,)), ((), ())), preferred_element_type=jnp.float32
        )
        coeff = jnp.sum(pay[observed:].astype(jnp.float32), axis=0, keepdims=True)
        terms = lax.psum((gram, coeff), ("cores", "face"))
        pieces = [saturate(n, packed) for n in range(len(SPANS))]
    out = pl.pallas_call(
        functools.partial(update_kernel, gathered),
        out_shape=jax.ShapeDtypeStruct((3 * rows, lanes, members), jnp.bfloat16),
        in_specs=[vmem()] * (len(terms) + 2 + 2 * len(SPANS)),
        out_specs=vmem(),
        scratch_shapes=[
            pltpu.VMEM((members, members), jnp.float32),
            pltpu.VMEM((members, members), jnp.bfloat16),
        ],
        compiler_params=params,
        name="update",
    )(*terms, *field_moments, *(part for piece in pieces for part in piece))
    return out.reshape(3, planes, columns, lanes, members)


def solution(mesh):
    return jax.shard_map(
        shards,
        mesh=mesh,
        in_specs=(
            P(None, "cores", "face", None, None),
            P("cores", "face", None),
            P(),
            P(),
            P(),
            P(("cores", "face")),
            P(("cores", "face")),
            P(("cores", "face")),
        ),
        out_specs=P(None, "cores", "face", None, None),
        check_vma=False,
    )
```

```python
import functools
import math

import jax
import jax.numpy as jnp
import numpy as np
from jax import lax
from jax.experimental import pallas as pl
from jax.experimental.pallas import tpu as pltpu
from jax.sharding import PartitionSpec as P

HIGHEST = lax.Precision.HIGHEST
PAY_ROWS = 16
GATHER_DEVICES = 64
BLOCK = 128
SPANS = (16, 16, 48, 48)
VMEM_BYTES = 8 * 1024 * 1024


def plane_places(planes, columns):
    own = [(f, z + 1, x + 1) for f in range(2) for z in range(planes) for x in range(columns)]
    low = [(f, 0, x + 1) for f in range(2) for x in range(columns)]
    high = [(f, planes + 1, x + 1) for f in range(2) for x in range(columns)]
    left = [(f, z + 1, 0) for f in range(2) for z in range(planes)]
    right = [(f, z + 1, columns + 1) for f in range(2) for z in range(planes)]
    corners = [
        (f, z, x) for z in (0, planes + 1) for f in range(2) for x in (0, columns + 1)
    ]
    return own + low + high + left + right + corners


def tap_selector(planes, columns):
    places = plane_places(planes, columns)
    chosen = np.zeros((54, planes * columns, 3 * len(places)), np.float32)
    for z in range(planes):
        for x in range(columns):
            for n, (f, zz, xx) in enumerate(places):
                a, b = zz - z, xx - x
                if 0 <= a <= 2 and 0 <= b <= 2:
                    for c in range(3):
                        chosen[27 * f + 9 * a + 3 * b + c, z * columns + x, c * len(places) + n] = 1.0
    return chosen


def swap_matrix(outer, inner):
    matrix = np.zeros((outer * inner, outer * inner), np.float32)
    for i in range(outer):
        for j in range(inner):
            matrix[j * outer + i, i * inner + j] = 1.0
    return matrix


def three_pieces(value):
    first = lax.reduce_precision(value, 8, 7)
    second = lax.reduce_precision(value - first, 8, 7)
    third = lax.reduce_precision(value - first - second, 8, 7)
    return first, second, third


def ones_rows(members):
    row_index = lax.broadcasted_iota(jnp.int32, (16, members), 0)
    return jnp.where(row_index < 3, 1.0, 0.0).astype(jnp.bfloat16)


def observe_kernel(
    own, low, high, left, right, corner_low, corner_high, by_row, swap_in, read_column,
    observations, cells, mask, packed, pay_out, pred
):
    lanes, members = own.shape[1], own.shape[2]
    count = packed.shape[1]
    observed = cells.shape[0]
    packed[0] = jnp.zeros((count, members), jnp.bfloat16)
    packed[lanes + 1] = jnp.zeros((count, members), jnp.bfloat16)

    for step in range(lanes // 16):
        at = step * 16
        part = lambda ref: ref[:, pl.ds(at, 16), :]
        sides = (left, right, corner_low, corner_high)
        blocks = (
            part(own),
            jnp.concatenate([part(low), part(high)], axis=0),
            jnp.concatenate([part(side) for side in sides], axis=0),
        )
        for g, block in enumerate(blocks):
            moved = jnp.dot(
                swap_in[...], block.reshape(256, members), preferred_element_type=jnp.float32
            )
            packed[pl.ds(at + 1, 16), 16 * g : 16 * g + 16, :] = (
                moved.astype(jnp.bfloat16).reshape(16, 16, members)
            )

    ones = ones_rows(members)
    read = jnp.broadcast_to(read_column[...], (read_column.shape[0], members))

    def some_cells(step, carry):
        for k in range(16):
            o = step * 16 + k
            cell = cells[o]
            row, y = cell // lanes, cell % lanes
            taps = jnp.concatenate(
                [packed[pl.ds(y, 3)].reshape(3 * count, members), ones], axis=0
            )
            half = jnp.dot(by_row[row], taps, preferred_element_type=jnp.float32)
            total = jnp.sum(read * (half * (1.0 + jnp.tanh(half))), axis=0, keepdims=True)
            found = (0.5 + 0.5 * jnp.tanh(total)) * mask[row, y].astype(jnp.float32)
            pred[pl.ds(o, 1), :] = found.astype(jnp.bfloat16).astype(jnp.float32)
        return carry

    lax.fori_loop(0, observed // 16, some_cells, 0)

    root_count = math.sqrt(members - 1)
    predicted = pred[...]
    center = jnp.mean(predicted, axis=1, keepdims=True)
    inverse_sigma = 1.0 / observations[:, 0:1]
    scaled = (predicted - center) * (inverse_sigma / root_count)
    innovation = (observations[:, 1:2] - center) * inverse_sigma
    coeff = jnp.sum(scaled * innovation, axis=0, keepdims=True) / root_count
    first = coeff.astype(jnp.bfloat16).astype(jnp.float32)
    second = (coeff - first).astype(jnp.bfloat16).astype(jnp.float32)
    third = coeff - first - second
    index = lax.broadcasted_iota(jnp.int32, (PAY_ROWS, members), 0)
    tail = jnp.where(index == 0, first, jnp.where(index == 1, second, jnp.where(index == 2, third, 0.0)))
    pay_out[0:observed, :] = scaled.astype(jnp.bfloat16)
    pay_out[observed : observed + PAY_ROWS, :] = tail.astype(jnp.bfloat16)


def saturate_kernel(
    start, packed, weights, swap_out, mask, read_half, anomaly_out, mean_out, sat_rows
):
    rows, span, members = anomaly_out.shape
    count = packed.shape[1]
    channels = read_half.shape[0]
    ones = ones_rows(members)
    lane_index = lax.broadcasted_iota(jnp.int32, mask.shape, 1)

    def some_rows(step, carry):
        found = []
        for k in range(8):
            y = start + step * 8 + k
            taps = jnp.concatenate(
                [packed[pl.ds(y, 3)].reshape(3 * count, members), ones], axis=0
            )
            half = jnp.dot(weights[...], taps, preferred_element_type=jnp.float32)
            total = jnp.zeros((rows, members), jnp.float32)
            for c in range(channels):
                part = half[rows * c : rows * c + rows]
                total = total + read_half[c] * (part * (1.0 + jnp.tanh(part)))
            here = jnp.sum(jnp.where(lane_index == y, mask[...], 0.0), axis=1, keepdims=True)
            found.append(here * (0.5 + 0.5 * jnp.tanh(total)))
        at = pl.multiple_of(step * 8 * rows, 8 * rows)
        sat_rows[pl.ds(at, 8 * rows), :] = jnp.concatenate(found, axis=0).astype(jnp.bfloat16)
        return carry

    lax.fori_loop(0, span // 8, some_rows, 0)
    for n in range(span // 16):
        block = sat_rows[n * 16 * rows : (n + 1) * 16 * rows, :]
        moved = jnp.dot(swap_out[...], block, preferred_element_type=jnp.float32)
        mean = jnp.mean(moved, axis=1, keepdims=True)
        anomalies = (moved - mean).astype(jnp.bfloat16)
        anomaly_out[:, n * 16 : n * 16 + 16, :] = anomalies.reshape(rows, 16, members)
        mean_out[:, n * 16 : n * 16 + 16, :] = mean.reshape(rows, 16, 1)


def moments_kernel(fields, anomaly_out, mean_out):
    def step(n, carry):
        state = fields[pl.ds(2 * n, 2)].astype(jnp.float32)
        mean = jnp.mean(state, axis=2, keepdims=True)
        anomaly_out[pl.ds(2 * n, 2)] = (state - mean).astype(jnp.bfloat16)
        mean_out[pl.ds(2 * n, 2)] = mean
        return carry

    lax.fori_loop(0, fields.shape[0] // 2, step, 0)


def transposed_dot(a, b, precision):
    return lax.dot_general(
        a, b, (((0,), (0,)), ((), ())), preferred_element_type=jnp.float32, precision=precision
    )


def spread_row(part, p):
    return jnp.broadcast_to(part[p : p + 1, :], part.shape)


def spread_lane(part, q):
    return jnp.broadcast_to(part[:, q : q + 1], part.shape)


def inverse_factor_block(block):
    lane = lax.broadcasted_iota(jnp.int32, (8, 2 * BLOCK), 1)
    sub = lax.broadcasted_iota(jnp.int32, (8, 2 * BLOCK), 0)
    groups = BLOCK // 8
    parts = []
    for i in range(groups):
        unit = jnp.where(lane == sub + (BLOCK + 8 * i), 1.0, 0.0)
        known = jnp.concatenate(
            [block[8 * i : 8 * i + 8, :], jnp.zeros((8, BLOCK), jnp.float32)], axis=1
        )
        parts.append(known + unit)
    done = []
    upcoming = [spread_lane(parts[0], q) for q in range(8)]
    for j in range(groups):
        corner = upcoming
        entry = {(p, q): spread_row(corner[q], p) for q in range(8) for p in range(q, 8)}
        line = [spread_row(parts[j], p) for p in range(8)]
        near = j + 1 < groups
        if near:
            beside = [spread_lane(parts[j + 1], 8 * j + q) for q in range(8)]
            upcoming = [spread_lane(parts[j + 1], 8 * j + 8 + q) for q in range(8)]
        factor, scale = {}, []
        for q in range(8):
            root = lax.rsqrt(entry[q, q])
            scale.append(root)
            line[q] = line[q] * root
            for p in range(q + 1, 8):
                factor[p, q] = entry[p, q] * root
            for t in range(q + 1, 8):
                for p in range(t, 8):
                    entry[p, t] = entry[p, t] - factor[p, q] * factor[t, q]
            for p in range(q + 1, 8):
                line[p] = line[p] - factor[p, q] * line[q]
            if near:
                lead = beside[q] * root
                upcoming = [
                    column - lead * spread_row(lead, p) for p, column in enumerate(upcoming)
                ]
                for t in range(q + 1, 8):
                    beside[t] = beside[t] - lead * factor[t, q]
                parts[j + 1] = parts[j + 1] - lead * line[q]
        if j + 2 < groups:
            weighted = [None] * 8
            for q in range(7, -1, -1):
                rest = line[q]
                for p in range(q + 1, 8):
                    rest = rest - factor[p, q] * weighted[p]
                weighted[q] = rest * scale[q]
            for i in range(j + 2, groups):
                change = spread_lane(parts[i], 8 * j) * weighted[0]
                for q in range(1, 8):
                    change = change + spread_lane(parts[i], 8 * j + q) * weighted[q]
                parts[i] = parts[i] - change
        merged = line[0]
        for q in range(1, 8):
            merged = jnp.where(sub == q, line[q], merged)
        done.append(merged[:, BLOCK:])
    return jnp.concatenate(done, axis=0)


def update_kernel(gathered, *refs):
    if gathered:
        pay, refs = refs[0], refs[1:]
    else:
        gram, coeff_in, refs = refs[0], refs[1], refs[2:]
    moments, (out, joint, mixing) = refs[:-3], refs[-3:]
    members = out.shape[2]
    sub = lax.broadcasted_iota(jnp.int32, (members, members), 0)
    lane = lax.broadcasted_iota(jnp.int32, (members, members), 1)
    identity = jnp.where(sub == lane, 1.0, 0.0)
    if gathered:
        devices, observed = pay.shape[0], pay.shape[1] - PAY_ROWS
        group = max(1, 2048 // observed)
        total = identity
        for d in range(0, devices, group):
            block = pay[d : d + group, 0:observed, :].reshape(-1, members)
            total = total + transposed_dot(block, block, None)
        coeff = jnp.zeros((PAY_ROWS, members), jnp.float32)
        for d in range(devices):
            coeff = coeff + pay[d, observed:, :].astype(jnp.float32)
        coeff = jnp.sum(coeff, axis=0, keepdims=True)
    else:
        total = identity + gram[...]
        coeff = coeff_in[...]
    joint[...] = total
    for k in range(members // BLOCK):
        at = k * BLOCK
        below = at + BLOCK
        wide_sub, wide_lane = sub[0:BLOCK, :], lane[0:BLOCK, :]
        inside = jnp.logical_and(wide_lane >= at, wide_lane < below)
        row = joint[at:below, :]
        inverse = inverse_factor_block(row[:, at:below])
        unit = jnp.where(wide_lane == wide_sub + at, 1.0, 0.0)
        row = jnp.dot(
            inverse,
            jnp.where(inside, unit, row),
            precision=HIGHEST,
            preferred_element_type=jnp.float32,
        )
        joint[at:below, :] = row
        if below < members:
            ahead = jnp.where(wide_lane >= below, row, 0.0)
            change = transposed_dot(ahead, row, HIGHEST)
            rest_lane = lane[below:, :]
            inside = jnp.logical_and(rest_lane >= at, rest_lane < below)
            joint[below:, :] = jnp.where(inside, 0.0, joint[below:, :]) - change[below:, :]
    inverse = jnp.where(lane <= sub, joint[...], 0.0)
    half = jnp.sum(inverse * coeff, axis=1, keepdims=True)
    weight = jnp.sum(inverse * half, axis=0, keepdims=True)
    mixing[...] = jnp.transpose((inverse + weight).astype(jnp.bfloat16))

    def blend(anomalies, mean):
        outer, inner = anomalies.shape[0], anomalies.shape[1]
        moved = jnp.dot(
            anomalies.reshape(outer * inner, members), mixing[...], preferred_element_type=jnp.float32
        )
        return (mean + moved.reshape(outer, inner, members)).astype(jnp.bfloat16)

    anomalies, mean = moments[:2]
    field_rows = anomalies.shape[0]

    def step(n, carry):
        for k in range(2):
            at = 4 * n + 2 * k
            out[pl.ds(at, 2)] = blend(anomalies[pl.ds(at, 2)], mean[pl.ds(at, 2)])
        return carry

    lax.fori_loop(0, field_rows // 4, step, 0)
    at = 0
    for n in range(1, len(moments) // 2):
        anomalies, mean = moments[2 * n : 2 * n + 2]
        span = anomalies.shape[1]
        out[field_rows:, at : at + span, :] = blend(anomalies[...], mean[...])
        at += span


def shift(value, axis, by, closed):
    count = lax.axis_size(axis)
    if by > 0:
        pairs = [(i, (i + 1) % count) for i in range(count if closed else count - 1)]
    else:
        pairs = [((i + 1) % count, i) for i in range(count if closed else count - 1)]
    return lax.ppermute(value, axis, pairs)


def gather_rows(block, steps, packed, saturate):
    pieces = []
    for n, (axis, bit) in enumerate(steps):
        count = lax.axis_size(axis)
        if n < len(SPANS):
            block, packed = lax.optimization_barrier((block, packed))
        other = lax.ppermute(block, axis, [(i, i ^ bit) for i in range(count)])
        if n < len(SPANS):
            piece = saturate(n, packed)
        block = jnp.concatenate([block, other], axis=0)
        if n < len(SPANS):
            block, piece = lax.optimization_barrier((block, piece))
            pieces.append(piece)
    return block, pieces + [saturate(n, packed) for n in range(len(pieces), len(SPANS))]


def bits_of(axis, count):
    bits = []
    while (1 << len(bits)) < count:
        bits.append((axis, 1 << len(bits)))
    return bits


def vmem():
    return pl.BlockSpec(memory_space=pltpu.VMEM)


def smem():
    return pl.BlockSpec(memory_space=pltpu.SMEM)


def moments_shape(outer, inner, members):
    return (
        jax.ShapeDtypeStruct((outer, inner, members), jnp.bfloat16),
        jax.ShapeDtypeStruct((outer, inner, 1), jnp.float32),
    )


def shards(
    fields, pore_mask, conv_kernel, conv_bias, read_weight, obs_cells, obs_values, obs_sigma
):
    _, planes, columns, lanes, members = fields.shape
    channels = conv_kernel.shape[1]
    rows = planes * columns
    observed = obs_cells.shape[0]

    left = shift(fields[:, :, -1:], "face", 1, False)
    right = shift(fields[:, :, :1], "face", -1, False)
    low = shift(fields[:, -1:], "cores", 1, True)
    high = shift(fields[:, :1], "cores", -1, True)
    low_sides = jnp.concatenate([left[:, -1:], right[:, -1:]], axis=2)
    high_sides = jnp.concatenate([left[:, :1], right[:, :1]], axis=2)
    corner_low = shift(low_sides, "cores", 1, True)
    corner_high = shift(high_sides, "cores", -1, True)

    selector = tap_selector(planes, columns)
    count = selector.shape[2] // 3
    taps = jnp.dot(
        jnp.transpose(conv_kernel),
        jnp.asarray(selector.reshape(54, -1), jnp.bfloat16),
        preferred_element_type=jnp.float32,
    ).reshape(channels, rows, 3 * count)
    bias = jnp.stack(three_pieces(0.5 * conv_bias), axis=1)
    bias = jnp.broadcast_to(bias[:, None, :], (channels, rows, 3))
    weights = jnp.concatenate(
        [0.5 * taps, bias, jnp.zeros((channels, rows, 13), jnp.float32)], axis=2
    ).astype(jnp.bfloat16)
    by_row = jnp.transpose(weights, (1, 0, 2))
    weights = weights.reshape(channels * rows, 3 * count + 16)
    flat = lambda a: a.reshape(-1, lanes, members)
    starts = [sum(SPANS[:n]) for n in range(len(SPANS))]
    mask = pore_mask.reshape(rows, lanes)
    mask_float = mask.astype(jnp.float32)
    read_half = 0.5 * read_weight
    swap_in = jnp.asarray(swap_matrix(16, 16), jnp.bfloat16)
    swap_out = jnp.asarray(swap_matrix(16, rows), jnp.bfloat16)
    params = pltpu.CompilerParams(vmem_limit_bytes=VMEM_BYTES)
    field_moments = pl.pallas_call(
        moments_kernel,
        out_shape=moments_shape(2 * rows, lanes, members),
        in_specs=[vmem()],
        out_specs=(vmem(), vmem()),
        compiler_params=params,
        name="moments",
    )(flat(fields))
    read_column = read_half[:, None]
    observations = jnp.stack([obs_sigma, obs_values], axis=1)
    packed, pay = pl.pallas_call(
        observe_kernel,
        out_shape=(
            jax.ShapeDtypeStruct((lanes + 2, count, members), jnp.bfloat16),
            jax.ShapeDtypeStruct((observed + PAY_ROWS, members), jnp.bfloat16),
        ),
        in_specs=[vmem()] * 11 + [smem()] * 2,
        out_specs=(vmem(), vmem()),
        scratch_shapes=[pltpu.VMEM((observed, members), jnp.float32)],
        compiler_params=params,
        name="observe",
    )(
        flat(fields), flat(low), flat(high), flat(left), flat(right), flat(corner_low),
        flat(corner_high), by_row, swap_in, read_column, observations, obs_cells, mask,
    )

    def saturate(n, packed):
        span = SPANS[n]
        return pl.pallas_call(
            functools.partial(saturate_kernel, starts[n]),
            out_shape=moments_shape(rows, span, members),
            in_specs=[vmem()] * 4 + [smem()],
            out_specs=(vmem(), vmem()),
            scratch_shapes=[pltpu.VMEM((rows * span, members), jnp.bfloat16)],
            compiler_params=params,
            cost_estimate=pl.CostEstimate(
                flops=2 * 256 * 256 * span * members,
                bytes_accessed=4 * 1024 * 1024,
                transcendentals=channels * rows * span * members,
            ),
            name="saturate",
        )(packed, weights, swap_out, mask_float, read_half)

    core_count, face_count = lax.axis_size("cores"), lax.axis_size("face")
    devices = core_count * face_count
    gathered = devices <= GATHER_DEVICES and devices & (devices - 1) == 0
    if gathered:
        steps = bits_of("face", face_count)[::-1] + bits_of("cores", core_count)[1:]
        steps = steps + bits_of("cores", core_count)[:1]
        block, pieces = gather_rows(pay[None], steps, packed, saturate)
        terms = (block,)
    else:
        part = pay[:observed]
        gram = lax.dot_general(
            part, part, (((0,), (0,)), ((), ())), preferred_element_type=jnp.float32
        )
        coeff = jnp.sum(pay[observed:].astype(jnp.float32), axis=0, keepdims=True)
        terms = lax.psum((gram, coeff), ("cores", "face"))
        pieces = [saturate(n, packed) for n in range(len(SPANS))]
    out = pl.pallas_call(
        functools.partial(update_kernel, gathered),
        out_shape=jax.ShapeDtypeStruct((3 * rows, lanes, members), jnp.bfloat16),
        in_specs=[vmem()] * (len(terms) + 2 + 2 * len(SPANS)),
        out_specs=vmem(),
        scratch_shapes=[
            pltpu.VMEM((members, members), jnp.float32),
            pltpu.VMEM((members, members), jnp.bfloat16),
        ],
        compiler_params=params,
        name="update",
    )(*terms, *field_moments, *(part for piece in pieces for part in piece))
    return out.reshape(3, planes, columns, lanes, members)


def solution(mesh):
    return jax.shard_map(
        shards,
        mesh=mesh,
        in_specs=(
            P(None, "cores", "face", None, None),
            P("cores", "face", None),
            P(),
            P(),
            P(),
            P(("cores", "face")),
            P(("cores", "face")),
            P(("cores", "face")),
        ),
        out_specs=P(None, "cores", "face", None, None),
        check_vma=False,
    )
```

```python
import functools
import math

import jax
import jax.numpy as jnp
import numpy as np
from jax import lax
from jax.experimental import pallas as pl
from jax.experimental.pallas import tpu as pltpu
from jax.sharding import PartitionSpec as P

HIGHEST = lax.Precision.HIGHEST
PAY_ROWS = 16
GATHER_DEVICES = 64
BLOCK = 128
SPANS = (16, 16, 48, 48)
VMEM_BYTES = 8 * 1024 * 1024


def plane_places(planes, columns):
    own = [(f, z + 1, x + 1) for f in range(2) for z in range(planes) for x in range(columns)]
    low = [(f, 0, x + 1) for f in range(2) for x in range(columns)]
    high = [(f, planes + 1, x + 1) for f in range(2) for x in range(columns)]
    left = [(f, z + 1, 0) for f in range(2) for z in range(planes)]
    right = [(f, z + 1, columns + 1) for f in range(2) for z in range(planes)]
    corners = [
        (f, z, x) for z in (0, planes + 1) for f in range(2) for x in (0, columns + 1)
    ]
    return own + low + high + left + right + corners


def tap_selector(planes, columns):
    places = plane_places(planes, columns)
    chosen = np.zeros((54, planes * columns, 3 * len(places)), np.float32)
    for z in range(planes):
        for x in range(columns):
            for n, (f, zz, xx) in enumerate(places):
                a, b = zz - z, xx - x
                if 0 <= a <= 2 and 0 <= b <= 2:
                    for c in range(3):
                        chosen[27 * f + 9 * a + 3 * b + c, z * columns + x, c * len(places) + n] = 1.0
    return chosen


def swap_matrix(outer, inner):
    matrix = np.zeros((outer * inner, outer * inner), np.float32)
    for i in range(outer):
        for j in range(inner):
            matrix[j * outer + i, i * inner + j] = 1.0
    return matrix


def three_pieces(value):
    first = lax.reduce_precision(value, 8, 7)
    second = lax.reduce_precision(value - first, 8, 7)
    third = lax.reduce_precision(value - first - second, 8, 7)
    return first, second, third


def ones_rows(members):
    row_index = lax.broadcasted_iota(jnp.int32, (16, members), 0)
    return jnp.where(row_index < 3, 1.0, 0.0).astype(jnp.bfloat16)


def observe_kernel(
    own, low, high, left, right, corner_low, corner_high, by_row, swap_in, read_column,
    observations, cells, mask, packed, pay_out, pred
):
    lanes, members = own.shape[1], own.shape[2]
    count = packed.shape[1]
    observed = cells.shape[0]
    packed[0] = jnp.zeros((count, members), jnp.bfloat16)
    packed[lanes + 1] = jnp.zeros((count, members), jnp.bfloat16)

    for step in range(lanes // 16):
        at = step * 16
        part = lambda ref: ref[:, pl.ds(at, 16), :]
        sides = (left, right, corner_low, corner_high)
        blocks = (
            part(own),
            jnp.concatenate([part(low), part(high)], axis=0),
            jnp.concatenate([part(side) for side in sides], axis=0),
        )
        for g, block in enumerate(blocks):
            moved = jnp.dot(
                swap_in[...], block.reshape(256, members), preferred_element_type=jnp.float32
            )
            packed[pl.ds(at + 1, 16), 16 * g : 16 * g + 16, :] = (
                moved.astype(jnp.bfloat16).reshape(16, 16, members)
            )

    ones = ones_rows(members)
    read = jnp.broadcast_to(read_column[...], (read_column.shape[0], members))

    def some_cells(step, carry):
        for k in range(16):
            o = step * 16 + k
            cell = cells[o]
            row, y = cell // lanes, cell % lanes
            taps = jnp.concatenate(
                [packed[pl.ds(y, 3)].reshape(3 * count, members), ones], axis=0
            )
            half = jnp.dot(by_row[row], taps, preferred_element_type=jnp.float32)
            total = jnp.sum(read * (half * (1.0 + jnp.tanh(half))), axis=0, keepdims=True)
            found = (0.5 + 0.5 * jnp.tanh(total)) * mask[row, y].astype(jnp.float32)
            pred[pl.ds(o, 1), :] = found.astype(jnp.bfloat16).astype(jnp.float32)
        return carry

    lax.fori_loop(0, observed // 16, some_cells, 0)

    root_count = math.sqrt(members - 1)
    predicted = pred[...]
    center = jnp.mean(predicted, axis=1, keepdims=True)
    inverse_sigma = 1.0 / observations[:, 0:1]
    scaled = (predicted - center) * (inverse_sigma / root_count)
    innovation = (observations[:, 1:2] - center) * inverse_sigma
    coeff = jnp.sum(scaled * innovation, axis=0, keepdims=True) / root_count
    first = coeff.astype(jnp.bfloat16).astype(jnp.float32)
    second = (coeff - first).astype(jnp.bfloat16).astype(jnp.float32)
    third = coeff - first - second
    index = lax.broadcasted_iota(jnp.int32, (PAY_ROWS, members), 0)
    tail = jnp.where(index == 0, first, jnp.where(index == 1, second, jnp.where(index == 2, third, 0.0)))
    pay_out[0:observed, :] = scaled.astype(jnp.bfloat16)
    pay_out[observed : observed + PAY_ROWS, :] = tail.astype(jnp.bfloat16)


def saturate_kernel(
    start, packed, weights, swap_out, mask, read_half, anomaly_out, mean_out, sat_rows
):
    rows, span, members = anomaly_out.shape
    count = packed.shape[1]
    channels = read_half.shape[0]
    ones = ones_rows(members)
    lane_index = lax.broadcasted_iota(jnp.int32, mask.shape, 1)

    def some_rows(step, carry):
        found = []
        for k in range(8):
            y = start + step * 8 + k
            taps = jnp.concatenate(
                [packed[pl.ds(y, 3)].reshape(3 * count, members), ones], axis=0
            )
            half = jnp.dot(weights[...], taps, preferred_element_type=jnp.float32)
            total = jnp.zeros((rows, members), jnp.float32)
            for c in range(channels):
                part = half[rows * c : rows * c + rows]
                total = total + read_half[c] * (part * (1.0 + jnp.tanh(part)))
            here = jnp.sum(jnp.where(lane_index == y, mask[...], 0.0), axis=1, keepdims=True)
            found.append(here * (0.5 + 0.5 * jnp.tanh(total)))
        at = pl.multiple_of(step * 8 * rows, 8 * rows)
        sat_rows[pl.ds(at, 8 * rows), :] = jnp.concatenate(found, axis=0).astype(jnp.bfloat16)
        return carry

    lax.fori_loop(0, span // 8, some_rows, 0)
    for n in range(span // 16):
        block = sat_rows[n * 16 * rows : (n + 1) * 16 * rows, :]
        moved = jnp.dot(swap_out[...], block, preferred_element_type=jnp.float32)
        mean = jnp.mean(moved, axis=1, keepdims=True)
        anomalies = (moved - mean).astype(jnp.bfloat16)
        anomaly_out[:, n * 16 : n * 16 + 16, :] = anomalies.reshape(rows, 16, members)
        mean_out[:, n * 16 : n * 16 + 16, :] = mean.reshape(rows, 16, 1)


def moments_kernel(fields, anomaly_out, mean_out):
    def step(n, carry):
        state = fields[pl.ds(2 * n, 2)].astype(jnp.float32)
        mean = jnp.mean(state, axis=2, keepdims=True)
        anomaly_out[pl.ds(2 * n, 2)] = (state - mean).astype(jnp.bfloat16)
        mean_out[pl.ds(2 * n, 2)] = mean
        return carry

    lax.fori_loop(0, fields.shape[0] // 2, step, 0)


def transposed_dot(a, b, precision):
    return lax.dot_general(
        a, b, (((0,), (0,)), ((), ())), preferred_element_type=jnp.float32, precision=precision
    )


def spread_row(part, p):
    return jnp.broadcast_to(part[p : p + 1, :], part.shape)


def spread_lane(part, q):
    return jnp.broadcast_to(part[:, q : q + 1], part.shape)


def inverse_factor_block(block):
    lane = lax.broadcasted_iota(jnp.int32, (8, 2 * BLOCK), 1)
    sub = lax.broadcasted_iota(jnp.int32, (8, 2 * BLOCK), 0)
    groups = BLOCK // 8
    parts = []
    for i in range(groups):
        unit = jnp.where(lane == sub + (BLOCK + 8 * i), 1.0, 0.0)
        known = jnp.concatenate(
            [block[8 * i : 8 * i + 8, :], jnp.zeros((8, BLOCK), jnp.float32)], axis=1
        )
        parts.append(known + unit)
    done = []
    upcoming = [spread_lane(parts[0], q) for q in range(8)]
    for j in range(groups):
        corner = upcoming
        entry = {(p, q): spread_row(corner[q], p) for q in range(8) for p in range(q, 8)}
        line = [spread_row(parts[j], p) for p in range(8)]
        near = j + 1 < groups
        if near:
            beside = [spread_lane(parts[j + 1], 8 * j + q) for q in range(8)]
            upcoming = [spread_lane(parts[j + 1], 8 * j + 8 + q) for q in range(8)]
        factor, scale = {}, []
        for q in range(8):
            root = lax.rsqrt(entry[q, q])
            scale.append(root)
            line[q] = line[q] * root
            for p in range(q + 1, 8):
                factor[p, q] = entry[p, q] * root
            for t in range(q + 1, 8):
                for p in range(t, 8):
                    entry[p, t] = entry[p, t] - factor[p, q] * factor[t, q]
            for p in range(q + 1, 8):
                line[p] = line[p] - factor[p, q] * line[q]
            if near:
                lead = beside[q] * root
                upcoming = [
                    column - lead * spread_row(lead, p) for p, column in enumerate(upcoming)
                ]
                for t in range(q + 1, 8):
                    beside[t] = beside[t] - lead * factor[t, q]
                parts[j + 1] = parts[j + 1] - lead * line[q]
        if j + 2 < groups:
            weighted = [None] * 8
            for q in range(7, -1, -1):
                rest = line[q]
                for p in range(q + 1, 8):
                    rest = rest - factor[p, q] * weighted[p]
                weighted[q] = rest * scale[q]
            for i in range(j + 2, groups):
                change = spread_lane(parts[i], 8 * j) * weighted[0]
                for q in range(1, 8):
                    change = change + spread_lane(parts[i], 8 * j + q) * weighted[q]
                parts[i] = parts[i] - change
        merged = line[0]
        for q in range(1, 8):
            merged = jnp.where(sub == q, line[q], merged)
        done.append(merged[:, BLOCK:])
    return jnp.concatenate(done, axis=0)


def update_kernel(gathered, *refs):
    if gathered:
        pay, refs = refs[0], refs[1:]
    else:
        gram, coeff_in, refs = refs[0], refs[1], refs[2:]
    moments, (out, joint, mixing) = refs[:-3], refs[-3:]
    members = out.shape[2]
    sub = lax.broadcasted_iota(jnp.int32, (members, members), 0)
    lane = lax.broadcasted_iota(jnp.int32, (members, members), 1)
    identity = jnp.where(sub == lane, 1.0, 0.0)
    if gathered:
        devices, observed = pay.shape[0], pay.shape[1] - PAY_ROWS
        group = max(1, 256 // observed)
        total = identity
        for d in range(0, devices, group):
            block = pay[d : d + group, 0:observed, :].reshape(-1, members)
            total = total + transposed_dot(block, block, None)
        coeff = jnp.zeros((PAY_ROWS, members), jnp.float32)
        for d in range(devices):
            coeff = coeff + pay[d, observed:, :].astype(jnp.float32)
        coeff = jnp.sum(coeff, axis=0, keepdims=True)
    else:
        total = identity + gram[...]
        coeff = coeff_in[...]
    joint[...] = total
    for k in range(members // BLOCK):
        at = k * BLOCK
        below = at + BLOCK
        wide_sub, wide_lane = sub[0:BLOCK, :], lane[0:BLOCK, :]
        inside = jnp.logical_and(wide_lane >= at, wide_lane < below)
        row = joint[at:below, :]
        inverse = inverse_factor_block(row[:, at:below])
        unit = jnp.where(wide_lane == wide_sub + at, 1.0, 0.0)
        row = jnp.dot(
            inverse,
            jnp.where(inside, unit, row),
            precision=HIGHEST,
            preferred_element_type=jnp.float32,
        )
        joint[at:below, :] = row
        if below < members:
            ahead = jnp.where(wide_lane >= below, row, 0.0)
            change = transposed_dot(ahead, row, HIGHEST)
            rest_lane = lane[below:, :]
            inside = jnp.logical_and(rest_lane >= at, rest_lane < below)
            joint[below:, :] = jnp.where(inside, 0.0, joint[below:, :]) - change[below:, :]
    inverse = jnp.where(lane <= sub, joint[...], 0.0)
    half = jnp.sum(inverse * coeff, axis=1, keepdims=True)
    weight = jnp.sum(inverse * half, axis=0, keepdims=True)
    mixing[...] = jnp.transpose((inverse + weight).astype(jnp.bfloat16))

    def blend(anomalies, mean):
        outer, inner = anomalies.shape[0], anomalies.shape[1]
        moved = jnp.dot(
            anomalies.reshape(outer * inner, members), mixing[...], preferred_element_type=jnp.float32
        )
        return (mean + moved.reshape(outer, inner, members)).astype(jnp.bfloat16)

    anomalies, mean = moments[:2]
    field_rows = anomalies.shape[0]

    def step(n, carry):
        for k in range(2):
            at = 4 * n + 2 * k
            out[pl.ds(at, 2)] = blend(anomalies[pl.ds(at, 2)], mean[pl.ds(at, 2)])
        return carry

    lax.fori_loop(0, field_rows // 4, step, 0)
    at = 0
    for n in range(1, len(moments) // 2):
        anomalies, mean = moments[2 * n : 2 * n + 2]
        span = anomalies.shape[1]
        out[field_rows:, at : at + span, :] = blend(anomalies[...], mean[...])
        at += span


def shift(value, axis, by, closed):
    count = lax.axis_size(axis)
    if by > 0:
        pairs = [(i, (i + 1) % count) for i in range(count if closed else count - 1)]
    else:
        pairs = [((i + 1) % count, i) for i in range(count if closed else count - 1)]
    return lax.ppermute(value, axis, pairs)


def gather_rows(block, steps, packed, saturate):
    pieces = []
    for n, (axis, bit) in enumerate(steps):
        count = lax.axis_size(axis)
        if n < len(SPANS):
            block, packed = lax.optimization_barrier((block, packed))
        other = lax.ppermute(block, axis, [(i, i ^ bit) for i in range(count)])
        if n < len(SPANS):
            piece = saturate(n, packed)
        block = jnp.concatenate([block, other], axis=0)
        if n < len(SPANS):
            block, piece = lax.optimization_barrier((block, piece))
            pieces.append(piece)
    return block, pieces + [saturate(n, packed) for n in range(len(pieces), len(SPANS))]


def bits_of(axis, count):
    bits = []
    while (1 << len(bits)) < count:
        bits.append((axis, 1 << len(bits)))
    return bits


def vmem():
    return pl.BlockSpec(memory_space=pltpu.VMEM)


def smem():
    return pl.BlockSpec(memory_space=pltpu.SMEM)


def moments_shape(outer, inner, members):
    return (
        jax.ShapeDtypeStruct((outer, inner, members), jnp.bfloat16),
        jax.ShapeDtypeStruct((outer, inner, 1), jnp.float32),
    )


def shards(
    fields, pore_mask, conv_kernel, conv_bias, read_weight, obs_cells, obs_values, obs_sigma
):
    _, planes, columns, lanes, members = fields.shape
    channels = conv_kernel.shape[1]
    rows = planes * columns
    observed = obs_cells.shape[0]

    ends = (fields[:, :, -1:], fields[:, :, :1], fields[:, -1:], fields[:, :1])
    left, right, low, high = lax.optimization_barrier(ends)
    low = shift(low, "cores", 1, True)
    high = shift(high, "cores", -1, True)
    left = shift(left, "face", 1, False)
    right = shift(right, "face", -1, False)
    low_sides = jnp.concatenate([left[:, -1:], right[:, -1:]], axis=2)
    high_sides = jnp.concatenate([left[:, :1], right[:, :1]], axis=2)
    corner_low = shift(low_sides, "cores", 1, True)
    corner_high = shift(high_sides, "cores", -1, True)

    selector = tap_selector(planes, columns)
    count = selector.shape[2] // 3
    taps = jnp.dot(
        jnp.transpose(conv_kernel),
        jnp.asarray(selector.reshape(54, -1), jnp.bfloat16),
        preferred_element_type=jnp.float32,
    ).reshape(channels, rows, 3 * count)
    bias = jnp.stack(three_pieces(0.5 * conv_bias), axis=1)
    bias = jnp.broadcast_to(bias[:, None, :], (channels, rows, 3))
    weights = jnp.concatenate(
        [0.5 * taps, bias, jnp.zeros((channels, rows, 13), jnp.float32)], axis=2
    ).astype(jnp.bfloat16)
    by_row = jnp.transpose(weights, (1, 0, 2))
    weights = weights.reshape(channels * rows, 3 * count + 16)
    flat = lambda a: a.reshape(-1, lanes, members)
    starts = [sum(SPANS[:n]) for n in range(len(SPANS))]
    mask = pore_mask.reshape(rows, lanes)
    mask_float = mask.astype(jnp.float32)
    read_half = 0.5 * read_weight
    swap_in = jnp.asarray(swap_matrix(16, 16), jnp.bfloat16)
    swap_out = jnp.asarray(swap_matrix(16, rows), jnp.bfloat16)
    params = pltpu.CompilerParams(vmem_limit_bytes=VMEM_BYTES)
    field_moments = pl.pallas_call(
        moments_kernel,
        out_shape=moments_shape(2 * rows, lanes, members),
        in_specs=[vmem()],
        out_specs=(vmem(), vmem()),
        compiler_params=params,
        name="moments",
    )(flat(fields))
    read_column = read_half[:, None]
    observations = jnp.stack([obs_sigma, obs_values], axis=1)
    packed, pay = pl.pallas_call(
        observe_kernel,
        out_shape=(
            jax.ShapeDtypeStruct((lanes + 2, count, members), jnp.bfloat16),
            jax.ShapeDtypeStruct((observed + PAY_ROWS, members), jnp.bfloat16),
        ),
        in_specs=[vmem()] * 11 + [smem()] * 2,
        out_specs=(vmem(), vmem()),
        scratch_shapes=[pltpu.VMEM((observed, members), jnp.float32)],
        compiler_params=params,
        name="observe",
    )(
        flat(fields), flat(low), flat(high), flat(left), flat(right), flat(corner_low),
        flat(corner_high), by_row, swap_in, read_column, observations, obs_cells, mask,
    )

    def saturate(n, packed):
        span = SPANS[n]
        return pl.pallas_call(
            functools.partial(saturate_kernel, starts[n]),
            out_shape=moments_shape(rows, span, members),
            in_specs=[vmem()] * 4 + [smem()],
            out_specs=(vmem(), vmem()),
            scratch_shapes=[pltpu.VMEM((rows * span, members), jnp.bfloat16)],
            compiler_params=params,
            cost_estimate=pl.CostEstimate(
                flops=2 * 256 * 256 * span * members,
                bytes_accessed=4 * 1024 * 1024,
                transcendentals=channels * rows * span * members,
            ),
            name="saturate",
        )(packed, weights, swap_out, mask_float, read_half)

    core_count, face_count = lax.axis_size("cores"), lax.axis_size("face")
    devices = core_count * face_count
    gathered = devices <= GATHER_DEVICES and devices & (devices - 1) == 0
    if gathered:
        steps = bits_of("face", face_count)[::-1] + bits_of("cores", core_count)[1:]
        steps = steps + bits_of("cores", core_count)[:1]
        block, pieces = gather_rows(pay[None], steps, packed, saturate)
        terms = (block,)
    else:
        part = pay[:observed]
        gram = lax.dot_general(
            part, part, (((0,), (0,)), ((), ())), preferred_element_type=jnp.float32
        )
        coeff = jnp.sum(pay[observed:].astype(jnp.float32), axis=0, keepdims=True)
        terms = lax.psum((gram, coeff), ("cores", "face"))
        pieces = [saturate(n, packed) for n in range(len(SPANS))]
    out = pl.pallas_call(
        functools.partial(update_kernel, gathered),
        out_shape=jax.ShapeDtypeStruct((3 * rows, lanes, members), jnp.bfloat16),
        in_specs=[vmem()] * (len(terms) + 2 + 2 * len(SPANS)),
        out_specs=vmem(),
        scratch_shapes=[
            pltpu.VMEM((members, members), jnp.float32),
            pltpu.VMEM((members, members), jnp.bfloat16),
        ],
        compiler_params=params,
        name="update",
    )(*terms, *field_moments, *(part for piece in pieces for part in piece))
    return out.reshape(3, planes, columns, lanes, members)


def solution(mesh):
    return jax.shard_map(
        shards,
        mesh=mesh,
        in_specs=(
            P(None, "cores", "face", None, None),
            P("cores", "face", None),
            P(),
            P(),
            P(),
            P(("cores", "face")),
            P(("cores", "face")),
            P(("cores", "face")),
        ),
        out_specs=P(None, "cores", "face", None, None),
        check_vma=False,
    )
```
